256 devices in a mesh: queue: 64 (over z, x, y_lo), heads: 4 (over y_hi, core).
Axes of the slice: x: 4, y: 4 (y_hi: 2, y_lo: 2; y = y_hi * 2 + y_lo), z: 8, core: 2. Of those that a mesh axis runs over, the one named last changes fastest.
Arguments:
- hidden: bfloat16 [32768, 3072], P('queue'), may hold values from -6 to 6
- levels: int32 [64], replicated, may hold values from 0 to 252, as said below
- frame_counts: int32 [64], replicated, may hold values from 1 to 2, as said below
- mod_weight: bfloat16 [512, 9216], P(None, 'queue')
- qkv_weight: bfloat16 [3, 3072, 1536], P(None, None, 'heads'), may hold values from -0.109375 to 0.109375
- out_weight: bfloat16 [1536, 3072], P('heads'), may hold values from -0.15625 to 0.15625
- fresh: bfloat16 [512, 3072], P(None, 'heads'), may hold values from -6 to 6
Outputs:
- queue_next: bfloat16 [32768, 3072], P('queue', 'heads')
The draws below stay inside these ranges and needn't reach their ends.
Inputs may be any that keep to these rules, and one draw needn't show every extreme that they name: `levels`: strictly rising along the queue, the first 0 and the last 252. `frame_counts`: some stretch has 2 live frames and some other has 1.
All inputs are finite; a program needn't handle non-finite values.
Results may differ from the reference program's by a relative error of at most 0.035.
The reference program's roundings to bfloat16 on the way (of `emb`, `normed`, `attn` and `updated`) count: a program that leaves them out, or rounds other values in their place, can miss the bound.
Values may be sent and summed in bfloat16 or wider, within the bound.
No kernel may reach another device: no remote copies, remote signals or barrier semaphores. Data moves between devices by JAX's collectives and lax.ppermute only.
A program may use at most 128 MiB of HBM per device.

```python
import math
import jax
import jax.numpy as jnp
from jax import lax

D = 3072
HEADS = 24
HD = 64
TE = 512
FR = 2
P_SIZE = 256
SPAN = 512
QUEUE = 64


def draw_levels(key, part):
    key = jax.random.fold_in(key, 11)
    steps = jax.random.randint(key, (QUEUE,), 1, 4)
    rising = jnp.cumsum(steps) - steps[0]
    position = jnp.arange(QUEUE)
    return jnp.where(position == QUEUE - 1, 4 * (QUEUE - 1), rising).astype(jnp.int32)


def draw_frame_counts(key, part):
    key = jax.random.fold_in(key, 12)
    first, second, third = jax.random.split(key, 3)
    base = jax.random.randint(first, (QUEUE,), 1, FR + 1)
    full_slot = jax.random.randint(second, (), 0, QUEUE)
    short_slot = (full_slot + jax.random.randint(third, (), 1, QUEUE)) % QUEUE
    position = jnp.arange(QUEUE)
    base = jnp.where(position == full_slot, FR, base)
    base = jnp.where(position == short_slot, 1, base)
    return base.astype(jnp.int32)


def draw_mod_weight(key, part):
    key = jax.random.fold_in(key, 13)
    values = jax.random.normal(key, (TE, 3 * D), jnp.float32)
    return (values * TE ** (-0.5)).astype(jnp.bfloat16)


def level_of(key, dims, shards, low, largest):
    factor_of = 1.0
    for dim, blocks in shards:
        steps = jax.random.uniform(jax.random.fold_in(jax.random.fold_in(key, 6), dim), (blocks,), jnp.float32, low / len(shards), largest / len(shards))
        factor_of = factor_of * jnp.repeat(jnp.exp(steps), dims[dim] // blocks).reshape((-1,) + (1,) * (len(dims) - 1 - dim))
    return factor_of


def noise(rng, extent, spread, bound, shards=(), kind=jnp.bfloat16):
    drawn = spread * jax.random.normal(rng, extent, jnp.float32)
    if shards:
        drawn = drawn * level_of(rng, extent, shards, -0.22, 0.18)
    return jnp.clip(drawn, -bound, bound).astype(kind)


def setup_inputs(seed: int = 0) -> dict:
    key_of = jax.random.split(jax.random.key(seed), 8)
    hidden = noise(key_of[0], (QUEUE * SPAN, D), 1.0, 6.0, ((0, 64),))
    levels = draw_levels(jax.random.fold_in(key_of[7], 71), 0)
    frame_counts = draw_frame_counts(jax.random.fold_in(key_of[7], 71), 0)
    mod_weight = draw_mod_weight(jax.random.fold_in(key_of[7], 71), 0)
    qkv_weight = noise(key_of[4], (3, D, HEADS * HD), D ** -0.5, 0.109375, ((2, 4),))
    out_weight = noise(key_of[5], (HEADS * HD, D), (HEADS * HD) ** -0.5, 0.15625, ((0, 4),))
    fresh = noise(key_of[6], (SPAN, D), 1.0, 6.0, ((1, 4),))
    return dict(hidden=hidden, levels=levels, frame_counts=frame_counts, mod_weight=mod_weight, qkv_weight=qkv_weight, out_weight=out_weight, fresh=fresh)


NEG = -1e+30

def embed_levels(levels, width):
    halfway = width // 2
    freqs = jnp.exp(-math.log(10000.0) * jnp.arange(halfway, dtype=jnp.float32) / halfway)
    angles = levels.astype(jnp.float32)[:, None] * freqs[None, :]
    return jax.nn.silu(jnp.concatenate([jnp.cos(angles), jnp.sin(angles)], axis=1)).astype(jnp.bfloat16)

def attend(query, keys, values, live):
    scores = jnp.einsum('qhd,khd->hqk', query.astype(jnp.float32), keys.astype(jnp.float32)) * HD ** (-0.5)
    scores = jnp.where(live[None, None, :], scores, NEG)
    peak = lax.optimization_barrier(jnp.max(scores, axis=2, keepdims=True))
    weights = jnp.where(live[None, None, :], jnp.exp(scores - peak), 0.0)
    total = lax.optimization_barrier(jnp.sum(weights, axis=2))
    rounded = lax.optimization_barrier(weights.astype(jnp.bfloat16))
    numer = jnp.einsum('hqk,khd->qhd', rounded.astype(jnp.float32), values.astype(jnp.float32))
    return (numer / jnp.transpose(total)[:, :, None]).astype(jnp.bfloat16).reshape(SPAN, HEADS * HD)

def reference(hidden, levels, frame_counts, mod_weight, qkv_weight, out_weight, fresh):
    emb = embed_levels(levels, TE)
    modulation = jnp.dot(emb, mod_weight, preferred_element_type=jnp.float32)
    shift = modulation[:, :D]
    scale = modulation[:, D:2 * D]
    gate = modulation[:, 2 * D:]
    rows = hidden.astype(jnp.float32).reshape(QUEUE, SPAN, D)
    mean = lax.optimization_barrier(jnp.mean(rows, axis=2, keepdims=True))
    centred = rows - mean
    var = lax.optimization_barrier(jnp.mean(centred * centred, axis=2, keepdims=True))
    normed = (centred * lax.rsqrt(var + 1e-05) * (1.0 + scale[:, None, :]) + shift[:, None, :]).astype(jnp.bfloat16)
    normed = normed.reshape(QUEUE * SPAN, D)
    query = jnp.dot(normed, qkv_weight[0], preferred_element_type=jnp.float32).astype(jnp.bfloat16)
    keys = jnp.dot(normed, qkv_weight[1], preferred_element_type=jnp.float32).astype(jnp.bfloat16)
    values = jnp.dot(normed, qkv_weight[2], preferred_element_type=jnp.float32).astype(jnp.bfloat16)
    query, keys, values = lax.optimization_barrier((query, keys, values))
    padding = jnp.zeros((SPAN, HEADS * HD), jnp.bfloat16)
    keys_pad = jnp.concatenate([padding, keys, padding], axis=0)
    values_pad = jnp.concatenate([padding, values, padding], axis=0)
    zero_count = jnp.zeros((1,), jnp.int32)
    counts_pad = jnp.concatenate([zero_count, frame_counts.astype(jnp.int32), zero_count])
    frame = jnp.arange(3 * SPAN, dtype=jnp.int32) % SPAN // P_SIZE

    def one_stretch(stretch):
        start = (stretch * SPAN).astype(jnp.int32)
        own = lax.dynamic_slice_in_dim(query, start, SPAN, 0).reshape(SPAN, HEADS, HD)
        near_keys = lax.dynamic_slice_in_dim(keys_pad, start, 3 * SPAN, 0).reshape(3 * SPAN, HEADS, HD)
        near_values = lax.dynamic_slice_in_dim(values_pad, start, 3 * SPAN, 0).reshape(3 * SPAN, HEADS, HD)
        counts_three = lax.dynamic_slice(counts_pad, (stretch.astype(jnp.int32),), (3,))
        live = frame < jnp.repeat(counts_three, SPAN)
        return attend(own, near_keys, near_values, live)
    attn = lax.map(one_stretch, jnp.arange(QUEUE, dtype=jnp.int32)).reshape(QUEUE * SPAN, HEADS * HD)
    proj = jnp.dot(attn, out_weight, preferred_element_type=jnp.float32).reshape(QUEUE, SPAN, D)
    updated = (rows + gate[:, None, :] * proj).astype(jnp.bfloat16)
    return jnp.concatenate([updated[1:], fresh[None]], axis=0).reshape(QUEUE * SPAN, D)
```

```python
import functools
import math

import jax
import jax.numpy as jnp
from jax import lax
from jax.experimental import pallas as pl
from jax.experimental.pallas import tpu as pltpu
from jax.sharding import PartitionSpec as P

HD = 64
P_SIZE = 256
PAIR = 2 * HD
NEG = -1e30
BOTH = ("queue", "heads")
MIB = 1024 * 1024


def embed_levels(levels, width):
    halfway = width // 2
    freqs = jnp.exp(-math.log(10000.0) * jnp.arange(halfway, dtype=jnp.float32) / halfway)
    angles = levels.astype(jnp.float32)[:, None] * freqs[None, :]
    return jax.nn.silu(jnp.concatenate([jnp.cos(angles), jnp.sin(angles)], axis=1)).astype(
        jnp.bfloat16
    )


def routed(array, queue_len, members, target):
    pairs = []
    for slot in range(queue_len):
        for member in range(members):
            goal = target(slot, member // 2, member % 2)
            if goal is not None and 0 <= goal[0] < queue_len:
                pairs.append((slot * members + member, goal[0] * members + goal[1] * 2 + goal[2]))
    return lax.ppermute(array, BOTH, pairs)


def low_lanes(shape):
    return lax.broadcasted_iota(jnp.int32, shape, len(shape) - 1) < HD


def qkv_kernel(where_ref, first_ref, second_ref, scale_ref, shift_ref, weight_hbm, query_ref, kv_ref, weight, sems):
    parity = where_ref[0]
    order = where_ref[1]
    copies = []
    for kind in range(3):
        for part in range(2):
            start = pl.multiple_of(2 * parity * PAIR, PAIR) if part == 0 else PAIR
            column = (kind if part == 0 else 3 + kind) * PAIR
            copies.append(
                pltpu.make_async_copy(
                    weight_hbm.at[kind, :, pl.ds(start, PAIR)],
                    weight.at[:, pl.ds(column, PAIR)],
                    sems.at[2 * kind + part],
                )
            )
    for copy in copies:
        copy.start()
    half = first_ref.shape[0]

    def normalised(ref):
        states = ref[...].astype(jnp.float32)
        mean = jnp.mean(states, axis=1, keepdims=True)
        centred = states - mean
        var = jnp.mean(centred * centred, axis=1, keepdims=True)
        return (centred * lax.rsqrt(var + 1e-05) * scale_ref[...] + shift_ref[...]).astype(jnp.bfloat16)

    def project(normed, block):
        out = jnp.dot(normed, weight[...], preferred_element_type=jnp.float32)
        low = low_lanes((half, PAIR))
        rows = pl.ds(pl.multiple_of(block * half, half), half)
        q_pair, k_pair, v_pair, q_mid, k_mid, v_mid = [out[:, i * PAIR : (i + 1) * PAIR] for i in range(6)]
        even = parity == 0
        turned = [pltpu.roll(a, HD, 1) for a in (q_mid, k_mid, v_mid)]
        q_one = jnp.where(even, q_mid, turned[0])
        k_one = jnp.where(even, k_mid, turned[1])
        v_one = jnp.where(even, turned[2], v_mid)
        query_ref[rows, :PAIR] = (q_pair.astype(jnp.bfloat16) * HD ** (-0.5)).astype(jnp.bfloat16)
        query_ref[rows, PAIR:] = jnp.where(
            low, q_one.astype(jnp.bfloat16).astype(jnp.float32) * HD ** (-0.5), 0.0
        ).astype(jnp.bfloat16)
        kv_ref[rows, :PAIR] = k_pair.astype(jnp.bfloat16)
        kv_ref[rows, PAIR : 2 * PAIR] = v_pair.astype(jnp.bfloat16)
        kv_ref[rows, 2 * PAIR :] = jnp.where(low, k_one, v_one).astype(jnp.bfloat16)

    normed_first = normalised(first_ref)
    for copy in copies:
        copy.wait()
    project(normed_first, order)
    project(normalised(second_ref), 1 - order)


def qkv(where, first, second, scale, shift, weight):
    half, width = first.shape
    vmem = pl.BlockSpec(memory_space=pltpu.VMEM)
    return pl.pallas_call(
        qkv_kernel,
        out_shape=(
            jax.ShapeDtypeStruct((2 * half, 2 * PAIR), jnp.bfloat16),
            jax.ShapeDtypeStruct((2 * half, 3 * PAIR), jnp.bfloat16),
        ),
        in_specs=[pl.BlockSpec(memory_space=pltpu.SMEM)] + [vmem] * 4 + [pl.BlockSpec(memory_space=pl.ANY)],
        out_specs=(vmem, vmem),
        scratch_shapes=[
            pltpu.VMEM((width, 6 * PAIR), jnp.bfloat16),
            pltpu.SemaphoreType.DMA((6,)),
        ],
        compiler_params=pltpu.CompilerParams(vmem_limit_bytes=40 * MIB),
        cost_estimate=pl.CostEstimate(
            flops=2 * 2 * half * width * 6 * PAIR, bytes_accessed=9 * MIB, transcendentals=0
        ),
    )(where, first, second, scale, shift, weight)


def head_views(query, kv):
    low = low_lanes((query.shape[0], PAIR))
    q_pair, q_one = query[:, :PAIR], query[:, PAIR:]
    k_pair, v_pair, mid = kv
    zero = jnp.zeros_like(q_pair)
    return (
        (jnp.where(low, q_pair, zero), k_pair, v_pair),
        (jnp.where(low, zero, q_pair), k_pair, v_pair),
        (q_one, mid, mid),
    )


def scores_of(query, keys):
    return lax.dot_general(query, keys, (((1,), (1,)), ((), ())), preferred_element_type=jnp.float32)


def local_kernel(counts_ref, qo_ref, qt_ref, kvo_ref, kvt_ref, oo, mo, lo, ot, mt, lt):
    span = kvo_ref.shape[0]
    tile = 256
    lane = lax.broadcasted_iota(jnp.int32, (1, 2 * span), 1)
    live_own = (lane < counts_ref[0] * P_SIZE) & (lane < span)
    live_other = (lane >= span) & (lane - span < counts_ref[1] * P_SIZE)
    bias = jnp.where(live_own | live_other, 0.0, NEG)
    kv = [
        jnp.concatenate([kvo_ref[:, i * PAIR : (i + 1) * PAIR], kvt_ref[:, i * PAIR : (i + 1) * PAIR]], axis=0)
        for i in range(3)
    ]
    low = low_lanes((tile, PAIR))
    for q_ref, o_ref, m_ref, l_ref in ((qo_ref, oo, mo, lo), (qt_ref, ot, mt, lt)):
        for start in range(0, span, tile):
            rows = pl.ds(start, tile)
            outs = []
            for query, keys, values in head_views(q_ref[rows, :], kv):
                scores = scores_of(query, keys) + bias
                peak = jnp.max(scores, axis=1, keepdims=True)
                probs = jnp.exp(scores - peak)
                total = jnp.sum(probs, axis=1, keepdims=True)
                numer = jnp.dot(probs.astype(jnp.bfloat16), values, preferred_element_type=jnp.float32)
                outs.append((numer, peak, total))
            (na, pa, ta), (nb, pb, tb), (nc, pc, tc) = outs
            o_ref[rows, :PAIR] = jnp.where(low, na, nb)
            m_ref[rows, :PAIR] = jnp.where(low, pa, pb)
            l_ref[rows, :PAIR] = jnp.where(low, ta, tb)
            o_ref[rows, PAIR:] = nc
            m_ref[rows, PAIR:] = jnp.broadcast_to(pc, (tile, PAIR))
            l_ref[rows, PAIR:] = jnp.broadcast_to(tc, (tile, PAIR))


def local_attention(counts, q_own, q_other, kv_own, kv_other):
    span = q_own.shape[0]
    vmem = pl.BlockSpec(memory_space=pltpu.VMEM)
    part = jax.ShapeDtypeStruct((span, 2 * PAIR), jnp.float32)
    return pl.pallas_call(
        local_kernel,
        out_shape=(part,) * 6,
        in_specs=[pl.BlockSpec(memory_space=pltpu.SMEM)] + [vmem] * 4,
        out_specs=(vmem,) * 6,
        compiler_params=pltpu.CompilerParams(vmem_limit_bytes=32 * MIB),
        cost_estimate=pl.CostEstimate(
            flops=8 * 3 * 4 * span * span * 256, bytes_accessed=5 * MIB, transcendentals=12 * span * span
        ),
    )(counts, q_own, q_other, kv_own, kv_other)


def remote_kernel(count_ref, q_ref, kv_ref, o_ref, m_ref, l_ref, piece_ref):
    span = kv_ref.shape[0]
    tile = 256
    lane = lax.broadcasted_iota(jnp.int32, (1, span), 1)
    bias = jnp.where(lane < count_ref[0] * P_SIZE, 0.0, NEG)
    kv = [kv_ref[:, i * PAIR : (i + 1) * PAIR] for i in range(3)]
    low = low_lanes((tile, PAIR))
    ones = []
    for start in range(0, span, tile):
        rows = pl.ds(start, tile)
        outs = []
        for head, (query, keys, values) in enumerate(head_views(q_ref[rows, :], kv)):
            at = head * HD if head < 2 else PAIR
            before = m_ref[rows, at : at + 1]
            scores = scores_of(query, keys) + bias
            peak = jnp.maximum(jnp.max(scores, axis=1, keepdims=True), before)
            probs = jnp.exp(scores - peak)
            fade = jnp.exp(before - peak)
            total = jnp.sum(probs, axis=1, keepdims=True) + fade * l_ref[rows, at : at + 1]
            numer = jnp.dot(probs.astype(jnp.bfloat16), values, preferred_element_type=jnp.float32)
            block = o_ref[rows, :PAIR] if head < 2 else o_ref[rows, PAIR:]
            outs.append((numer + fade * block) / total)
        piece_ref[rows, :] = jnp.where(low, outs[0], outs[1]).astype(jnp.bfloat16)
        ones.append(outs[2])
    piece_ref[span:, :] = jnp.where(low, pltpu.roll(ones[0], HD, 1), ones[1]).astype(jnp.bfloat16)


def remote_attention(count, query, kv, o, m, l):
    span = query.shape[0]
    vmem = pl.BlockSpec(memory_space=pltpu.VMEM)
    return pl.pallas_call(
        remote_kernel,
        out_shape=jax.ShapeDtypeStruct((span + span // 2, PAIR), jnp.bfloat16),
        in_specs=[pl.BlockSpec(memory_space=pltpu.SMEM)] + [vmem] * 5,
        out_specs=vmem,
        compiler_params=pltpu.CompilerParams(vmem_limit_bytes=32 * MIB),
        cost_estimate=pl.CostEstimate(
            flops=4 * 3 * span * span * 256, bytes_accessed=2 * MIB, transcendentals=3 * span * span
        ),
    )(count, query, kv, o, m, l)


def out_kernel(
    where_ref,
    *refs,
):
    (
        w_own, w_twin, w_far0, w_far1, w_fart0, w_fart1,
        p1, p2, p3, p4, t1, t2, t3, t4,
        residual_ref, gate_ref, fresh_ref, out_ref, attn, weight,
    ) = refs
    even = where_ref[1] == 0
    last = where_ref[2] == 1
    z_half = where_ref[3]
    span = residual_ref.shape[0]
    half = span // 2
    block = w_own.shape[0]

    @pl.when(pl.program_id(0) == 0)
    def _():
        low = low_lanes((half, PAIR))
        for index, (other, own) in enumerate(((p4, p1), (p3, p2), (t4, t1), (t3, t2))):
            first = jnp.where(even, other[...], own[...])
            second = jnp.where(even, own[...], other[...])
            base = index * 3 * PAIR
            attn[:, base : base + PAIR] = first[:span]
            attn[:, base + 2 * PAIR : base + 3 * PAIR] = second[:span]
            one_f, one_s = first[span:].astype(jnp.float32), second[span:].astype(jnp.float32)
            attn[:half, base + PAIR : base + 2 * PAIR] = jnp.where(
                low, one_f, pltpu.roll(one_s, HD, 1)
            ).astype(jnp.bfloat16)
            attn[half:, base + PAIR : base + 2 * PAIR] = jnp.where(
                low, pltpu.roll(one_f, HD, 1), one_s
            ).astype(jnp.bfloat16)

    near = pl.multiple_of(z_half * (block // 2), block // 2)
    away = pl.multiple_of((1 - z_half) * (block // 2), block // 2)
    weight[:block, :] = w_own[...]
    weight[pl.ds(block + near, block // 2), :] = w_far0[...]
    weight[pl.ds(block + away, block // 2), :] = w_far1[...]
    weight[2 * block : 3 * block, :] = w_twin[...]
    weight[pl.ds(3 * block + near, block // 2), :] = w_fart0[...]
    weight[pl.ds(3 * block + away, block // 2), :] = w_fart1[...]
    summed = jnp.dot(attn[...], weight[...], preferred_element_type=jnp.float32)
    updated = residual_ref[...].astype(jnp.float32) + gate_ref[...] * summed
    out_ref[...] = jnp.where(last, fresh_ref[...], updated.astype(jnp.bfloat16))


def out_projection(where, out_weight, w_twin, far, pieces, residual, gate, fresh):
    span, share = residual.shape
    block = out_weight.shape[0]
    tile = 256
    steps = share // tile
    whole = lambda a: pl.BlockSpec(a.shape, lambda j, w: (0,) * a.ndim)
    cols = lambda rows: pl.BlockSpec((rows, tile), lambda j, w: (0, j))
    by_core = pl.BlockSpec((block // 2, tile), lambda j, w: (0, w[4] * steps + j))
    by_member = pl.BlockSpec((block, tile), lambda j, w: (0, w[0] * steps + j))
    return pl.pallas_call(
        out_kernel,
        out_shape=jax.ShapeDtypeStruct((span, share), jnp.bfloat16),
        grid_spec=pltpu.PrefetchScalarGridSpec(
            num_scalar_prefetch=1,
            grid=(steps,),
            in_specs=[by_member, cols(block)]
            + [by_core] * 4
            + [whole(a) for a in pieces]
            + [cols(span), cols(1), cols(span)],
            out_specs=cols(span),
            scratch_shapes=[
                pltpu.VMEM((span, 4 * block), jnp.bfloat16),
                pltpu.VMEM((4 * block, tile), jnp.bfloat16),
            ],
        ),
        compiler_params=pltpu.CompilerParams(vmem_limit_bytes=32 * MIB),
        cost_estimate=pl.CostEstimate(
            flops=2 * span * 4 * block * share, bytes_accessed=7 * MIB, transcendentals=0
        ),
    )(where, out_weight, w_twin, *far, *pieces, residual, gate, fresh)


def on_device(hidden, levels, frame_counts, mod_weight, qkv_weight, out_weight, fresh):
    rows, width = hidden.shape
    slot = lax.axis_index("queue")
    queue_len = lax.axis_size("queue")
    member = lax.axis_index("heads")
    members = lax.axis_size("heads")
    share = width // members
    parity, core, y_hi = slot % 2, member % 2, member // 2
    z_half = (slot // 8) % 2
    half = rows // 2
    route = functools.partial(routed, queue_len=queue_len, members=members)
    twin = lambda a: route(a, target=lambda s, y, k: (s, y, 1 - k))

    mine = lax.dynamic_slice(hidden, (core * half, 0), (half, width))
    other_mine = route(mine, target=lambda s, y, k: (s ^ 1, y ^ k, k))
    own_share = lax.dynamic_slice_in_dim(hidden, member * share, share, 1)
    residual_near = route(own_share, target=lambda s, y, k: (s - 2 if s % 2 == 0 else s, y, k))

    modulation = jnp.dot(
        embed_levels(levels, mod_weight.shape[0]), mod_weight, preferred_element_type=jnp.float32
    )
    columns = modulation.shape[1]
    swapped = modulation.reshape(queue_len // 2, 2, columns)[:, ::-1].reshape(queue_len, columns)
    following = jnp.roll(modulation, -1, axis=0)
    rows_three = lax.all_to_all(
        jnp.concatenate([modulation, swapped, following], axis=1), "queue", 0, 0, tiled=True
    )
    mod_own, mod_other, mod_next = [
        rows_three[:, i * columns : (i + 1) * columns].reshape(1, queue_len * columns) for i in range(3)
    ]
    gate = lax.dynamic_slice_in_dim(mod_next, 2 * width + member * share, share, 1)

    other_twin = twin(other_mine)
    residual = route(residual_near, target=lambda s, y, k: (s ^ 1, y, k))
    far_mine = lax.dynamic_slice(
        out_weight, (z_half * (out_weight.shape[0] // 2), (1 - y_hi) * 2 * share), (out_weight.shape[0] // 2, 2 * share)
    )
    w_far0 = route(far_mine, target=lambda s, y, k: (s ^ 1, 1 - y, k))
    w_far1 = route(w_far0, target=lambda s, y, k: (s ^ 8, y, k))
    w_twin = twin(lax.dynamic_slice_in_dim(out_weight, (y_hi * 2 + 1 - core) * share, share, 1))
    w_fart0 = twin(w_far0)
    w_fart1 = twin(w_far1)

    def qkv_of(order, first, second, mod):
        return qkv(
            jnp.stack([parity, order]).astype(jnp.int32),
            first,
            second,
            1.0 + mod[:, width : 2 * width],
            mod[:, :width],
            qkv_weight,
        )

    q_own, kv_own = qkv_of(jnp.int32(0), hidden[:half], hidden[half:], mod_own)
    kv_far = route(kv_own, target=lambda s, y, k: (s - 2 if s % 2 == 0 else s + 2, y, k))
    q_other, kv_other = qkv_of(core, other_mine, other_twin, mod_other)
    kv_back = route(kv_other, target=lambda s, y, k: (s + 2 if s % 2 == 0 else s - 2, y, k))

    counts_pad = jnp.pad(frame_counts.astype(jnp.int32), (2, 2))
    step = 1 - 2 * parity
    count_at = lambda where: lax.dynamic_slice(counts_pad, (where + 2,), (1,))
    counts_pair = jnp.concatenate([count_at(slot), count_at(slot + step)])
    oo, mo, lo, ot, mt, lt = local_attention(counts_pair, q_own, q_other, kv_own, kv_other)
    attn_other = remote_attention(count_at(slot + 2 * step), q_other, kv_far, ot, mt, lt)
    p3 = route(attn_other, target=lambda s, y, k: (s if s % 2 == 0 else s - 2, 1 - y, k))
    p4 = route(attn_other, target=lambda s, y, k: (s if s % 2 == 0 else s - 2, y, k))
    attn_own = remote_attention(count_at(slot - step), q_own, kv_back, oo, mo, lo)
    p1 = route(attn_own, target=lambda s, y, k: (s - 1, y, k))
    p2 = route(attn_own, target=lambda s, y, k: (s - 1, 1 - y, k))
    pieces = [p1, p2, p3, p4]
    pieces = pieces + [twin(a) for a in pieces]

    where = jnp.stack(
        [member, parity, (slot == queue_len - 1).astype(jnp.int32), z_half, core]
    ).astype(jnp.int32)
    return out_projection(
        where, out_weight, w_twin, [w_far0, w_far1, w_fart0, w_fart1], pieces, residual, gate, fresh
    )


def solution(mesh):
    placed = (
        P("queue", None),
        P(),
        P(),
        P(None, "queue"),
        P(None, None, "heads"),
        P("heads", None),
        P(None, "heads"),
    )
    return jax.shard_map(
        on_device, mesh=mesh, in_specs=placed, out_specs=P("queue", "heads"), check_vma=False
    )
```

```python
import functools
import math

import jax
import jax.numpy as jnp
from jax import lax
from jax.experimental import pallas as pl
from jax.experimental.pallas import tpu as pltpu
from jax.sharding import PartitionSpec as P

HD = 64
P_SIZE = 256
PAIR = 2 * HD
NEG = -1e30
BOTH = ("queue", "heads")
MIB = 1024 * 1024


def embed_levels(levels, width):
    halfway = width // 2
    freqs = jnp.exp(-math.log(10000.0) * jnp.arange(halfway, dtype=jnp.float32) / halfway)
    angles = levels.astype(jnp.float32)[:, None] * freqs[None, :]
    return jax.nn.silu(jnp.concatenate([jnp.cos(angles), jnp.sin(angles)], axis=1)).astype(
        jnp.bfloat16
    )


def routed(array, queue_len, members, target):
    pairs = []
    for slot in range(queue_len):
        for member in range(members):
            goal = target(slot, member // 2, member % 2)
            if goal is not None and 0 <= goal[0] < queue_len:
                pairs.append((slot * members + member, goal[0] * members + goal[1] * 2 + goal[2]))
    return lax.ppermute(array, BOTH, pairs)


def low_lanes(shape):
    return lax.broadcasted_iota(jnp.int32, shape, len(shape) - 1) < HD


def copies_of(source, target, sems, chunks, first=0):
    step = source.shape[0] // chunks
    return [
        pltpu.make_async_copy(
            source.at[pl.ds(i * step, step), :], target.at[pl.ds(i * step, step), :], sems.at[first + i]
        )
        for i in range(chunks)
    ]


def any_spec():
    return pl.BlockSpec(memory_space=pl.ANY)


def far(array):
    return pltpu.with_memory_space_constraint(array, pltpu.HBM)


def near(array):
    return pltpu.with_memory_space_constraint(array, pltpu.VMEM)


def near_out(shape, dtype=jnp.bfloat16):
    return pltpu.VMEM(shape, dtype)


def cost(flops, moved, transcendentals=0):
    return pl.CostEstimate(flops=flops, bytes_accessed=moved, transcendentals=transcendentals)


def vmem_spec():
    return pl.BlockSpec(memory_space=pltpu.VMEM)


def smem_spec():
    return pl.BlockSpec(memory_space=pltpu.SMEM)


def lanes_at(index, size):
    return pl.ds(pl.multiple_of(index * size, size), size)


def slices_kernel(where_ref, hidden, out_weight, mine, share_out, far_out, sems):
    member, core, y_hi, z_half = where_ref[0], where_ref[1], where_ref[2], where_ref[3]
    half, width, deep = mine.shape[0], share_out.shape[1], far_out.shape[0]
    copies = (
        copies_of(hidden.at[lanes_at(core, half), :], mine, sems, 4)
        + copies_of(hidden.at[:, lanes_at(member, width)], share_out, sems, 4, 4)
        + copies_of(out_weight.at[lanes_at(z_half, deep), lanes_at(1 - y_hi, 2 * width)], far_out, sems, 2, 8)
    )
    for copy in copies:
        copy.start()
    for copy in copies:
        copy.wait()


def slices(where, hidden, out_weight, members):
    rows, width = hidden.shape
    share, depth = width // members, out_weight.shape[0]
    return pl.pallas_call(
        slices_kernel,
        out_shape=(
            near_out((rows // 2, width)),
            near_out((rows, share)),
            near_out((depth // 2, 2 * share)),
        ),
        in_specs=[smem_spec(), any_spec(), any_spec()],
        out_specs=(vmem_spec(),) * 3,
        scratch_shapes=[pltpu.SemaphoreType.DMA((10,))],
        compiler_params=pltpu.CompilerParams(vmem_limit_bytes=2 * MIB),
        cost_estimate=cost(0, 4 * MIB),
    )(where, far(hidden), far(out_weight))


ROW = 512


def modulate_kernel(emb_ref, mod_ref, payload, rows_ref):
    rows_ref[...] = jnp.zeros_like(rows_ref)
    columns = mod_ref.shape[0]
    rows_ref[:, :columns] = lax.dot_general(
        emb_ref[...], mod_ref[...], (((1,), (1,)), ((), ())), preferred_element_type=jnp.float32
    )
    rows = rows_ref[...]
    slots = rows.shape[0]
    even = lax.broadcasted_iota(jnp.int32, rows.shape, 0) % 2 == 0
    following = pltpu.roll(rows, slots - 1, 0)
    partner = jnp.where(even, following, pltpu.roll(rows, 1, 0))
    joined = rows + pltpu.roll(partner, columns, 1) + pltpu.roll(following, 2 * columns, 1)
    for slot in range(slots):
        payload[slot] = joined[slot : slot + 1, :]


def modulate(emb, mod_weight):
    return pl.pallas_call(
        modulate_kernel,
        out_shape=jax.ShapeDtypeStruct((emb.shape[0], 1, ROW), jnp.float32),
        in_specs=[vmem_spec(), vmem_spec()],
        out_specs=vmem_spec(),
        scratch_shapes=[pltpu.VMEM((emb.shape[0], ROW), jnp.float32)],
        compiler_params=pltpu.CompilerParams(vmem_limit_bytes=2 * MIB),
        cost_estimate=cost(10**7, MIB),
    )(emb, mod_weight.T)


NORM_ROWS = 16


def spread(rows_ref, part, flat):
    slots = rows_ref.shape[0]
    columns = flat.shape[1] // slots
    step = columns - PAIR
    row = lax.broadcasted_iota(jnp.int32, (8, 2 * PAIR), 0)
    at = lax.broadcasted_iota(jnp.int32, (8, 2 * PAIR), 1) - step * row
    held = (at >= 0) & (at < columns)
    first_row = row[:, :PAIR] == 0
    for i in range(slots // 8):
        block = rows_ref[8 * i : 8 * i + 8, :]
        if part:
            block = pltpu.roll(block, ROW - columns * part, 1)
        turned = pltpu.roll(block, 0, 1, stride=step, stride_axis=0)
        turned = jnp.where(held, turned[:, : 2 * PAIR], 0.0)
        carried = turned[:, PAIR:]
        tiles = turned[:, :PAIR] + jnp.where(first_row, 0.0, pltpu.roll(carried, 1, 0))
        base = 8 * i * columns
        for j in range(8):
            flat[:, base + j * PAIR : base + (j + 1) * PAIR] = tiles[j : j + 1, :]
        flat[:, base + 8 * PAIR : base + 9 * PAIR] = carried[7:8, :]


def qkv_kernel(part, where_ref, rows_ref, *refs):
    if part == 0:
        (source, weight_hbm, out_weight), (held_ref, kv_ref, weight, twin_out) = refs[:3], refs[3:7]
        states_ref, flat, x_sems, w_sems = refs[7:]
        sources = [source]
    else:
        weight, *sources, held_ref, kv_ref, states_ref, flat, x_sems = refs
    even = where_ref[4] == 0
    order = where_ref[1]
    rows, width = states_ref.shape
    part_rows = rows // len(sources)
    chunks = 8 // len(sources)
    x_copies = []
    for index, source in enumerate(sources):
        start = index * part_rows if len(sources) == 1 else pl.multiple_of(
            (order if index == 0 else 1 - order) * part_rows, part_rows
        )
        x_copies += copies_of(source, states_ref.at[pl.ds(start, part_rows), :], x_sems, chunks, index * chunks)
    for copy in x_copies:
        copy.start()
    w_copies = []
    if part == 0:
        for kind in range(3):
            for piece in range(2):
                start = pl.multiple_of(2 * where_ref[4] * PAIR, PAIR) if piece == 0 else PAIR
                column = (kind if piece == 0 else 3 + kind) * PAIR
                w_copies += copies_of(
                    weight_hbm.at[kind, :, pl.ds(start, PAIR)],
                    weight.at[:, pl.ds(column, PAIR)],
                    w_sems,
                    2,
                    4 * kind + 2 * piece,
                )
        beside = where_ref[2] * 2 + 1 - where_ref[1]
        w_copies += copies_of(out_weight.at[:, lanes_at(beside, twin_out.shape[1])], twin_out, w_sems, 2, 12)
        for copy in w_copies:
            copy.start()
    spread(rows_ref, part, flat)
    scale, shift = 1.0 + flat[:, width : 2 * width], flat[:, :width]
    half = rows // 2
    low = low_lanes((half, PAIR))

    def normalise(first, count):
        for start in range(first, first + count, NORM_ROWS):
            block = pl.ds(start, NORM_ROWS)
            states = states_ref[block, :].astype(jnp.float32)
            mean = jnp.mean(states, axis=1, keepdims=True)
            centred = states - mean
            var = jnp.mean(centred * centred, axis=1, keepdims=True)
            states_ref[block, :] = (centred * lax.rsqrt(var + 1e-05) * scale + shift).astype(jnp.bfloat16)

    def project(first):
        block = pl.ds(first, half)
        out = jnp.dot(states_ref[block, :], weight[...], preferred_element_type=jnp.float32)
        q_pair, k_pair, v_pair, q_mid, k_mid, v_mid = [out[:, i * PAIR : (i + 1) * PAIR] for i in range(6)]
        turned = [pltpu.roll(a, HD, 1) for a in (q_mid, k_mid, v_mid)]
        q_one = jnp.where(even, q_mid, turned[0])
        k_one = jnp.where(even, k_mid, turned[1])
        v_one = jnp.where(even, turned[2], v_mid)
        held_ref[block, :PAIR] = (q_pair.astype(jnp.bfloat16) * HD ** (-0.5)).astype(jnp.bfloat16)
        held_ref[block, PAIR : 2 * PAIR] = (
            jnp.where(low, q_one, 0.0).astype(jnp.bfloat16) * HD ** (-0.5)
        ).astype(jnp.bfloat16)
        for index, lanes in enumerate((k_pair, v_pair, jnp.where(low, k_one, v_one))):
            kv_ref[block, index * PAIR : (index + 1) * PAIR] = lanes.astype(jnp.bfloat16)
            held_ref[block, (2 + index) * PAIR : (3 + index) * PAIR] = lanes.astype(jnp.bfloat16)

    for copy in x_copies:
        copy.wait()
    normalise(0, half)
    for copy in w_copies:
        copy.wait()
    project(0)
    normalise(half, half)
    project(half)


def qkv(part, where, mod_rows, sources, weight, out_weight=None):
    rows, width = sources[0].shape[0] * len(sources), sources[0].shape[1]
    outs = [near_out((rows, 8 * PAIR)), near_out((rows, 3 * PAIR))]
    scratch = [
        pltpu.VMEM((rows, width), jnp.bfloat16),
        pltpu.VMEM((1, 3 * width), jnp.float32),
        pltpu.SemaphoreType.DMA((8,)),
    ]
    if part == 0:
        outs += [near_out((width, 6 * PAIR)), near_out((out_weight.shape[0], width // 4))]
        scratch.append(pltpu.SemaphoreType.DMA((14,)))
        inputs = [far(a) for a in (sources[0], weight, out_weight)]
        specs = [any_spec()] * 3
    else:
        inputs = [near(weight), *sources]
        specs = [vmem_spec()] + [any_spec()] * len(sources)
    return pl.pallas_call(
        functools.partial(qkv_kernel, part),
        out_shape=tuple(outs),
        in_specs=[smem_spec(), vmem_spec()] + specs,
        out_specs=(vmem_spec(),) * len(outs),
        scratch_shapes=scratch,
        compiler_params=pltpu.CompilerParams(vmem_limit_bytes=12 * MIB),
        cost_estimate=cost(2 * rows * width * 6 * PAIR, 9 * MIB),
    )(where, mod_rows, *inputs)


def head_views(query, kv):
    low = low_lanes((query.shape[0], PAIR))
    q_pair, q_one = query[:, :PAIR], query[:, PAIR:]
    k_pair, v_pair, mid = kv
    zero = jnp.zeros_like(q_pair)
    return (
        (jnp.where(low, q_pair, zero), k_pair, v_pair),
        (jnp.where(low, zero, q_pair), k_pair, v_pair),
        (q_one, mid, mid),
    )


def scores_of(query, keys):
    return lax.dot_general(query, keys, (((1,), (1,)), ((), ())), preferred_element_type=jnp.float32)


def attend_kernel(queries, where_ref, counts_ref, own_ref, other_ref, remote_ref, piece_ref):
    span = own_ref.shape[0]
    tile = 256
    q_ref = (own_ref, other_ref)[queries]
    lane = lax.broadcasted_iota(jnp.int32, (1, span), 1)
    slot = where_ref[6]
    step = 1 - 2 * where_ref[4]

    def count(at):
        inside = (at >= 0) & (at < counts_ref.shape[0])
        return jnp.where(inside, counts_ref[jnp.where(inside, at, 0)], 0)

    counts = [count(slot), count(slot + step), count(slot - step if queries == 0 else slot + 2 * step)]
    bias = jnp.concatenate([jnp.where(lane < c * P_SIZE, 0.0, NEG) for c in counts], axis=1)
    kv = [
        jnp.concatenate(
            [
                own_ref[:, (2 + i) * PAIR : (3 + i) * PAIR],
                other_ref[:, (2 + i) * PAIR : (3 + i) * PAIR],
                remote_ref[:, i * PAIR : (i + 1) * PAIR],
            ],
            axis=0,
        )
        for i in range(3)
    ]
    low = low_lanes((tile, PAIR))
    ones = []
    for start in range(0, span, tile):
        rows = pl.ds(start, tile)
        outs = []
        for query, keys, values in head_views(q_ref[rows, : 2 * PAIR], kv):
            scores = scores_of(query, keys) + bias
            peak = jnp.max(scores, axis=1, keepdims=True)
            probs = jnp.exp(scores - peak)
            total = jnp.sum(probs, axis=1, keepdims=True)
            numer = jnp.dot(probs.astype(jnp.bfloat16), values, preferred_element_type=jnp.float32)
            outs.append(numer / total)
        piece_ref[rows, :] = jnp.where(low, outs[0], outs[1]).astype(jnp.bfloat16)
        ones.append(outs[2])
    piece_ref[span:, :] = jnp.where(low, pltpu.roll(ones[0], HD, 1), ones[1]).astype(jnp.bfloat16)


def attention(queries, where, counts, own, other, remote):
    span = own.shape[0]
    return pl.pallas_call(
        functools.partial(attend_kernel, queries),
        out_shape=near_out((span + span // 2, PAIR)),
        in_specs=[smem_spec()] * 2 + [vmem_spec()] * 3,
        out_specs=vmem_spec(),
        compiler_params=pltpu.CompilerParams(vmem_limit_bytes=16 * MIB),
        cost_estimate=cost(12 * 3 * span * span * 256, 3 * MIB, 9 * span * span),
    )(where, counts, near(own), near(other), remote)


def tail_kernel(
    where_ref, rows_ref, out_weight, w_twin, near0, near1, twin0, twin1, arrived, first, second, gathered, residual,
    gate, flat, sems,
):
    member, core, z_half, parity = where_ref[0], where_ref[1], where_ref[3], where_ref[4]
    share = gathered.shape[1]
    width = flat.shape[1] // 3
    block, half, part = out_weight.shape[0], near0.shape[0], first.shape[0]
    mine = pl.ds(pl.multiple_of(core * share, share), share)
    place = lambda base, first: pl.ds(pl.multiple_of(base + first * half, half), half)
    own = pl.ds(pl.multiple_of(member * share, share), share)
    copies = (
        copies_of(out_weight.at[:, own], gathered.at[pl.ds(0, block), :], sems, 2)
        + copies_of(w_twin, gathered.at[pl.ds(2 * block, block), :], sems, 2, 2)
        + copies_of(near0.at[:, mine], gathered.at[place(block, z_half), :], sems, 1, 4)
        + copies_of(near1.at[:, mine], gathered.at[place(block, 1 - z_half), :], sems, 1, 5)
        + copies_of(twin0.at[:, mine], gathered.at[place(3 * block, z_half), :], sems, 1, 6)
        + copies_of(twin1.at[:, mine], gathered.at[place(3 * block, 1 - z_half), :], sems, 1, 7)
    )
    for copy in copies:
        copy.start()

    @pl.when(parity == 0)
    def _():
        rows = lambda index: pl.ds(pl.multiple_of(index * part, part), part)
        held = copies_of(first.at[:, own], residual.at[rows(core), :], sems, 2, 8) + copies_of(
            second.at[:, own], residual.at[rows(1 - core), :], sems, 2, 10
        )
        for copy in held:
            copy.start()
        for copy in held:
            copy.wait()

    @pl.when(parity == 1)
    def _():
        held = copies_of(arrived, residual, sems, 4, 8)
        for copy in held:
            copy.start()
        for copy in held:
            copy.wait()

    spread(rows_ref, 2, flat)
    gate[...] = flat[:, pl.ds(pl.multiple_of(2 * width + member * share, PAIR), share)]
    for copy in copies:
        copy.wait()


def tail_inputs(where, mod_rows, out_weight, w_twin, near0, near1, twin0, twin1, arrived, first, second):
    block, share = w_twin.shape
    width = out_weight.shape[1]
    return pl.pallas_call(
        tail_kernel,
        out_shape=(near_out((4 * block, share)), near_out(arrived.shape), near_out((1, share), jnp.float32)),
        in_specs=[smem_spec(), vmem_spec()] + [any_spec()] * 9,
        out_specs=(vmem_spec(),) * 3,
        scratch_shapes=[pltpu.VMEM((1, 3 * width), jnp.float32), pltpu.SemaphoreType.DMA((12,))],
        compiler_params=pltpu.CompilerParams(vmem_limit_bytes=2 * MIB),
        cost_estimate=cost(0, 5 * MIB),
    )(where, mod_rows, far(out_weight), w_twin, near0, near1, twin0, twin1, arrived, first, second)


def heads_in_order(even, other, own, span, held=None):
    half = span // 2
    low = low_lanes((half, PAIR))
    first = jnp.where(even, (other if held is None else held)[...], own[...])
    second = jnp.where(even, own[...], other[...])
    one_f, one_s = first[span:].astype(jnp.float32), second[span:].astype(jnp.float32)
    middle = jnp.concatenate(
        [
            jnp.where(low, one_f, pltpu.roll(one_s, HD, 1)),
            jnp.where(low, pltpu.roll(one_f, HD, 1), one_s),
        ],
        axis=0,
    ).astype(jnp.bfloat16)
    return jnp.concatenate([first[:span], middle, second[:span]], axis=1)


def first_out_kernel(where_ref, p1, p2, p3, p4, held, weight, partial):
    even = where_ref[4] == 0
    span = partial.shape[0]
    block = 3 * PAIR
    attn = jnp.concatenate(
        [heads_in_order(even, p4, p1, span, held), heads_in_order(even, p3, p2, span)], axis=1
    )
    partial[...] = jnp.dot(attn, weight[: 2 * block, :], preferred_element_type=jnp.float32)


def first_out(where, pieces, weight):
    span, share = pieces[0].shape[0] * 2 // 3, weight.shape[1]
    return pl.pallas_call(
        first_out_kernel,
        out_shape=near_out((span, share), jnp.float32),
        in_specs=[smem_spec()] + [vmem_spec()] * 6,
        out_specs=vmem_spec(),
        compiler_params=pltpu.CompilerParams(vmem_limit_bytes=8 * MIB),
        cost_estimate=cost(512 * 768 * 768 * 2, 3 * MIB),
    )(where, *[near(a) for a in pieces], near(weight))


def last_out_kernel(where_ref, p1, p2, p3, p4, held, weight, partial, residual, gate, fresh, out, ready, sems):
    even = where_ref[4] == 0
    last = where_ref[5] == 1
    span = partial.shape[0]
    block = 3 * PAIR
    tiles = 4
    tile = span // tiles

    @pl.when(last)
    def _():
        for source, target in ((fresh, ready), (ready, out)):
            copies = copies_of(source, target, sems, tiles)
            for copy in copies:
                copy.start()
            for copy in copies:
                copy.wait()

    @pl.when(jnp.logical_not(last))
    def _():
        attn = jnp.concatenate(
            [heads_in_order(even, p4, p1, span, held), heads_in_order(even, p3, p2, span)], axis=1
        )
        copies = copies_of(ready, out, sems, tiles)
        for i in range(tiles):
            rows = slice(i * tile, (i + 1) * tile)
            summed = partial[rows, :] + jnp.dot(
                attn[rows], weight[2 * block :, :], preferred_element_type=jnp.float32
            )
            ready[rows, :] = (residual[rows, :].astype(jnp.float32) + gate[...] * summed).astype(jnp.bfloat16)
            copies[i].start()
        for copy in copies:
            copy.wait()


def last_out(where, pieces, weight, partial, residual, gate, fresh):
    span, share = partial.shape
    return pl.pallas_call(
        last_out_kernel,
        out_shape=jax.ShapeDtypeStruct((span, share), jnp.bfloat16),
        in_specs=[smem_spec()] + [vmem_spec()] * 9 + [any_spec()],
        out_specs=any_spec(),
        scratch_shapes=[pltpu.VMEM((span, share), jnp.bfloat16), pltpu.SemaphoreType.DMA((4,))],
        compiler_params=pltpu.CompilerParams(vmem_limit_bytes=8 * MIB),
        cost_estimate=cost(512 * 768 * 768 * 2, 5 * MIB),
    )(where, *[near(a) for a in pieces], near(weight), near(partial), near(residual), near(gate), far(fresh))


def on_device(hidden, levels, frame_counts, mod_weight, qkv_weight, out_weight, fresh):
    rows, width = hidden.shape
    slot = lax.axis_index("queue")
    queue_len = lax.axis_size("queue")
    member = lax.axis_index("heads")
    members = lax.axis_size("heads")
    share = width // members
    parity, core, y_hi = slot % 2, member % 2, member // 2
    z_half = (slot // 8) % 2
    half = rows // 2
    route = functools.partial(routed, queue_len=queue_len, members=members)
    twin = lambda a: route(a, target=lambda s, y, k: (s, y, 1 - k))

    where = jnp.stack(
        [member, core, y_hi, z_half, parity, (slot == queue_len - 1).astype(jnp.int32), slot]
    ).astype(jnp.int32)
    after = lambda a, *b: lax.optimization_barrier((a, *b))[0]
    frame_counts = frame_counts.astype(jnp.int32)

    mine, own_share, far_mine = slices(where, hidden, out_weight, members)
    other_mine = route(mine, target=lambda s, y, k: (s ^ 1, y ^ k, k))

    payload = modulate(embed_levels(levels, mod_weight.shape[0]), mod_weight)
    mod_rows = lax.all_to_all(payload, "queue", 0, 0, tiled=True)[:, 0, :]

    other_twin = twin(after(other_mine, mod_rows))
    w_far0 = route(after(far_mine, mod_rows), target=lambda s, y, k: (s ^ 1, 1 - y, k))
    residual_far = route(
        after(own_share, mod_rows), target=lambda s, y, k: (s - 1, y, k) if s % 2 == 0 else None
    )

    held_own, kv_own, weight, twin_mine = qkv(0, where, mod_rows, [hidden], qkv_weight, out_weight)
    kv_far = route(kv_own, target=lambda s, y, k: (s - 2 if s % 2 == 0 else s + 2, y, k))
    w_twin = twin(twin_mine)
    held_other, kv_other = qkv(1, where, after(mod_rows, kv_own), [other_mine, other_twin], weight)
    kv_back = route(kv_other, target=lambda s, y, k: (s + 2 if s % 2 == 0 else s - 2, y, k))
    w_far0 = after(w_far0, kv_other)
    w_far1 = route(w_far0, target=lambda s, y, k: (s ^ 8, y, k))

    attn_other = attention(1, where, frame_counts, held_own, held_other, kv_far)
    p3 = route(attn_other, target=lambda s, y, k: (s if s % 2 == 0 else s - 2, 1 - y, k))
    p4 = route(attn_other, target=lambda s, y, k: (s, y, 1 - k) if s % 2 == 0 else (s - 2, y, k))
    w_fart0 = twin(after(w_far0, attn_other))
    attn_own = attention(0, after(where, attn_other), frame_counts, held_own, held_other, kv_back)
    p1 = route(attn_own, target=lambda s, y, k: (s - 1, y, k))
    p2 = route(attn_own, target=lambda s, y, k: (s - 1, 1 - y, k))
    w_fart1 = twin(after(w_far1, attn_own))
    weight, residual, gate = tail_inputs(
        where, mod_rows, out_weight, w_twin, w_far0, w_far1, w_fart0, w_fart1, residual_far, other_mine, other_twin
    )
    p1, p2, _ = lax.optimization_barrier((p1, p2, weight))
    partial = first_out(where, [p1, p2, p3, p4, attn_other], weight)
    pieces = [twin(p1), twin(p2), twin(p3)]
    return last_out(where, pieces + [twin(p4), p4], weight, partial, residual, gate, fresh)


def solution(mesh):
    placed = (
        P("queue", None),
        P(),
        P(),
        P(None, "queue"),
        P(None, None, "heads"),
        P("heads", None),
        P(None, "heads"),
    )
    return jax.shard_map(
        on_device, mesh=mesh, in_specs=placed, out_specs=P("queue", "heads"), check_vma=False
    )
```

```python
import functools
import math

import jax
import jax.numpy as jnp
from jax import lax
from jax.experimental import pallas as pl
from jax.experimental.pallas import tpu as pltpu
from jax.sharding import PartitionSpec as P

HD = 64
P_SIZE = 256
PAIR = 2 * HD
NEG = -1e30
BOTH = ("queue", "heads")
MIB = 1024 * 1024


def embed_levels(levels, width):
    halfway = width // 2
    freqs = jnp.exp(-math.log(10000.0) * jnp.arange(halfway, dtype=jnp.float32) / halfway)
    angles = levels.astype(jnp.float32)[:, None] * freqs[None, :]
    return jax.nn.silu(jnp.concatenate([jnp.cos(angles), jnp.sin(angles)], axis=1)).astype(
        jnp.bfloat16
    )


def routed(array, queue_len, members, target):
    pairs = []
    for slot in range(queue_len):
        for member in range(members):
            goal = target(slot, member // 2, member % 2)
            if goal is not None and 0 <= goal[0] < queue_len:
                pairs.append((slot * members + member, goal[0] * members + goal[1] * 2 + goal[2]))
    return lax.ppermute(array, BOTH, pairs)


def low_lanes(shape):
    return lax.broadcasted_iota(jnp.int32, shape, len(shape) - 1) < HD


def copies_of(source, target, sems, chunks, first=0):
    step = source.shape[0] // chunks
    return [
        pltpu.make_async_copy(
            source.at[pl.ds(i * step, step), :], target.at[pl.ds(i * step, step), :], sems.at[first + i]
        )
        for i in range(chunks)
    ]


def any_spec():
    return pl.BlockSpec(memory_space=pl.ANY)


def far(array):
    return pltpu.with_memory_space_constraint(array, pltpu.HBM)


def near(array):
    return pltpu.with_memory_space_constraint(array, pltpu.VMEM)


def near_out(shape, dtype=jnp.bfloat16):
    return pltpu.VMEM(shape, dtype)


def cost(flops, moved, transcendentals=0):
    return pl.CostEstimate(flops=flops, bytes_accessed=moved, transcendentals=transcendentals)


def vmem_spec():
    return pl.BlockSpec(memory_space=pltpu.VMEM)


def smem_spec():
    return pl.BlockSpec(memory_space=pltpu.SMEM)


def lanes_at(index, size):
    return pl.ds(pl.multiple_of(index * size, size), size)


SPLIT = 288


def slices_kernel(where_ref, hidden, out_weight, mine, share_a, share_b, far_out, sems):
    member, core, y_hi = where_ref[0], where_ref[1], where_ref[2]
    half, width = mine.shape[0], share_a.shape[1]
    copies = (
        copies_of(hidden.at[lanes_at(core, half), :], mine, sems, 4)
        + copies_of(hidden.at[pl.ds(0, SPLIT), lanes_at(member, width)], share_a, sems, 2, 4)
        + copies_of(hidden.at[pl.ds(SPLIT, 2 * half - SPLIT), lanes_at(member, width)], share_b, sems, 2, 6)
        + copies_of(out_weight.at[:, lanes_at(1 - y_hi, 2 * width)], far_out, sems, 2, 8)
    )
    for copy in copies:
        copy.start()
    for copy in copies:
        copy.wait()


def slices(where, hidden, out_weight, members):
    rows, width = hidden.shape
    share, depth = width // members, out_weight.shape[0]
    return pl.pallas_call(
        slices_kernel,
        out_shape=(
            near_out((rows // 2, width)),
            near_out((SPLIT, share)),
            near_out((rows - SPLIT, share)),
            near_out((depth, 2 * share)),
        ),
        in_specs=[smem_spec(), any_spec(), any_spec()],
        out_specs=(vmem_spec(),) * 4,
        scratch_shapes=[pltpu.SemaphoreType.DMA((10,))],
        compiler_params=pltpu.CompilerParams(vmem_limit_bytes=2 * MIB),
        cost_estimate=cost(0, 4 * MIB),
    )(where, far(hidden), far(out_weight))


ROW = 384


def modulate_kernel(where_ref, emb_ref, mod_ref, payload, rows_ref):
    rows_ref[...] = jnp.zeros_like(rows_ref)
    columns = mod_ref.shape[0]
    rows_ref[:, :columns] = lax.dot_general(
        emb_ref[...], mod_ref[...], (((1,), (1,)), ((), ())), preferred_element_type=jnp.float32
    )
    rows = rows_ref[...]
    slots = rows.shape[0]
    even = lax.broadcasted_iota(jnp.int32, rows.shape, 0) % 2 == 0
    following = pltpu.roll(rows, slots - 1, 0)
    partner = jnp.where(even, following, pltpu.roll(rows, 1, 0))
    joined = jnp.where(where_ref[1] == 0, rows, partner) + pltpu.roll(following, columns, 1)
    for slot in range(slots):
        payload[slot] = joined[slot : slot + 1, :]


def modulate(where, emb, mod_weight):
    return pl.pallas_call(
        modulate_kernel,
        out_shape=jax.ShapeDtypeStruct((emb.shape[0], 1, ROW), jnp.float32),
        in_specs=[smem_spec(), vmem_spec(), vmem_spec()],
        out_specs=vmem_spec(),
        scratch_shapes=[pltpu.VMEM((emb.shape[0], ROW), jnp.float32)],
        compiler_params=pltpu.CompilerParams(vmem_limit_bytes=2 * MIB),
        cost_estimate=cost(10**7, MIB),
    )(where, emb, mod_weight.T)


NORM_ROWS = 16


def spread(rows_ref, part, flat):
    slots = rows_ref.shape[0]
    columns = flat.shape[1] // slots
    step = columns - PAIR
    row = lax.broadcasted_iota(jnp.int32, (8, 2 * PAIR), 0)
    at = lax.broadcasted_iota(jnp.int32, (8, 2 * PAIR), 1) - step * row
    held = (at >= 0) & (at < columns)
    first_row = row[:, :PAIR] == 0
    for i in range(slots // 8):
        block = rows_ref[8 * i : 8 * i + 8, :]
        if part:
            block = pltpu.roll(block, ROW - columns * part, 1)
        turned = pltpu.roll(block, 0, 1, stride=step, stride_axis=0)
        turned = jnp.where(held, turned[:, : 2 * PAIR], 0.0)
        carried = turned[:, PAIR:]
        tiles = turned[:, :PAIR] + jnp.where(first_row, 0.0, pltpu.roll(carried, 1, 0))
        base = 8 * i * columns
        for j in range(8):
            flat[:, base + j * PAIR : base + (j + 1) * PAIR] = tiles[j : j + 1, :]
        flat[:, base + 8 * PAIR : base + 9 * PAIR] = carried[7:8, :]


def kv_kernel(
    where_ref, rows_ref, hidden, first, second, own_weight, twin_weight, out_weight, kv_ref, k_ref, v_ref, states_ref, q_weight,
    twin_out,
    flat, weight, x_sems, w_sems,
):
    core, parity = where_ref[1], where_ref[4]
    rows, width = states_ref.shape
    half = rows // 2
    each = q_weight.shape[1]
    from_own = copies_of(hidden, states_ref, x_sems, 4)
    from_pair = copies_of(first, states_ref.at[pl.ds(0, half), :], x_sems, 2) + copies_of(
        second, states_ref.at[pl.ds(half, half), :], x_sems, 2, 2
    )

    def weights_from(source):
        return [
            copies_of(source.at[kind], target, w_sems, 2, 2 * kind)
            for kind, target in (
                (1, weight.at[:, pl.ds(0, each)]),
                (2, weight.at[:, pl.ds(each, each)]),
                (0, q_weight),
            )
        ]

    def start(condition, copies):
        @pl.when(condition)
        def _():
            for copy in copies:
                copy.start()

    start(core == 0, from_own)
    start(core == 1, from_pair)
    start(core == parity, sum(weights_from(own_weight), []))
    start(core != parity, sum(weights_from(twin_weight), []))
    beside = where_ref[2] * 2 + 1 - core
    asides = copies_of(out_weight.at[:, lanes_at(beside, twin_out.shape[1])], twin_out, w_sems, 2, 6)
    for copy in asides:
        copy.start()
    spread(rows_ref, 0, flat)
    scale, shift = 1.0 + flat[:, width : 2 * width], flat[:, :width]

    def normalise(first_row):
        for start in range(first_row, first_row + half, NORM_ROWS):
            block = pl.ds(start, NORM_ROWS)
            states = states_ref[block, :].astype(jnp.float32)
            mean = jnp.mean(states, axis=1, keepdims=True)
            centred = states - mean
            var = jnp.mean(centred * centred, axis=1, keepdims=True)
            states_ref[block, :] = (centred * lax.rsqrt(var + 1e-05) * scale + shift).astype(jnp.bfloat16)

    for copy in from_own:
        copy.wait()
    normalise(0)
    normalise(half)
    keys, values, queries = weights_from(own_weight)
    for copy in keys + values:
        copy.wait()
    kv = jnp.dot(states_ref[...], weight[...], preferred_element_type=jnp.float32).astype(jnp.bfloat16)
    kv_ref[...] = kv
    k_ref[...] = kv[:, :each]
    v_ref[...] = kv[:, each:]
    for copy in queries + asides:
        copy.wait()


def keys_values(where, mod_rows, hidden, first, second, own_weight, twin_weight, out_weight):
    rows, width = hidden.shape
    each = own_weight.shape[2]
    return pl.pallas_call(
        kv_kernel,
        out_shape=(
            near_out((rows, 2 * each)),
            near_out((rows, each)),
            near_out((rows, each)),
            near_out((rows, width)),
            near_out((width, each)),
            near_out((out_weight.shape[0], width // 4)),
        ),
        in_specs=[smem_spec(), vmem_spec()] + [any_spec()] * 6,
        out_specs=(vmem_spec(),) * 6,
        scratch_shapes=[
            pltpu.VMEM((1, 3 * width), jnp.float32),
            pltpu.VMEM((width, 2 * each), jnp.bfloat16),
            pltpu.SemaphoreType.DMA((4,)),
            pltpu.SemaphoreType.DMA((8,)),
        ],
        compiler_params=pltpu.CompilerParams(vmem_limit_bytes=24 * MIB),
        cost_estimate=cost(1, 1),
    )(where, mod_rows, far(hidden), first, second, far(own_weight), twin_weight, far(out_weight))


def query_kernel(normed, weight, query_ref):
    query = jnp.dot(normed[...], weight[...], preferred_element_type=jnp.float32).astype(jnp.bfloat16)
    query_ref[...] = (query * HD ** (-0.5)).astype(jnp.bfloat16)


def queries(normed, weight):
    return pl.pallas_call(
        query_kernel,
        out_shape=near_out((normed.shape[0], weight.shape[1])),
        in_specs=[vmem_spec()] * 2,
        out_specs=vmem_spec(),
        compiler_params=pltpu.CompilerParams(vmem_limit_bytes=4 * MIB),
        cost_estimate=cost(1, 1),
    )(near(normed), near(weight))


def count_at(counts_ref, at):
    inside = (at >= 0) & (at < counts_ref.shape[0])
    return jnp.where(inside, counts_ref[jnp.where(inside, at, 0)], 0)


def bias_of(counts, span):
    lane = lax.broadcasted_iota(jnp.int32, (1, span), 1)
    return jnp.concatenate([jnp.where(lane < c * P_SIZE, 0.0, NEG) for c in counts], axis=1)


def scores_of(query, keys):
    return lax.dot_general(query, keys, (((1,), (1,)), ((), ())), preferred_element_type=jnp.float32)


def local_kernel(where_ref, counts_ref, q_ref, own_ref, k_twin, v_twin, o_ref, m_ref, l_ref):
    span = own_ref.shape[0]
    tile = 256
    core, slot = where_ref[1], where_ref[6]
    partner = slot + 1 - 2 * where_ref[4]
    counts = [
        count_at(counts_ref, jnp.where(core == 0, slot, partner)),
        count_at(counts_ref, jnp.where(core == 0, partner, slot)),
    ]
    bias = bias_of(counts, span)
    low = low_lanes((tile, PAIR))
    for index in range(3):
        lanes = slice(index * PAIR, (index + 1) * PAIR)
        values_at = slice((3 + index) * PAIR, (4 + index) * PAIR)
        keys = jnp.concatenate([own_ref[:, lanes], k_twin[:, lanes]], axis=0)
        values = jnp.concatenate([own_ref[:, values_at], v_twin[:, lanes]], axis=0)
        for start in range(0, span, tile):
            rows = pl.ds(start, tile)
            query = q_ref[rows, lanes]
            zero = jnp.zeros_like(query)
            outs = []
            for masked in (jnp.where(low, query, zero), jnp.where(low, zero, query)):
                scores = scores_of(masked, keys) + bias
                peak = jnp.max(scores, axis=1, keepdims=True)
                probs = jnp.exp(scores - peak)
                total = jnp.sum(probs, axis=1, keepdims=True)
                numer = jnp.dot(probs.astype(jnp.bfloat16), values, preferred_element_type=jnp.float32)
                outs.append((numer, peak, total))
            for ref, a, b in zip((o_ref, m_ref, l_ref), *outs):
                ref[rows, lanes] = jnp.where(low, a, b)


def local_attention(where, counts, query, own, k_twin, v_twin):
    span = query.shape[0]
    part = near_out((span, 3 * PAIR), jnp.float32)
    return pl.pallas_call(
        local_kernel,
        out_shape=(part,) * 3,
        in_specs=[smem_spec()] * 2 + [vmem_spec()] * 4,
        out_specs=(vmem_spec(),) * 3,
        compiler_params=pltpu.CompilerParams(vmem_limit_bytes=16 * MIB),
        cost_estimate=cost(8 * 6 * span * span * 256, 3 * MIB),
    )(where, counts, near(query), near(own), k_twin, v_twin)


def remote_kernel(where_ref, counts_ref, q_ref, kv_ref, o_ref, m_ref, l_ref, piece_ref):
    span = kv_ref.shape[0]
    tile = 256
    core, slot = where_ref[1], where_ref[6]
    step = 1 - 2 * where_ref[4]
    bias = bias_of([count_at(counts_ref, jnp.where(core == 0, slot - step, slot + 2 * step))], span)
    low = low_lanes((tile, PAIR))
    for index in range(3):
        lanes = slice(index * PAIR, (index + 1) * PAIR)
        keys, values = kv_ref[:, lanes], kv_ref[:, (3 + index) * PAIR : (4 + index) * PAIR]
        for start in range(0, span, tile):
            rows = pl.ds(start, tile)
            query = q_ref[rows, lanes]
            zero = jnp.zeros_like(query)
            outs = []
            for head, masked in enumerate((jnp.where(low, query, zero), jnp.where(low, zero, query))):
                at = index * PAIR + head * HD
                before = m_ref[rows, at : at + 1]
                scores = scores_of(masked, keys) + bias
                peak = jnp.maximum(jnp.max(scores, axis=1, keepdims=True), before)
                probs = jnp.exp(scores - peak)
                fade = jnp.exp(before - peak)
                total = jnp.sum(probs, axis=1, keepdims=True) + fade * l_ref[rows, at : at + 1]
                numer = jnp.dot(probs.astype(jnp.bfloat16), values, preferred_element_type=jnp.float32)
                outs.append((numer + fade * o_ref[rows, lanes]) / total)
            piece_ref[rows, lanes] = jnp.where(low, *outs).astype(jnp.bfloat16)


def remote_attention(where, counts, query, kv, o, m, l):
    span = query.shape[0]
    return pl.pallas_call(
        remote_kernel,
        out_shape=near_out((span, 3 * PAIR)),
        in_specs=[smem_spec()] * 2 + [vmem_spec()] * 5,
        out_specs=vmem_spec(),
        compiler_params=pltpu.CompilerParams(vmem_limit_bytes=16 * MIB),
        cost_estimate=cost(4 * 6 * span * span * 256, 3 * MIB),
    )(where, counts, near(query), kv, near(o), near(m), near(l))


def tail_kernel(
    where_ref, rows_ref, out_weight, w_twin, w_far, w_far_twin, gathered, gate, flat, sems,
):
    member, core, parity = where_ref[0], where_ref[1], where_ref[4]
    share = gathered.shape[1]
    width = flat.shape[1] // 3
    block = out_weight.shape[0]
    local = jnp.where(core == 0, 1 - parity, parity)
    whole, mine, own = pl.ds(0, share), lanes_at(core, share), lanes_at(member, share)
    copies = []
    for source, lanes, far_half, y_lo in (
        (out_weight, own, 0, core),
        (w_twin, whole, 0, 1 - core),
        (w_far, mine, 1, core),
        (w_far_twin, mine, 1, 1 - core),
    ):
        base = jnp.where(local == y_lo, 0, 2 * block) + far_half * block
        to = pl.ds(pl.multiple_of(base, block), block)
        copies += copies_of(source.at[:, lanes], gathered.at[to, :], sems, 2, len(copies))
    for copy in copies:
        copy.start()
    spread(rows_ref, 1, flat)
    gate[...] = flat[:, pl.ds(pl.multiple_of(2 * width + member * share, PAIR), share)]
    for copy in copies:
        copy.wait()


def tail_inputs(where, mod_rows, out_weight, w_twin, w_far, w_far_twin):
    block, share = w_twin.shape
    width = out_weight.shape[1]
    return pl.pallas_call(
        tail_kernel,
        out_shape=(near_out((4 * block, share)), near_out((1, share), jnp.float32)),
        in_specs=[smem_spec(), vmem_spec()] + [any_spec()] * 4,
        out_specs=(vmem_spec(),) * 2,
        scratch_shapes=[pltpu.VMEM((1, 3 * width), jnp.float32), pltpu.SemaphoreType.DMA((8,))],
        compiler_params=pltpu.CompilerParams(vmem_limit_bytes=2 * MIB),
        cost_estimate=cost(0, 5 * MIB),
    )(where, mod_rows, far(out_weight), w_twin, w_far, w_far_twin)


def first_out_kernel(where_ref, same, cross, held, weight, partial):
    here = (where_ref[4] == 0) & (where_ref[1] == 1)
    attn = jnp.concatenate([jnp.where(here, held[...], same[...]), cross[...]], axis=1)
    partial[...] = jnp.dot(attn, weight[: attn.shape[1], :], preferred_element_type=jnp.float32)


def first_out(where, same, cross, held, weight):
    span, share = same.shape[0], weight.shape[1]
    return pl.pallas_call(
        first_out_kernel,
        out_shape=near_out((span, share), jnp.float32),
        in_specs=[smem_spec()] + [vmem_spec()] * 4,
        out_specs=vmem_spec(),
        compiler_params=pltpu.CompilerParams(vmem_limit_bytes=8 * MIB),
        cost_estimate=cost(512 * 768 * 768 * 2, 3 * MIB),
    )(where, same, cross, near(held), near(weight))


TILE = 128


def last_out_kernel(
    where_ref, same, cross, held, weight, partial, residual_a, residual_b, gate, fresh, out, ready, sems
):
    here = (where_ref[4] == 0) & (where_ref[1] == 0)
    last = where_ref[5] == 1
    span = partial.shape[0]
    tiles = span // TILE

    @pl.when(last)
    def _():
        for source, target in ((fresh, ready), (ready, out)):
            copies = copies_of(source, target, sems, tiles)
            for copy in copies:
                copy.start()
            for copy in copies:
                copy.wait()

    @pl.when(jnp.logical_not(last))
    def _():
        copies = []
        for index, first_row in enumerate(range(0, span, TILE)):
            rows = slice(first_row, first_row + TILE)
            attn = jnp.concatenate([jnp.where(here, held[rows, :], same[rows, :]), cross[rows, :]], axis=1)
            summed = partial[rows, :] + jnp.dot(
                attn, weight[attn.shape[1] :, :], preferred_element_type=jnp.float32
            )
            if first_row + TILE <= SPLIT:
                states = residual_a[rows, :]
            elif first_row >= SPLIT:
                states = residual_b[first_row - SPLIT : first_row - SPLIT + TILE, :]
            else:
                states = jnp.concatenate(
                    [residual_a[first_row:SPLIT, :], residual_b[: first_row + TILE - SPLIT, :]], axis=0
                )
            ready[rows, :] = (states.astype(jnp.float32) + gate[...] * summed).astype(jnp.bfloat16)
            block = pl.ds(first_row, TILE)
            copies.append(pltpu.make_async_copy(ready.at[block, :], out.at[block, :], sems.at[index]))
            copies[-1].start()
        for copy in copies:
            copy.wait()


def last_out(where, same, cross, held, weight, partial, residual_a, residual_b, gate, fresh):
    span, share = partial.shape
    return pl.pallas_call(
        last_out_kernel,
        out_shape=jax.ShapeDtypeStruct((span, share), jnp.bfloat16),
        in_specs=[smem_spec()] + [vmem_spec()] * 8 + [any_spec()],
        out_specs=any_spec(),
        scratch_shapes=[pltpu.VMEM((span, share), jnp.bfloat16), pltpu.SemaphoreType.DMA((4,))],
        compiler_params=pltpu.CompilerParams(vmem_limit_bytes=8 * MIB),
        cost_estimate=cost(512 * 768 * 768 * 2, 5 * MIB),
    )(where, same, cross, held, near(weight), near(partial), residual_a, residual_b, near(gate), far(fresh))


def on_device(hidden, levels, frame_counts, mod_weight, qkv_weight, out_weight, fresh):
    rows, width = hidden.shape
    slot = lax.axis_index("queue")
    queue_len = lax.axis_size("queue")
    member = lax.axis_index("heads")
    members = lax.axis_size("heads")
    share = width // members
    parity, core, y_hi = slot % 2, member % 2, member // 2
    z_half = (slot // 8) % 2
    half = rows // 2
    route = functools.partial(routed, queue_len=queue_len, members=members)
    twin = lambda a: route(a, target=lambda s, y, k: (s, y, 1 - k))

    where = jnp.stack(
        [member, core, y_hi, z_half, parity, (slot == queue_len - 1).astype(jnp.int32), slot]
    ).astype(jnp.int32)
    after = lambda a, *b: lax.optimization_barrier((a, *b))[0]
    frame_counts = frame_counts.astype(jnp.int32)

    twin_weight = twin(qkv_weight)
    mine, share_a, share_b, far_mine = slices(where, hidden, out_weight, members)
    second = route(mine, target=lambda s, y, k: (s ^ 1, y ^ k, k))

    payload = modulate(where, embed_levels(levels, mod_weight.shape[0]), mod_weight)
    mod_rows = lax.all_to_all(payload, "queue", 0, 0, tiled=True)[:, 0, :]

    first = twin(after(second, mod_rows))
    w_far = route(after(far_mine, mod_rows), target=lambda s, y, k: (s ^ 1, 1 - y, k))
    residual_a = route(after(share_a, mod_rows), target=lambda s, y, k: (s - 1, y, k))
    kv, k, v, normed, q_weight, twin_mine = keys_values(where, mod_rows, hidden, first, second, qkv_weight, twin_weight, out_weight)

    def remote_target(s, y, k):
        back = (s % 2 == 0) == (k == 0)
        return (s - 2 if back else s + 2, y, 1 - k)

    kv_remote = route(kv, target=remote_target)
    k_twin, v_twin = twin(k), twin(v)
    query = queries(after(normed, kv), q_weight)
    w_twin = twin(twin_mine)
    o, m, l = local_attention(after(where, residual_a), frame_counts, query, kv, k_twin, v_twin)
    w_far_twin = twin(after(w_far, o))
    residual_b = route(after(share_b, o), target=lambda s, y, k: (s - 1, y, k))
    attn = remote_attention(where, frame_counts, query, kv_remote, o, m, l)

    def goal(s, y, k):
        if k == 0:
            return (s - 1, y, 0)
        return (s if s % 2 == 0 else s - 2, y, 1)

    attn = after(attn, residual_b)
    same = route(attn, target=lambda s, y, k: None if s % 2 == 0 and k == 1 else goal(s, y, k))
    cross = route(attn, target=lambda s, y, k: goal(s, 1 - y, k))
    twin_attn = twin(attn)
    weight, gate = tail_inputs(where, mod_rows, out_weight, w_twin, w_far, w_far_twin)
    same, cross, _ = lax.optimization_barrier((same, cross, weight))
    partial = first_out(where, same, cross, attn, weight)
    return last_out(where, twin(same), twin(cross), twin_attn, weight, partial, residual_a, residual_b, gate, fresh)


def solution(mesh):
    placed = (
        P("queue", None),
        P(),
        P(),
        P(None, "queue"),
        P(None, None, "heads"),
        P("heads", None),
        P(None, "heads"),
    )
    return jax.shard_map(
        on_device, mesh=mesh, in_specs=placed, out_specs=P("queue", "heads"), check_vma=False
    )
```

```python
import functools
import math

import jax
import jax.numpy as jnp
from jax import lax
from jax.experimental import pallas as pl
from jax.experimental.pallas import tpu as pltpu
from jax.sharding import PartitionSpec as P

HD = 64
P_SIZE = 256
PAIR = 2 * HD
NEG = -1e30
BOTH = ("queue", "heads")
MIB = 1024 * 1024


def embed_levels(levels, width):
    halfway = width // 2
    freqs = jnp.exp(-math.log(10000.0) * jnp.arange(halfway, dtype=jnp.float32) / halfway)
    angles = levels.astype(jnp.float32)[:, None] * freqs[None, :]
    return jax.nn.silu(jnp.concatenate([jnp.cos(angles), jnp.sin(angles)], axis=1)).astype(
        jnp.bfloat16
    )


def routed(array, queue_len, members, target):
    pairs = []
    for slot in range(queue_len):
        for member in range(members):
            goal = target(slot, member // 2, member % 2)
            if goal is not None and 0 <= goal[0] < queue_len:
                pairs.append((slot * members + member, goal[0] * members + goal[1] * 2 + goal[2]))
    return lax.ppermute(array, BOTH, pairs)


def low_lanes(shape):
    return lax.broadcasted_iota(jnp.int32, shape, len(shape) - 1) < HD


def copies_of(source, target, sems, chunks, first=0):
    step = source.shape[0] // chunks
    return [
        pltpu.make_async_copy(
            source.at[pl.ds(i * step, step), :], target.at[pl.ds(i * step, step), :], sems.at[first + i]
        )
        for i in range(chunks)
    ]


def any_spec():
    return pl.BlockSpec(memory_space=pl.ANY)


def far(array):
    return pltpu.with_memory_space_constraint(array, pltpu.HBM)


def near(array):
    return pltpu.with_memory_space_constraint(array, pltpu.VMEM)


def near_out(shape, dtype=jnp.bfloat16):
    return pltpu.VMEM(shape, dtype)


def cost(flops, moved, transcendentals=0):
    return pl.CostEstimate(flops=flops, bytes_accessed=moved, transcendentals=transcendentals)


def vmem_spec():
    return pl.BlockSpec(memory_space=pltpu.VMEM)


def smem_spec():
    return pl.BlockSpec(memory_space=pltpu.SMEM)


def lanes_at(index, size):
    return pl.ds(pl.multiple_of(index * size, size), size)


def slices_kernel(where_ref, hidden, out_weight, mine, far_same, far_cross, sems):
    core, y_hi = where_ref[1], where_ref[2]
    half, width = mine.shape[0], far_same.shape[1]
    away = (1 - y_hi) * 2
    copies = (
        copies_of(hidden.at[lanes_at(core, half), :], mine, sems, 4)
        + copies_of(out_weight.at[:, lanes_at(away + core, width)], far_same, sems, 2, 4)
        + copies_of(out_weight.at[:, lanes_at(away + 1 - core, width)], far_cross, sems, 2, 6)
    )
    for copy in copies:
        copy.start()
    for copy in copies:
        copy.wait()


def slices(where, hidden, out_weight, members):
    rows, width = hidden.shape
    share, depth = width // members, out_weight.shape[0]
    return pl.pallas_call(
        slices_kernel,
        out_shape=(
            near_out((rows // 2, width)),
            near_out((depth, share)),
            near_out((depth, share)),
        ),
        in_specs=[smem_spec(), any_spec(), any_spec()],
        out_specs=(vmem_spec(),) * 3,
        scratch_shapes=[pltpu.SemaphoreType.DMA((8,))],
        compiler_params=pltpu.CompilerParams(vmem_limit_bytes=2 * MIB),
        cost_estimate=cost(0, 4 * MIB),
    )(where, far(hidden), far(out_weight))


ROW = 384


def modulate_kernel(where_ref, emb_ref, mod_ref, payload, rows_ref):
    rows_ref[...] = jnp.zeros_like(rows_ref)
    columns = mod_ref.shape[0]
    rows_ref[:, :columns] = lax.dot_general(
        emb_ref[...], mod_ref[...], (((1,), (1,)), ((), ())), preferred_element_type=jnp.float32
    )
    rows = rows_ref[...]
    slots = rows.shape[0]
    even = lax.broadcasted_iota(jnp.int32, rows.shape, 0) % 2 == 0
    following = pltpu.roll(rows, slots - 1, 0)
    partner = jnp.where(even, following, pltpu.roll(rows, 1, 0))
    joined = jnp.where(where_ref[1] == 0, rows, partner) + pltpu.roll(following, columns, 1)
    for slot in range(slots):
        payload[slot] = joined[slot : slot + 1, :]


def modulate(where, emb, mod_weight):
    return pl.pallas_call(
        modulate_kernel,
        out_shape=jax.ShapeDtypeStruct((emb.shape[0], 1, ROW), jnp.float32),
        in_specs=[smem_spec(), vmem_spec(), vmem_spec()],
        out_specs=vmem_spec(),
        scratch_shapes=[pltpu.VMEM((emb.shape[0], ROW), jnp.float32)],
        compiler_params=pltpu.CompilerParams(vmem_limit_bytes=2 * MIB),
        cost_estimate=cost(10**7, MIB),
    )(where, emb, mod_weight.T)


NORM_ROWS = 16


def spread(rows_ref, part, flat):
    slots = rows_ref.shape[0]
    columns = flat.shape[1] // slots
    step = columns - PAIR
    row = lax.broadcasted_iota(jnp.int32, (8, 2 * PAIR), 0)
    at = lax.broadcasted_iota(jnp.int32, (8, 2 * PAIR), 1) - step * row
    held = (at >= 0) & (at < columns)
    first_row = row[:, :PAIR] == 0
    for i in range(slots // 8):
        block = rows_ref[8 * i : 8 * i + 8, :]
        if part:
            block = pltpu.roll(block, ROW - columns * part, 1)
        turned = pltpu.roll(block, 0, 1, stride=step, stride_axis=0)
        turned = jnp.where(held, turned[:, : 2 * PAIR], 0.0)
        carried = turned[:, PAIR:]
        tiles = turned[:, :PAIR] + jnp.where(first_row, 0.0, pltpu.roll(carried, 1, 0))
        base = 8 * i * columns
        for j in range(8):
            flat[:, base + j * PAIR : base + (j + 1) * PAIR] = tiles[j : j + 1, :]
        flat[:, base + 8 * PAIR : base + 9 * PAIR] = carried[7:8, :]


def kv_kernel(
    where_ref, rows_ref, hidden, first, second, own_weight, twin_weight, out_weight, kv_ref, k_ref, v_ref, states_ref, q_weight,
    twin_out, share_ref,
    flat, weight, x_sems, w_sems,
):
    core, parity = where_ref[1], where_ref[4]
    rows, width = states_ref.shape
    half = rows // 2
    each = q_weight.shape[1]
    from_own = copies_of(hidden, states_ref, x_sems, 4)
    from_pair = copies_of(first, states_ref.at[pl.ds(0, half), :], x_sems, 2) + copies_of(
        second, states_ref.at[pl.ds(half, half), :], x_sems, 2, 2
    )

    def weights_from(source):
        return [
            copies_of(source.at[kind], target, w_sems, 2, 2 * kind)
            for kind, target in (
                (1, weight.at[:, pl.ds(0, each)]),
                (2, weight.at[:, pl.ds(each, each)]),
                (0, q_weight),
            )
        ]

    def start(condition, copies):
        @pl.when(condition)
        def _():
            for copy in copies:
                copy.start()

    start(core == 0, from_own)
    start(core == 1, from_pair)
    start(core == parity, sum(weights_from(own_weight), []))
    start(core != parity, sum(weights_from(twin_weight), []))
    beside = where_ref[2] * 2 + 1 - core
    asides = copies_of(out_weight.at[:, lanes_at(beside, twin_out.shape[1])], twin_out, w_sems, 2, 6)
    for copy in asides:
        copy.start()
    spread(rows_ref, 0, flat)
    scale, shift = 1.0 + flat[:, width : 2 * width], flat[:, :width]

    def normalise(first_row):
        for start in range(first_row, first_row + half, NORM_ROWS):
            block = pl.ds(start, NORM_ROWS)
            states = states_ref[block, :].astype(jnp.float32)
            mean = jnp.mean(states, axis=1, keepdims=True)
            centred = states - mean
            var = jnp.mean(centred * centred, axis=1, keepdims=True)
            states_ref[block, :] = (centred * lax.rsqrt(var + 1e-05) * scale + shift).astype(jnp.bfloat16)

    for copy in from_own:
        copy.wait()
    share_ref[...] = states_ref[:, lanes_at(where_ref[0], share_ref.shape[1])]
    normalise(0)
    normalise(half)
    keys, values, queries = weights_from(own_weight)
    for copy in keys + values:
        copy.wait()
    kv = jnp.dot(states_ref[...], weight[...], preferred_element_type=jnp.float32).astype(jnp.bfloat16)
    kv_ref[...] = kv
    k_ref[...] = kv[:, :each]
    v_ref[...] = kv[:, each:]
    for copy in queries + asides:
        copy.wait()


def keys_values(where, mod_rows, hidden, first, second, own_weight, twin_weight, out_weight):
    rows, width = hidden.shape
    each = own_weight.shape[2]
    return pl.pallas_call(
        kv_kernel,
        out_shape=(
            near_out((rows, 2 * each)),
            near_out((rows, each)),
            near_out((rows, each)),
            near_out((rows, width)),
            near_out((width, each)),
            near_out((out_weight.shape[0], width // 4)),
            near_out((rows, width // 4)),
        ),
        in_specs=[smem_spec(), vmem_spec()] + [any_spec()] * 6,
        out_specs=(vmem_spec(),) * 7,
        scratch_shapes=[
            pltpu.VMEM((1, 3 * width), jnp.float32),
            pltpu.VMEM((width, 2 * each), jnp.bfloat16),
            pltpu.SemaphoreType.DMA((4,)),
            pltpu.SemaphoreType.DMA((8,)),
        ],
        compiler_params=pltpu.CompilerParams(vmem_limit_bytes=24 * MIB),
        cost_estimate=cost(1, 1),
    )(where, mod_rows, far(hidden), first, second, far(own_weight), twin_weight, far(out_weight))


def query_kernel(normed, weight, query_ref):
    query = jnp.dot(normed[...], weight[...], preferred_element_type=jnp.float32).astype(jnp.bfloat16)
    query_ref[...] = (query * HD ** (-0.5)).astype(jnp.bfloat16)


def queries(normed, weight):
    return pl.pallas_call(
        query_kernel,
        out_shape=near_out((normed.shape[0], weight.shape[1])),
        in_specs=[vmem_spec()] * 2,
        out_specs=vmem_spec(),
        compiler_params=pltpu.CompilerParams(vmem_limit_bytes=4 * MIB),
        cost_estimate=cost(1, 1),
    )(near(normed), near(weight))


def count_at(counts_ref, at):
    inside = (at >= 0) & (at < counts_ref.shape[0])
    return jnp.where(inside, counts_ref[jnp.where(inside, at, 0)], 0)


def bias_of(counts, span):
    lane = lax.broadcasted_iota(jnp.int32, (1, span), 1)
    return jnp.concatenate([jnp.where(lane < c * P_SIZE, 0.0, NEG) for c in counts], axis=1)


def scores_of(query, keys):
    return lax.dot_general(query, keys, (((1,), (1,)), ((), ())), preferred_element_type=jnp.float32)


def local_kernel(where_ref, counts_ref, q_ref, own_ref, k_twin, v_twin, o_ref, m_ref, l_ref):
    span = own_ref.shape[0]
    tile = 256
    core, slot = where_ref[1], where_ref[6]
    partner = slot + 1 - 2 * where_ref[4]
    counts = [
        count_at(counts_ref, jnp.where(core == 0, slot, partner)),
        count_at(counts_ref, jnp.where(core == 0, partner, slot)),
    ]
    bias = bias_of(counts, span)
    low = low_lanes((tile, PAIR))
    for index in range(3):
        lanes = slice(index * PAIR, (index + 1) * PAIR)
        values_at = slice((3 + index) * PAIR, (4 + index) * PAIR)
        keys = jnp.concatenate([own_ref[:, lanes], k_twin[:, lanes]], axis=0)
        values = jnp.concatenate([own_ref[:, values_at], v_twin[:, lanes]], axis=0)
        for start in range(0, span, tile):
            rows = pl.ds(start, tile)
            query = q_ref[rows, lanes]
            zero = jnp.zeros_like(query)
            outs = []
            for masked in (jnp.where(low, query, zero), jnp.where(low, zero, query)):
                scores = scores_of(masked, keys) + bias
                peak = jnp.max(scores, axis=1, keepdims=True)
                probs = jnp.exp(scores - peak)
                total = jnp.sum(probs, axis=1, keepdims=True)
                numer = jnp.dot(probs.astype(jnp.bfloat16), values, preferred_element_type=jnp.float32)
                outs.append((numer, peak, total))
            for ref, a, b in zip((o_ref, m_ref, l_ref), *outs):
                ref[rows, lanes] = jnp.where(low, a, b)


def local_attention(where, counts, query, own, k_twin, v_twin):
    span = query.shape[0]
    part = near_out((span, 3 * PAIR), jnp.float32)
    return pl.pallas_call(
        local_kernel,
        out_shape=(part,) * 3,
        in_specs=[smem_spec()] * 2 + [vmem_spec()] * 4,
        out_specs=(vmem_spec(),) * 3,
        compiler_params=pltpu.CompilerParams(vmem_limit_bytes=16 * MIB),
        cost_estimate=cost(8 * 6 * span * span * 256, 3 * MIB),
    )(where, counts, near(query), near(own), k_twin, v_twin)


def remote_kernel(where_ref, counts_ref, q_ref, kv_ref, o_ref, m_ref, l_ref, piece_ref):
    span = kv_ref.shape[0]
    tile = 256
    core, slot = where_ref[1], where_ref[6]
    step = 1 - 2 * where_ref[4]
    bias = bias_of([count_at(counts_ref, jnp.where(core == 0, slot - step, slot + 2 * step))], span)
    low = low_lanes((tile, PAIR))
    for index in range(3):
        lanes = slice(index * PAIR, (index + 1) * PAIR)
        keys, values = kv_ref[:, lanes], kv_ref[:, (3 + index) * PAIR : (4 + index) * PAIR]
        for start in range(0, span, tile):
            rows = pl.ds(start, tile)
            query = q_ref[rows, lanes]
            zero = jnp.zeros_like(query)
            outs = []
            for head, masked in enumerate((jnp.where(low, query, zero), jnp.where(low, zero, query))):
                at = index * PAIR + head * HD
                before = m_ref[rows, at : at + 1]
                scores = scores_of(masked, keys) + bias
                peak = jnp.maximum(jnp.max(scores, axis=1, keepdims=True), before)
                probs = jnp.exp(scores - peak)
                fade = jnp.exp(before - peak)
                total = jnp.sum(probs, axis=1, keepdims=True) + fade * l_ref[rows, at : at + 1]
                numer = jnp.dot(probs.astype(jnp.bfloat16), values, preferred_element_type=jnp.float32)
                outs.append((numer + fade * o_ref[rows, lanes]) / total)
            piece_ref[rows, lanes] = jnp.where(low, *outs).astype(jnp.bfloat16)


def remote_attention(where, counts, query, kv, o, m, l):
    span = query.shape[0]
    return pl.pallas_call(
        remote_kernel,
        out_shape=near_out((span, 3 * PAIR)),
        in_specs=[smem_spec()] * 2 + [vmem_spec()] * 5,
        out_specs=vmem_spec(),
        compiler_params=pltpu.CompilerParams(vmem_limit_bytes=16 * MIB),
        cost_estimate=cost(1, 1),
    )(where, counts, near(query), kv, near(o), near(m), near(l))


def tail_kernel(
    where_ref, rows_ref, out_weight, w_twin, w_far, w_far_twin, gathered, gate, flat, sems,
):
    member, core, parity = where_ref[0], where_ref[1], where_ref[4]
    share = gathered.shape[1]
    width = flat.shape[1] // 3
    block = out_weight.shape[0]
    local = jnp.where(core == 0, 1 - parity, parity)
    whole, own = pl.ds(0, share), lanes_at(member, share)
    copies = []
    for source, lanes, far_half, y_lo in (
        (out_weight, own, 0, core),
        (w_twin, whole, 0, 1 - core),
        (w_far, whole, 1, core),
        (w_far_twin, whole, 1, 1 - core),
    ):
        base = jnp.where(local == y_lo, 0, 2 * block) + far_half * block
        to = pl.ds(pl.multiple_of(base, block), block)
        copies += copies_of(source.at[:, lanes], gathered.at[to, :], sems, 2, len(copies))
    for copy in copies:
        copy.start()
    spread(rows_ref, 1, flat)
    gate[...] = flat[:, pl.ds(pl.multiple_of(2 * width + member * share, PAIR), share)]
    for copy in copies:
        copy.wait()


def tail_inputs(where, mod_rows, out_weight, w_twin, w_far, w_far_twin):
    block, share = w_twin.shape
    width = out_weight.shape[1]
    return pl.pallas_call(
        tail_kernel,
        out_shape=(near_out((4 * block, share)), near_out((1, share), jnp.float32)),
        in_specs=[smem_spec(), vmem_spec()] + [any_spec()] * 4,
        out_specs=(vmem_spec(),) * 2,
        scratch_shapes=[pltpu.VMEM((1, 3 * width), jnp.float32), pltpu.SemaphoreType.DMA((8,))],
        compiler_params=pltpu.CompilerParams(vmem_limit_bytes=2 * MIB),
        cost_estimate=cost(1, 1),
    )(where, mod_rows, far(out_weight), w_twin, w_far, w_far_twin)


def first_out_kernel(where_ref, same, cross, held, weight, partial):
    here = (where_ref[4] == 0) & (where_ref[1] == 1)
    attn = jnp.concatenate([jnp.where(here, held[...], same[...]), cross[...]], axis=1)
    partial[...] = jnp.dot(attn, weight[: attn.shape[1], :], preferred_element_type=jnp.float32)


def first_out(where, same, cross, held, weight):
    span, share = same.shape[0], weight.shape[1]
    return pl.pallas_call(
        first_out_kernel,
        out_shape=near_out((span, share), jnp.float32),
        in_specs=[smem_spec()] + [vmem_spec()] * 4,
        out_specs=vmem_spec(),
        compiler_params=pltpu.CompilerParams(vmem_limit_bytes=8 * MIB),
        cost_estimate=cost(1, 1),
    )(where, same, cross, near(held), near(weight))


TILE = 128


def last_out_kernel(
    where_ref, same, cross, held, weight, partial, kept, residual, gate, fresh, out, ready, sems
):
    here = (where_ref[4] == 0) & (where_ref[1] == 0)
    holds = (where_ref[4] == 0) & (where_ref[1] == 1)
    last = where_ref[5] == 1
    span = partial.shape[0]
    tiles = span // TILE

    @pl.when(last)
    def _():
        for source, target in ((fresh, ready), (ready, out)):
            copies = copies_of(source, target, sems, tiles)
            for copy in copies:
                copy.start()
            for copy in copies:
                copy.wait()

    @pl.when(jnp.logical_not(last))
    def _():
        copies = []
        for index, first_row in enumerate(range(0, span, TILE)):
            rows = slice(first_row, first_row + TILE)
            attn = jnp.concatenate([jnp.where(here, held[rows, :], same[rows, :]), cross[rows, :]], axis=1)
            summed = partial[rows, :] + jnp.dot(
                attn, weight[attn.shape[1] :, :], preferred_element_type=jnp.float32
            )
            states = jnp.where(holds, kept[rows, :], residual[rows, :])
            ready[rows, :] = (states.astype(jnp.float32) + gate[...] * summed).astype(jnp.bfloat16)
            block = pl.ds(first_row, TILE)
            copies.append(pltpu.make_async_copy(ready.at[block, :], out.at[block, :], sems.at[index]))
            copies[-1].start()
        for copy in copies:
            copy.wait()


def last_out(where, same, cross, held, weight, partial, kept, residual, gate, fresh):
    span, share = partial.shape
    return pl.pallas_call(
        last_out_kernel,
        out_shape=jax.ShapeDtypeStruct((span, share), jnp.bfloat16),
        in_specs=[smem_spec()] + [vmem_spec()] * 8 + [any_spec()],
        out_specs=any_spec(),
        scratch_shapes=[pltpu.VMEM((span, share), jnp.bfloat16), pltpu.SemaphoreType.DMA((4,))],
        compiler_params=pltpu.CompilerParams(vmem_limit_bytes=8 * MIB),
        cost_estimate=cost(1, 1),
    )(where, same, cross, held, near(weight), near(partial), near(kept), residual, near(gate), far(fresh))


def on_device(hidden, levels, frame_counts, mod_weight, qkv_weight, out_weight, fresh):
    rows, width = hidden.shape
    slot = lax.axis_index("queue")
    queue_len = lax.axis_size("queue")
    member = lax.axis_index("heads")
    members = lax.axis_size("heads")
    share = width // members
    parity, core, y_hi = slot % 2, member % 2, member // 2
    z_half = (slot // 8) % 2
    half = rows // 2
    route = functools.partial(routed, queue_len=queue_len, members=members)
    twin = lambda a: route(a, target=lambda s, y, k: (s, y, 1 - k))

    where = jnp.stack(
        [member, core, y_hi, z_half, parity, (slot == queue_len - 1).astype(jnp.int32), slot]
    ).astype(jnp.int32)
    after = lambda a, *b: lax.optimization_barrier((a, *b))[0]
    frame_counts = frame_counts.astype(jnp.int32)

    twin_weight = twin(qkv_weight)
    mine, far_same, far_cross = slices(where, hidden, out_weight, members)
    second = route(mine, target=lambda s, y, k: (s ^ 1, y ^ k, k))

    payload = modulate(where, embed_levels(levels, mod_weight.shape[0]), mod_weight)
    mod_rows = lax.all_to_all(payload, "queue", 0, 0, tiled=True)[:, 0, :]

    first = twin(after(second, mod_rows))
    w_far = route(after(far_same, mod_rows), target=lambda s, y, k: (s ^ 1, 1 - y, k))
    w_far_twin = route(after(far_cross, mod_rows), target=lambda s, y, k: (s ^ 1, 1 - y, 1 - k))
    kv, k, v, normed, q_weight, twin_mine, share_states = keys_values(where, mod_rows, hidden, first, second, qkv_weight, twin_weight, out_weight)

    def remote_target(s, y, k):
        back = (s % 2 == 0) == (k == 0)
        return (s - 2 if back else s + 2, y, 1 - k)

    kv_remote = route(kv, target=remote_target)
    k_twin, v_twin = twin(k), twin(v)
    query = queries(after(normed, kv), q_weight)
    w_twin = twin(twin_mine)
    o, m, l = local_attention(after(where, w_far_twin), frame_counts, query, kv, k_twin, v_twin)
    residual = route(
        after(share_states, o),
        target=lambda s, y, k: (s - 1, y, 0) if k == 0 else ((s - 2, y, 1) if s % 2 else None),
    )
    attn = remote_attention(after(where, w_far), frame_counts, query, kv_remote, o, m, l)

    def goal(s, y, k):
        if k == 0:
            return (s - 1, y, 0)
        return (s if s % 2 == 0 else s - 2, y, 1)

    same = route(attn, target=lambda s, y, k: None if s % 2 == 0 and k == 1 else goal(s, y, k))
    cross = route(attn, target=lambda s, y, k: goal(s, 1 - y, k))
    twin_attn = twin(attn)
    weight, gate = tail_inputs(where, mod_rows, out_weight, w_twin, w_far, w_far_twin)
    same, cross, residual, _ = lax.optimization_barrier((same, cross, residual, weight))
    partial = first_out(where, same, cross, attn, weight)
    return last_out(where, twin(same), twin(cross), twin_attn, weight, partial, share_states, residual, gate, fresh)


def solution(mesh):
    placed = (
        P("queue", None),
        P(),
        P(),
        P(None, "queue"),
        P(None, None, "heads"),
        P("heads", None),
        P(None, "heads"),
    )
    return jax.shard_map(
        on_device, mesh=mesh, in_specs=placed, out_specs=P("queue", "heads"), check_vma=False
    )
```

```python
import functools
import math

import jax
import jax.numpy as jnp
from jax import lax
from jax.experimental import pallas as pl
from jax.experimental.pallas import tpu as pltpu
from jax.sharding import PartitionSpec as P

HD = 64
P_SIZE = 256
PAIR = 2 * HD
NEG = -1e30
BOTH = ("queue", "heads")
MIB = 1024 * 1024


def embed_levels(levels, width):
    halfway = width // 2
    freqs = jnp.exp(-math.log(10000.0) * jnp.arange(halfway, dtype=jnp.float32) / halfway)
    angles = levels.astype(jnp.float32)[:, None] * freqs[None, :]
    return jax.nn.silu(jnp.concatenate([jnp.cos(angles), jnp.sin(angles)], axis=1)).astype(
        jnp.bfloat16
    )


def routed(array, queue_len, members, target):
    pairs = []
    for slot in range(queue_len):
        for member in range(members):
            goal = target(slot, member // 2, member % 2)
            if goal is not None and 0 <= goal[0] < queue_len:
                pairs.append((slot * members + member, goal[0] * members + goal[1] * 2 + goal[2]))
    return lax.ppermute(array, BOTH, pairs)


def low_lanes(shape):
    return lax.broadcasted_iota(jnp.int32, shape, len(shape) - 1) < HD


def copies_of(source, target, sems, chunks, first=0):
    step = source.shape[0] // chunks
    return [
        pltpu.make_async_copy(
            source.at[pl.ds(i * step, step), :], target.at[pl.ds(i * step, step), :], sems.at[first + i]
        )
        for i in range(chunks)
    ]


def any_spec():
    return pl.BlockSpec(memory_space=pl.ANY)


def far(array):
    return pltpu.with_memory_space_constraint(array, pltpu.HBM)


def near(array):
    return pltpu.with_memory_space_constraint(array, pltpu.VMEM)


def near_out(shape, dtype=jnp.bfloat16):
    return pltpu.VMEM(shape, dtype)


def cost(flops, moved, transcendentals=0):
    return pl.CostEstimate(flops=flops, bytes_accessed=moved, transcendentals=transcendentals)


def vmem_spec():
    return pl.BlockSpec(memory_space=pltpu.VMEM)


def smem_spec():
    return pl.BlockSpec(memory_space=pltpu.SMEM)


def lanes_at(index, size):
    return pl.ds(pl.multiple_of(index * size, size), size)


def slices_kernel(where_ref, hidden, out_weight, mine, far_same, far_cross, sems):
    core, y_hi = where_ref[1], where_ref[2]
    half, width = mine.shape[0], far_same.shape[1]
    away = (1 - y_hi) * 2
    copies = (
        copies_of(hidden.at[lanes_at(core, half), :], mine, sems, 4)
        + copies_of(out_weight.at[:, lanes_at(away + core, width)], far_same, sems, 2, 4)
        + copies_of(out_weight.at[:, lanes_at(away + 1 - core, width)], far_cross, sems, 2, 6)
    )
    for copy in copies:
        copy.start()
    for copy in copies:
        copy.wait()


def slices(where, hidden, out_weight, members):
    rows, width = hidden.shape
    share, depth = width // members, out_weight.shape[0]
    return pl.pallas_call(
        slices_kernel,
        out_shape=(
            near_out((rows // 2, width)),
            near_out((depth, share)),
            near_out((depth, share)),
        ),
        in_specs=[smem_spec(), any_spec(), any_spec()],
        out_specs=(vmem_spec(),) * 3,
        scratch_shapes=[pltpu.SemaphoreType.DMA((8,))],
        compiler_params=pltpu.CompilerParams(vmem_limit_bytes=2 * MIB),
        cost_estimate=cost(0, 4 * MIB),
    )(where, far(hidden), far(out_weight))


ROW = 384


def modulate_kernel(where_ref, emb_ref, mod_ref, payload, rows_ref):
    rows_ref[...] = jnp.zeros_like(rows_ref)
    columns = mod_ref.shape[0]
    rows_ref[:, :columns] = lax.dot_general(
        emb_ref[...], mod_ref[...], (((1,), (1,)), ((), ())), preferred_element_type=jnp.float32
    )
    rows = rows_ref[...]
    slots = rows.shape[0]
    even = lax.broadcasted_iota(jnp.int32, rows.shape, 0) % 2 == 0
    following = pltpu.roll(rows, slots - 1, 0)
    partner = jnp.where(even, following, pltpu.roll(rows, 1, 0))
    joined = jnp.where(where_ref[1] == 0, rows, partner) + pltpu.roll(following, columns, 1)
    for slot in range(slots):
        payload[slot] = joined[slot : slot + 1, :]


def modulate(where, emb, mod_weight):
    return pl.pallas_call(
        modulate_kernel,
        out_shape=jax.ShapeDtypeStruct((emb.shape[0], 1, ROW), jnp.float32),
        in_specs=[smem_spec(), vmem_spec(), vmem_spec()],
        out_specs=vmem_spec(),
        scratch_shapes=[pltpu.VMEM((emb.shape[0], ROW), jnp.float32)],
        compiler_params=pltpu.CompilerParams(vmem_limit_bytes=2 * MIB),
        cost_estimate=cost(10**7, MIB),
    )(where, emb, mod_weight.T)


NORM_ROWS = 16


def spread(rows_ref, part, flat):
    slots = rows_ref.shape[0]
    columns = flat.shape[1] // slots
    step = columns - PAIR
    row = lax.broadcasted_iota(jnp.int32, (8, 2 * PAIR), 0)
    at = lax.broadcasted_iota(jnp.int32, (8, 2 * PAIR), 1) - step * row
    held = (at >= 0) & (at < columns)
    first_row = row[:, :PAIR] == 0
    for i in range(slots // 8):
        block = rows_ref[8 * i : 8 * i + 8, :]
        if part:
            block = pltpu.roll(block, ROW - columns * part, 1)
        turned = pltpu.roll(block, 0, 1, stride=step, stride_axis=0)
        turned = jnp.where(held, turned[:, : 2 * PAIR], 0.0)
        carried = turned[:, PAIR:]
        tiles = turned[:, :PAIR] + jnp.where(first_row, 0.0, pltpu.roll(carried, 1, 0))
        base = 8 * i * columns
        for j in range(8):
            flat[:, base + j * PAIR : base + (j + 1) * PAIR] = tiles[j : j + 1, :]
        flat[:, base + 8 * PAIR : base + 9 * PAIR] = carried[7:8, :]


def kv_kernel(
    where_ref, rows_ref, hidden, first, second, own_weight, twin_weight, out_weight, kv_ref, k_ref, v_ref, states_ref, q_weight,
    twin_out, share_ref,
    flat, weight, x_sems, w_sems,
):
    core, parity = where_ref[1], where_ref[4]
    rows, width = states_ref.shape
    half = rows // 2
    each = q_weight.shape[1]
    from_own = copies_of(hidden, states_ref, x_sems, 4)
    from_pair = copies_of(first, states_ref.at[pl.ds(0, half), :], x_sems, 2) + copies_of(
        second, states_ref.at[pl.ds(half, half), :], x_sems, 2, 2
    )

    def weights_from(source):
        return [
            copies_of(source.at[kind], target, w_sems, 2, 2 * kind)
            for kind, target in (
                (1, weight.at[:, pl.ds(0, each)]),
                (2, weight.at[:, pl.ds(each, each)]),
                (0, q_weight),
            )
        ]

    def start(condition, copies):
        @pl.when(condition)
        def _():
            for copy in copies:
                copy.start()

    start(core == 0, from_own)
    start(core == 1, from_pair)
    start(core == parity, sum(weights_from(own_weight)[:2], []))
    start(core != parity, sum(weights_from(twin_weight)[:2], []))
    beside = where_ref[2] * 2 + 1 - core
    asides = copies_of(out_weight.at[:, lanes_at(beside, twin_out.shape[1])], twin_out, w_sems, 2, 6)
    spread(rows_ref, 0, flat)
    scale, shift = 1.0 + flat[:, width : 2 * width], flat[:, :width]

    def normalise(first_row):
        for start in range(first_row, first_row + half, NORM_ROWS):
            block = pl.ds(start, NORM_ROWS)
            states = states_ref[block, :].astype(jnp.float32)
            mean = jnp.mean(states, axis=1, keepdims=True)
            centred = states - mean
            var = jnp.mean(centred * centred, axis=1, keepdims=True)
            states_ref[block, :] = (centred * lax.rsqrt(var + 1e-05) * scale + shift).astype(jnp.bfloat16)

    for copy in from_own:
        copy.wait()
    share_ref[...] = states_ref[:, lanes_at(where_ref[0], share_ref.shape[1])]
    normalise(0)
    normalise(half)
    keys, values, queries = weights_from(own_weight)
    for copy in keys + values:
        copy.wait()
    start(core == parity, weights_from(own_weight)[2])
    start(core != parity, weights_from(twin_weight)[2])
    for copy in asides:
        copy.start()
    kv = jnp.dot(states_ref[...], weight[...], preferred_element_type=jnp.float32).astype(jnp.bfloat16)
    kv_ref[...] = kv
    k_ref[...] = kv[:, :each]
    v_ref[...] = kv[:, each:]
    for copy in queries + asides:
        copy.wait()


def keys_values(where, mod_rows, hidden, first, second, own_weight, twin_weight, out_weight):
    rows, width = hidden.shape
    each = own_weight.shape[2]
    return pl.pallas_call(
        kv_kernel,
        out_shape=(
            near_out((rows, 2 * each)),
            near_out((rows, each)),
            near_out((rows, each)),
            near_out((rows, width)),
            near_out((width, each)),
            near_out((out_weight.shape[0], width // 4)),
            near_out((rows, width // 4)),
        ),
        in_specs=[smem_spec(), vmem_spec()] + [any_spec()] * 6,
        out_specs=(vmem_spec(),) * 7,
        scratch_shapes=[
            pltpu.VMEM((1, 3 * width), jnp.float32),
            pltpu.VMEM((width, 2 * each), jnp.bfloat16),
            pltpu.SemaphoreType.DMA((4,)),
            pltpu.SemaphoreType.DMA((8,)),
        ],
        compiler_params=pltpu.CompilerParams(vmem_limit_bytes=24 * MIB),
        cost_estimate=cost(1, 1),
    )(where, mod_rows, far(hidden), first, second, far(own_weight), twin_weight, far(out_weight))


def query_kernel(normed, weight, query_ref):
    query = jnp.dot(normed[...], weight[...], preferred_element_type=jnp.float32).astype(jnp.bfloat16)
    query_ref[...] = (query * HD ** (-0.5)).astype(jnp.bfloat16)


def queries(normed, weight):
    return pl.pallas_call(
        query_kernel,
        out_shape=near_out((normed.shape[0], weight.shape[1])),
        in_specs=[vmem_spec()] * 2,
        out_specs=vmem_spec(),
        compiler_params=pltpu.CompilerParams(vmem_limit_bytes=4 * MIB),
        cost_estimate=cost(1, 1),
    )(near(normed), near(weight))


def count_at(counts_ref, at):
    inside = (at >= 0) & (at < counts_ref.shape[0])
    return jnp.where(inside, counts_ref[jnp.where(inside, at, 0)], 0)


LOG2E = math.log2(math.e)


def scores_of(query, keys):
    return lax.dot_general(query, keys, (((1,), (1,)), ((), ())), preferred_element_type=jnp.float32)


def dead_rows(span, count):
    row = lax.broadcasted_iota(jnp.int32, (span, PAIR), 0)
    return jnp.where(row < count * P_SIZE, 0.0, NEG).astype(jnp.bfloat16)


def two_heads(keys, values, dead):
    low = low_lanes(keys.shape)
    lane = lax.broadcasted_iota(jnp.int32, keys.shape, 1)
    zero, one = jnp.zeros_like(keys), jnp.ones_like(values)
    return (
        (jnp.where(low, keys, jnp.where(lane == HD, dead, zero)), jnp.where(low, values, one)),
        (jnp.where(low, jnp.where(lane == 0, dead, zero), keys), jnp.where(low, one, values)),
    )


def two_queries(query):
    low = low_lanes(query.shape)
    lane = lax.broadcasted_iota(jnp.int32, query.shape, 1)
    zero, one = jnp.zeros_like(query), jnp.ones_like(query)
    return (
        jnp.where(low, query, jnp.where(lane == HD, one, zero)),
        jnp.where(low, jnp.where(lane == 0, one, zero), query),
    )


def attend(query_of, pairs, blocks, before_of, finish):
    units = [(pair, rows) for pair in range(len(pairs)) for rows in blocks]

    def scores(unit):
        pair, rows = unit
        return [scores_of(q, keys) for q, (keys, _) in zip(two_queries(query_of(pair, rows)), pairs[pair])]

    following = scores(units[0])
    for index, (pair, rows) in enumerate(units):
        current = following
        if index + 1 < len(units):
            following = scores(units[index + 1])
        peaks, numers = [], []
        for head in range(2):
            peak = jnp.max(current[head], axis=1, keepdims=True)
            before = before_of(pair, rows, head)
            peak = peak if before is None else jnp.maximum(peak, before)
            probs = jnp.exp2((current[head] - peak) * LOG2E).astype(jnp.bfloat16)
            peaks.append(peak)
            numers.append(jnp.dot(probs, pairs[pair][head][1], preferred_element_type=jnp.float32))
        low = low_lanes(numers[0].shape)
        total = pltpu.roll(jnp.where(low, numers[1], numers[0]), HD, 1)
        finish(pair, rows, jnp.where(low, *numers), jnp.where(low, *peaks), total)


def pair_lanes(pair):
    return slice(pair * PAIR, (pair + 1) * PAIR)


def local_kernel(where_ref, counts_ref, q_ref, own_ref, k_twin, v_twin, o_ref, m_ref, l_ref):
    span = own_ref.shape[0]
    tile = 256
    core, slot = where_ref[1], where_ref[6]
    partner = slot + 1 - 2 * where_ref[4]
    own_count = count_at(counts_ref, jnp.where(core == 0, slot, partner))
    twin_count = count_at(counts_ref, jnp.where(core == 0, partner, slot))
    dead = jnp.concatenate([dead_rows(span, own_count), dead_rows(span, twin_count)], axis=0)
    pairs = [
        two_heads(
            jnp.concatenate([own_ref[:, pair_lanes(pair)], k_twin[:, pair_lanes(pair)]], axis=0),
            jnp.concatenate([own_ref[:, pair_lanes(3 + pair)], v_twin[:, pair_lanes(pair)]], axis=0),
            dead,
        )
        for pair in range(3)
    ]

    def finish(pair, rows, numer, peak, total):
        o_ref[rows, pair_lanes(pair)] = numer
        m_ref[rows, pair_lanes(pair)] = peak
        l_ref[rows, pair_lanes(pair)] = total

    attend(
        lambda pair, rows: q_ref[rows, pair_lanes(pair)],
        pairs,
        [pl.ds(start, tile) for start in range(0, span, tile)],
        lambda pair, rows, head: None,
        finish,
    )


def local_attention(where, counts, query, own, k_twin, v_twin):
    span = query.shape[0]
    part = near_out((span, 3 * PAIR), jnp.float32)
    return pl.pallas_call(
        local_kernel,
        out_shape=(part,) * 3,
        in_specs=[smem_spec()] * 2 + [vmem_spec()] * 4,
        out_specs=(vmem_spec(),) * 3,
        compiler_params=pltpu.CompilerParams(vmem_limit_bytes=16 * MIB),
        cost_estimate=cost(8 * 6 * span * span * 256, 3 * MIB),
    )(where, counts, near(query), near(own), k_twin, v_twin)


def remote_kernel(where_ref, counts_ref, q_ref, kv_ref, o_ref, m_ref, l_ref, piece_ref):
    span = kv_ref.shape[0]
    tile = 256
    core, slot = where_ref[1], where_ref[6]
    step = 1 - 2 * where_ref[4]
    count = count_at(counts_ref, jnp.where(core == 0, slot - step, slot + 2 * step))
    dead = dead_rows(span, count)
    pairs = [
        two_heads(kv_ref[:, pair_lanes(pair)], kv_ref[:, pair_lanes(3 + pair)], dead) for pair in range(3)
    ]

    def before(pair, rows, head):
        at = pair * PAIR + head * HD
        return m_ref[rows, at : at + 1]

    def finish(pair, rows, numer, peak, total):
        lanes = pair_lanes(pair)
        fade = jnp.exp2((m_ref[rows, lanes] - peak) * LOG2E)
        attn = (numer + fade * o_ref[rows, lanes]) / (total + fade * l_ref[rows, lanes])
        piece_ref[rows, lanes] = attn.astype(jnp.bfloat16)

    attend(
        lambda pair, rows: q_ref[rows, pair_lanes(pair)],
        pairs,
        [pl.ds(start, tile) for start in range(0, span, tile)],
        before,
        finish,
    )


def remote_attention(where, counts, query, kv, o, m, l):
    span = query.shape[0]
    return pl.pallas_call(
        remote_kernel,
        out_shape=near_out((span, 3 * PAIR)),
        in_specs=[smem_spec()] * 2 + [vmem_spec()] * 5,
        out_specs=vmem_spec(),
        compiler_params=pltpu.CompilerParams(vmem_limit_bytes=16 * MIB),
        cost_estimate=cost(1, 1),
    )(where, counts, near(query), kv, near(o), near(m), near(l))


def tail_kernel(
    where_ref, rows_ref, out_weight, w_twin, w_far, w_far_twin, gathered, gate, flat, sems,
):
    member, core, parity = where_ref[0], where_ref[1], where_ref[4]
    share = gathered.shape[1]
    width = flat.shape[1] // 3
    block = out_weight.shape[0]
    local = jnp.where(core == 0, 1 - parity, parity)
    whole, own = pl.ds(0, share), lanes_at(member, share)
    copies = []
    for source, lanes, far_half, y_lo in (
        (out_weight, own, 0, core),
        (w_twin, whole, 0, 1 - core),
        (w_far, whole, 1, core),
        (w_far_twin, whole, 1, 1 - core),
    ):
        base = jnp.where(local == y_lo, 0, 2 * block) + far_half * block
        to = pl.ds(pl.multiple_of(base, block), block)
        copies += copies_of(source.at[:, lanes], gathered.at[to, :], sems, 2, len(copies))
    for copy in copies:
        copy.start()
    spread(rows_ref, 1, flat)
    gate[...] = flat[:, pl.ds(pl.multiple_of(2 * width + member * share, PAIR), share)]
    for copy in copies:
        copy.wait()


def tail_inputs(where, mod_rows, out_weight, w_twin, w_far, w_far_twin):
    block, share = w_twin.shape
    width = out_weight.shape[1]
    return pl.pallas_call(
        tail_kernel,
        out_shape=(near_out((4 * block, share)), near_out((1, share), jnp.float32)),
        in_specs=[smem_spec(), vmem_spec()] + [any_spec()] * 4,
        out_specs=(vmem_spec(),) * 2,
        scratch_shapes=[pltpu.VMEM((1, 3 * width), jnp.float32), pltpu.SemaphoreType.DMA((8,))],
        compiler_params=pltpu.CompilerParams(vmem_limit_bytes=2 * MIB),
        cost_estimate=cost(1, 1),
    )(where, mod_rows, far(out_weight), w_twin, w_far, w_far_twin)


def first_out_kernel(where_ref, same, cross, held, weight, partial):
    here = (where_ref[4] == 0) & (where_ref[1] == 1)
    attn = jnp.concatenate([jnp.where(here, held[...], same[...]), cross[...]], axis=1)
    partial[...] = jnp.dot(attn, weight[: attn.shape[1], :], preferred_element_type=jnp.float32)


def first_out(where, same, cross, held, weight):
    span, share = same.shape[0], weight.shape[1]
    return pl.pallas_call(
        first_out_kernel,
        out_shape=near_out((span, share), jnp.float32),
        in_specs=[smem_spec()] + [vmem_spec()] * 4,
        out_specs=vmem_spec(),
        compiler_params=pltpu.CompilerParams(vmem_limit_bytes=8 * MIB),
        cost_estimate=cost(1, 1),
    )(where, same, cross, near(held), near(weight))


TILE = 128


def last_out_kernel(
    where_ref, same, cross, held, weight, partial, kept, residual, gate, fresh, out, ready, sems
):
    here = (where_ref[4] == 0) & (where_ref[1] == 0)
    holds = (where_ref[4] == 0) & (where_ref[1] == 1)
    last = where_ref[5] == 1
    span = partial.shape[0]
    tiles = span // TILE

    @pl.when(last)
    def _():
        for source, target in ((fresh, ready), (ready, out)):
            copies = copies_of(source, target, sems, tiles)
            for copy in copies:
                copy.start()
            for copy in copies:
                copy.wait()

    @pl.when(jnp.logical_not(last))
    def _():
        copies = []
        for index, first_row in enumerate(range(0, span, TILE)):
            rows = slice(first_row, first_row + TILE)
            attn = jnp.concatenate([jnp.where(here, held[rows, :], same[rows, :]), cross[rows, :]], axis=1)
            summed = partial[rows, :] + jnp.dot(
                attn, weight[attn.shape[1] :, :], preferred_element_type=jnp.float32
            )
            states = jnp.where(holds, kept[rows, :], residual[rows, :])
            ready[rows, :] = (states.astype(jnp.float32) + gate[...] * summed).astype(jnp.bfloat16)
            block = pl.ds(first_row, TILE)
            copies.append(pltpu.make_async_copy(ready.at[block, :], out.at[block, :], sems.at[index]))
            copies[-1].start()
        for copy in copies:
            copy.wait()


def last_out(where, same, cross, held, weight, partial, kept, residual, gate, fresh):
    span, share = partial.shape
    return pl.pallas_call(
        last_out_kernel,
        out_shape=jax.ShapeDtypeStruct((span, share), jnp.bfloat16),
        in_specs=[smem_spec()] + [vmem_spec()] * 8 + [any_spec()],
        out_specs=any_spec(),
        scratch_shapes=[pltpu.VMEM((span, share), jnp.bfloat16), pltpu.SemaphoreType.DMA((4,))],
        compiler_params=pltpu.CompilerParams(vmem_limit_bytes=8 * MIB),
        cost_estimate=cost(1, 1),
    )(where, same, cross, held, near(weight), near(partial), near(kept), residual, near(gate), far(fresh))


def on_device(hidden, levels, frame_counts, mod_weight, qkv_weight, out_weight, fresh):
    rows, width = hidden.shape
    slot = lax.axis_index("queue")
    queue_len = lax.axis_size("queue")
    member = lax.axis_index("heads")
    members = lax.axis_size("heads")
    share = width // members
    parity, core, y_hi = slot % 2, member % 2, member // 2
    z_half = (slot // 8) % 2
    half = rows // 2
    route = functools.partial(routed, queue_len=queue_len, members=members)
    twin = lambda a: route(a, target=lambda s, y, k: (s, y, 1 - k))

    where = jnp.stack(
        [member, core, y_hi, z_half, parity, (slot == queue_len - 1).astype(jnp.int32), slot]
    ).astype(jnp.int32)
    after = lambda a, *b: lax.optimization_barrier((a, *b))[0]
    frame_counts = frame_counts.astype(jnp.int32)

    twin_weight = twin(qkv_weight)
    mine, far_same, far_cross = slices(where, hidden, out_weight, members)
    second = route(mine, target=lambda s, y, k: (s ^ 1, y ^ k, k))

    payload = modulate(where, embed_levels(levels, mod_weight.shape[0]), mod_weight)
    mod_rows = lax.all_to_all(payload, "queue", 0, 0, tiled=True)[:, 0, :]

    first = twin(after(second, mod_rows))
    w_far = route(after(far_same, mod_rows), target=lambda s, y, k: (s ^ 1, 1 - y, k))
    w_far_twin = route(after(far_cross, mod_rows), target=lambda s, y, k: (s ^ 1, 1 - y, 1 - k))
    kv, k, v, normed, q_weight, twin_mine, share_states = keys_values(where, mod_rows, hidden, first, second, qkv_weight, twin_weight, out_weight)

    def remote_target(s, y, k):
        back = (s % 2 == 0) == (k == 0)
        return (s - 2 if back else s + 2, y, 1 - k)

    kv_remote = route(kv, target=remote_target)
    k_twin, v_twin = twin(k), twin(v)
    query = queries(after(normed, kv), q_weight)
    w_twin = twin(twin_mine)
    o, m, l = local_attention(after(where, w_far_twin), frame_counts, query, kv, k_twin, v_twin)
    residual = route(
        after(share_states, o),
        target=lambda s, y, k: (s - 1, y, 0) if k == 0 else ((s - 2, y, 1) if s % 2 else None),
    )
    attn = remote_attention(after(where, w_far), frame_counts, query, kv_remote, o, m, l)

    def goal(s, y, k):
        if k == 0:
            return (s - 1, y, 0)
        return (s if s % 2 == 0 else s - 2, y, 1)

    same = route(attn, target=lambda s, y, k: None if s % 2 == 0 and k == 1 else goal(s, y, k))
    cross = route(attn, target=lambda s, y, k: goal(s, 1 - y, k))
    twin_attn = twin(attn)
    weight, gate = tail_inputs(where, mod_rows, out_weight, w_twin, w_far, w_far_twin)
    same, cross, residual, _ = lax.optimization_barrier((same, cross, residual, weight))
    partial = first_out(where, same, cross, attn, weight)
    return last_out(where, twin(same), twin(cross), twin_attn, weight, partial, share_states, residual, gate, fresh)


def solution(mesh):
    placed = (
        P("queue", None),
        P(),
        P(),
        P(None, "queue"),
        P(None, None, "heads"),
        P("heads", None),
        P(None, "heads"),
    )
    return jax.shard_map(
        on_device, mesh=mesh, in_specs=placed, out_specs=P("queue", "heads"), check_vma=False
    )
```

```python
import functools
import math

import jax
import jax.numpy as jnp
from jax import lax
from jax.experimental import pallas as pl
from jax.experimental.pallas import tpu as pltpu
from jax.sharding import PartitionSpec as P

HD = 64
P_SIZE = 256
PAIR = 2 * HD
NEG = -1e30
BOTH = ("queue", "heads")
MIB = 1024 * 1024


def embed_levels(levels, width):
    halfway = width // 2
    freqs = jnp.exp(-math.log(10000.0) * jnp.arange(halfway, dtype=jnp.float32) / halfway)
    angles = levels.astype(jnp.float32)[:, None] * freqs[None, :]
    return jax.nn.silu(jnp.concatenate([jnp.cos(angles), jnp.sin(angles)], axis=1)).astype(
        jnp.bfloat16
    )


def routed(array, queue_len, members, target):
    pairs = []
    for slot in range(queue_len):
        for member in range(members):
            goal = target(slot, member // 2, member % 2)
            if goal is not None and 0 <= goal[0] < queue_len:
                pairs.append((slot * members + member, goal[0] * members + goal[1] * 2 + goal[2]))
    return lax.ppermute(array, BOTH, pairs)


def low_lanes(shape):
    return lax.broadcasted_iota(jnp.int32, shape, len(shape) - 1) < HD


def copies_of(source, target, sems, chunks, first=0):
    step = source.shape[0] // chunks
    return [
        pltpu.make_async_copy(
            source.at[pl.ds(i * step, step), :], target.at[pl.ds(i * step, step), :], sems.at[first + i]
        )
        for i in range(chunks)
    ]


def any_spec():
    return pl.BlockSpec(memory_space=pl.ANY)


def far(array):
    return pltpu.with_memory_space_constraint(array, pltpu.HBM)


def near(array):
    return pltpu.with_memory_space_constraint(array, pltpu.VMEM)


def near_out(shape, dtype=jnp.bfloat16):
    return pltpu.VMEM(shape, dtype)


def cost(flops, moved, transcendentals=0):
    return pl.CostEstimate(flops=flops, bytes_accessed=moved, transcendentals=transcendentals)


def vmem_spec():
    return pl.BlockSpec(memory_space=pltpu.VMEM)


def smem_spec():
    return pl.BlockSpec(memory_space=pltpu.SMEM)


def lanes_at(index, size):
    return pl.ds(pl.multiple_of(index * size, size), size)


def slices_kernel(where_ref, hidden, out_weight, mine, far_out, sems):
    core, y_hi = where_ref[1], where_ref[2]
    half, width = mine.shape[0], far_out.shape[1]
    copies = (
        copies_of(hidden.at[lanes_at(core, half), :], mine, sems, 4)
        + copies_of(out_weight.at[:, lanes_at(1 - y_hi, width)], far_out, sems, 4, 4)
    )
    for copy in copies:
        copy.start()
    for copy in copies:
        copy.wait()


def slices(where, hidden, out_weight, members):
    rows, width = hidden.shape
    share, depth = width // members, out_weight.shape[0]
    return pl.pallas_call(
        slices_kernel,
        out_shape=(
            near_out((rows // 2, width)),
            near_out((depth, 2 * share)),
        ),
        in_specs=[smem_spec(), any_spec(), any_spec()],
        out_specs=(vmem_spec(),) * 2,
        scratch_shapes=[pltpu.SemaphoreType.DMA((8,))],
        compiler_params=pltpu.CompilerParams(vmem_limit_bytes=2 * MIB),
        cost_estimate=cost(0, 4 * MIB),
    )(where, far(hidden), far(out_weight))


ROW = 384


def modulate_kernel(where_ref, emb_ref, mod_ref, payload, rows_ref):
    rows_ref[...] = jnp.zeros_like(rows_ref)
    columns = mod_ref.shape[0]
    rows_ref[:, :columns] = lax.dot_general(
        emb_ref[...], mod_ref[...], (((1,), (1,)), ((), ())), preferred_element_type=jnp.float32
    )
    rows = rows_ref[...]
    slots = rows.shape[0]
    even = lax.broadcasted_iota(jnp.int32, rows.shape, 0) % 2 == 0
    following = pltpu.roll(rows, slots - 1, 0)
    partner = jnp.where(even, following, pltpu.roll(rows, 1, 0))
    joined = jnp.where(where_ref[1] == 0, rows, partner) + pltpu.roll(following, columns, 1)
    for slot in range(slots):
        payload[slot] = joined[slot : slot + 1, :]


def modulate(where, emb, mod_weight):
    return pl.pallas_call(
        modulate_kernel,
        out_shape=jax.ShapeDtypeStruct((emb.shape[0], 1, ROW), jnp.float32),
        in_specs=[smem_spec(), vmem_spec(), vmem_spec()],
        out_specs=vmem_spec(),
        scratch_shapes=[pltpu.VMEM((emb.shape[0], ROW), jnp.float32)],
        compiler_params=pltpu.CompilerParams(vmem_limit_bytes=2 * MIB),
        cost_estimate=cost(10**7, MIB),
    )(where, emb, mod_weight.T)


NORM_ROWS = 16


def spread(rows_ref, part, flat):
    slots = rows_ref.shape[0]
    columns = flat.shape[1] // slots
    step = columns - PAIR
    row = lax.broadcasted_iota(jnp.int32, (8, 2 * PAIR), 0)
    at = lax.broadcasted_iota(jnp.int32, (8, 2 * PAIR), 1) - step * row
    held = (at >= 0) & (at < columns)
    first_row = row[:, :PAIR] == 0
    for i in range(slots // 8):
        block = rows_ref[8 * i : 8 * i + 8, :]
        if part:
            block = pltpu.roll(block, ROW - columns * part, 1)
        turned = pltpu.roll(block, 0, 1, stride=step, stride_axis=0)
        turned = jnp.where(held, turned[:, : 2 * PAIR], 0.0)
        carried = turned[:, PAIR:]
        tiles = turned[:, :PAIR] + jnp.where(first_row, 0.0, pltpu.roll(carried, 1, 0))
        base = 8 * i * columns
        for j in range(8):
            flat[:, base + j * PAIR : base + (j + 1) * PAIR] = tiles[j : j + 1, :]
        flat[:, base + 8 * PAIR : base + 9 * PAIR] = carried[7:8, :]


def kv_kernel(
    where_ref, rows_ref, hidden, first, second, own_weight, twin_weight, out_weight, kv_ref, k_ref, v_ref, states_ref, q_weight,
    twin_out, share_ref,
    flat, weight, x_sems, w_sems,
):
    core, parity = where_ref[1], where_ref[4]
    rows, width = states_ref.shape
    half = rows // 2
    each = q_weight.shape[1]
    from_own = copies_of(hidden, states_ref, x_sems, 4)
    from_pair = copies_of(first, states_ref.at[pl.ds(0, half), :], x_sems, 2) + copies_of(
        second, states_ref.at[pl.ds(half, half), :], x_sems, 2, 2
    )

    def weights_from(source):
        return [
            copies_of(source.at[kind], target, w_sems, 2, 2 * kind)
            for kind, target in (
                (1, weight.at[:, pl.ds(0, each)]),
                (2, weight.at[:, pl.ds(each, each)]),
                (0, q_weight),
            )
        ]

    def start(condition, copies):
        @pl.when(condition)
        def _():
            for copy in copies:
                copy.start()

    start(core == 0, from_own)
    start(core == 1, from_pair)
    start(core == parity, sum(weights_from(own_weight)[:2], []))
    start(core != parity, sum(weights_from(twin_weight)[:2], []))
    beside = where_ref[2] * 2 + 1 - core
    asides = copies_of(out_weight.at[:, lanes_at(beside, twin_out.shape[1])], twin_out, w_sems, 2, 6)
    spread(rows_ref, 0, flat)
    scale, shift = 1.0 + flat[:, width : 2 * width], flat[:, :width]

    def normalise(first_row, count):
        for start in range(first_row, first_row + count, NORM_ROWS):
            block = pl.ds(start, NORM_ROWS)
            states = states_ref[block, :].astype(jnp.float32)
            mean = jnp.mean(states, axis=1, keepdims=True)
            centred = states - mean
            var = jnp.mean(centred * centred, axis=1, keepdims=True)
            states_ref[block, :] = (centred * lax.rsqrt(var + 1e-05) * scale + shift).astype(jnp.bfloat16)

    step = rows // len(from_own)
    for index, copy in enumerate(from_own):
        copy.wait()
        block = pl.ds(index * step, step)
        share_ref[block, :] = states_ref[block, lanes_at(where_ref[0], share_ref.shape[1])]
        normalise(index * step, step)
    keys, values, queries = weights_from(own_weight)
    for copy in keys + values:
        copy.wait()
    start(core == parity, weights_from(own_weight)[2])
    start(core != parity, weights_from(twin_weight)[2])
    for copy in asides:
        copy.start()
    kv = jnp.dot(states_ref[...], weight[...], preferred_element_type=jnp.float32).astype(jnp.bfloat16)
    kv_ref[...] = kv
    k_ref[...] = kv[:, :each]
    v_ref[...] = kv[:, each:]
    for copy in queries + asides:
        copy.wait()


def keys_values(where, mod_rows, hidden, first, second, own_weight, twin_weight, out_weight):
    rows, width = hidden.shape
    each = own_weight.shape[2]
    return pl.pallas_call(
        kv_kernel,
        out_shape=(
            near_out((rows, 2 * each)),
            near_out((rows, each)),
            near_out((rows, each)),
            near_out((rows, width)),
            near_out((width, each)),
            near_out((out_weight.shape[0], width // 4)),
            near_out((rows, width // 4)),
        ),
        in_specs=[smem_spec(), vmem_spec()] + [any_spec()] * 6,
        out_specs=(vmem_spec(),) * 7,
        scratch_shapes=[
            pltpu.VMEM((1, 3 * width), jnp.float32),
            pltpu.VMEM((width, 2 * each), jnp.bfloat16),
            pltpu.SemaphoreType.DMA((4,)),
            pltpu.SemaphoreType.DMA((8,)),
        ],
        compiler_params=pltpu.CompilerParams(vmem_limit_bytes=24 * MIB),
        cost_estimate=cost(1, 1),
    )(where, mod_rows, far(hidden), first, second, far(own_weight), twin_weight, far(out_weight))


def query_kernel(normed, weight, query_ref):
    query = jnp.dot(normed[...], weight[...], preferred_element_type=jnp.float32).astype(jnp.bfloat16)
    query_ref[...] = (query * HD ** (-0.5)).astype(jnp.bfloat16)


def queries(normed, weight):
    return pl.pallas_call(
        query_kernel,
        out_shape=near_out((normed.shape[0], weight.shape[1])),
        in_specs=[vmem_spec()] * 2,
        out_specs=vmem_spec(),
        compiler_params=pltpu.CompilerParams(vmem_limit_bytes=4 * MIB),
        cost_estimate=cost(1, 1),
    )(near(normed), near(weight))


def count_at(counts_ref, at):
    inside = (at >= 0) & (at < counts_ref.shape[0])
    return jnp.where(inside, counts_ref[jnp.where(inside, at, 0)], 0)


LOG2E = math.log2(math.e)


def scores_of(query, keys):
    return lax.dot_general(query, keys, (((1,), (1,)), ((), ())), preferred_element_type=jnp.float32)


def dead_rows(span, count):
    row = lax.broadcasted_iota(jnp.int32, (span, PAIR), 0)
    return jnp.where(row < count * P_SIZE, 0.0, NEG).astype(jnp.bfloat16)


def two_heads(keys, values, dead):
    low = low_lanes(keys.shape)
    lane = lax.broadcasted_iota(jnp.int32, keys.shape, 1)
    zero, one = jnp.zeros_like(keys), jnp.ones_like(values)
    return (
        (jnp.where(low, keys, jnp.where(lane == HD, dead, zero)), jnp.where(low, values, one)),
        (jnp.where(low, jnp.where(lane == 0, dead, zero), keys), jnp.where(low, one, values)),
    )


def two_queries(query):
    low = low_lanes(query.shape)
    lane = lax.broadcasted_iota(jnp.int32, query.shape, 1)
    zero, one = jnp.zeros_like(query), jnp.ones_like(query)
    return (
        jnp.where(low, query, jnp.where(lane == HD, one, zero)),
        jnp.where(low, jnp.where(lane == 0, one, zero), query),
    )


def attend(query_of, pairs, blocks, before_of, finish):
    units = [(pair, rows) for pair in range(len(pairs)) for rows in blocks]

    def scores(unit):
        pair, rows = unit
        return [scores_of(q, keys) for q, (keys, _) in zip(two_queries(query_of(pair, rows)), pairs[pair])]

    following = scores(units[0])
    for index, (pair, rows) in enumerate(units):
        current = following
        if index + 1 < len(units):
            following = scores(units[index + 1])
        peaks, numers = [], []
        for head in range(2):
            peak = jnp.max(current[head], axis=1, keepdims=True)
            before = before_of(pair, rows, head)
            peak = peak if before is None else jnp.maximum(peak, before)
            probs = jnp.exp2((current[head] - peak) * LOG2E).astype(jnp.bfloat16)
            peaks.append(peak)
            numers.append(jnp.dot(probs, pairs[pair][head][1], preferred_element_type=jnp.float32))
        low = low_lanes(numers[0].shape)
        total = pltpu.roll(jnp.where(low, numers[1], numers[0]), HD, 1)
        finish(pair, rows, jnp.where(low, *numers), jnp.where(low, *peaks), total)


def pair_lanes(pair):
    return slice(pair * PAIR, (pair + 1) * PAIR)


def local_kernel(where_ref, counts_ref, q_ref, own_ref, k_twin, v_twin, o_ref, m_ref, l_ref):
    span = own_ref.shape[0]
    tile = 256
    core, slot = where_ref[1], where_ref[6]
    partner = slot + 1 - 2 * where_ref[4]
    own_count = count_at(counts_ref, jnp.where(core == 0, slot, partner))
    twin_count = count_at(counts_ref, jnp.where(core == 0, partner, slot))
    dead = jnp.concatenate([dead_rows(span, own_count), dead_rows(span, twin_count)], axis=0)
    pairs = [
        two_heads(
            jnp.concatenate([own_ref[:, pair_lanes(pair)], k_twin[:, pair_lanes(pair)]], axis=0),
            jnp.concatenate([own_ref[:, pair_lanes(3 + pair)], v_twin[:, pair_lanes(pair)]], axis=0),
            dead,
        )
        for pair in range(3)
    ]

    def finish(pair, rows, numer, peak, total):
        o_ref[rows, pair_lanes(pair)] = numer
        m_ref[rows, pair_lanes(pair)] = peak
        l_ref[rows, pair_lanes(pair)] = total

    attend(
        lambda pair, rows: q_ref[rows, pair_lanes(pair)],
        pairs,
        [pl.ds(start, tile) for start in range(0, span, tile)],
        lambda pair, rows, head: None,
        finish,
    )


def local_attention(where, counts, query, own, k_twin, v_twin):
    span = query.shape[0]
    part = near_out((span, 3 * PAIR), jnp.float32)
    return pl.pallas_call(
        local_kernel,
        out_shape=(part,) * 3,
        in_specs=[smem_spec()] * 2 + [vmem_spec()] * 4,
        out_specs=(vmem_spec(),) * 3,
        compiler_params=pltpu.CompilerParams(vmem_limit_bytes=16 * MIB),
        cost_estimate=cost(1, 1),
    )(where, counts, near(query), near(own), k_twin, v_twin)


def remote_kernel(where_ref, counts_ref, q_ref, kv_ref, o_ref, m_ref, l_ref, piece_ref):
    span = kv_ref.shape[0]
    tile = 256
    core, slot = where_ref[1], where_ref[6]
    step = 1 - 2 * where_ref[4]
    count = count_at(counts_ref, jnp.where(core == 0, slot - step, slot + 2 * step))
    dead = dead_rows(span, count)
    pairs = [
        two_heads(kv_ref[:, pair_lanes(pair)], kv_ref[:, pair_lanes(3 + pair)], dead) for pair in range(3)
    ]

    def before(pair, rows, head):
        at = pair * PAIR + head * HD
        return m_ref[rows, at : at + 1]

    def finish(pair, rows, numer, peak, total):
        lanes = pair_lanes(pair)
        fade = jnp.exp2((m_ref[rows, lanes] - peak) * LOG2E)
        attn = (numer + fade * o_ref[rows, lanes]) / (total + fade * l_ref[rows, lanes])
        piece_ref[rows, lanes] = attn.astype(jnp.bfloat16)

    attend(
        lambda pair, rows: q_ref[rows, pair_lanes(pair)],
        pairs,
        [pl.ds(start, tile) for start in range(0, span, tile)],
        before,
        finish,
    )


def remote_attention(where, counts, query, kv, o, m, l):
    span = query.shape[0]
    return pl.pallas_call(
        remote_kernel,
        out_shape=near_out((span, 3 * PAIR)),
        in_specs=[smem_spec()] * 2 + [vmem_spec()] * 5,
        out_specs=vmem_spec(),
        compiler_params=pltpu.CompilerParams(vmem_limit_bytes=16 * MIB),
        cost_estimate=cost(1, 1),
    )(where, counts, near(query), kv, near(o), near(m), near(l))


def tail_kernel(
    where_ref, rows_ref, out_weight, w_twin, w_far, w_far_twin, gathered, gate, flat, sems,
):
    member, core, parity = where_ref[0], where_ref[1], where_ref[4]
    share = gathered.shape[1]
    width = flat.shape[1] // 3
    block = out_weight.shape[0]
    local = jnp.where(core == 0, 1 - parity, parity)
    whole, mine, own = pl.ds(0, share), lanes_at(core, share), lanes_at(member, share)
    copies = []
    for source, lanes, far_half, y_lo in (
        (out_weight, own, 0, core),
        (w_twin, whole, 0, 1 - core),
        (w_far, mine, 1, core),
        (w_far_twin, whole, 1, 1 - core),
    ):
        base = jnp.where(local == y_lo, 0, 2 * block) + far_half * block
        to = pl.ds(pl.multiple_of(base, block), block)
        copies += copies_of(source.at[:, lanes], gathered.at[to, :], sems, 2, len(copies))
    for copy in copies:
        copy.start()
    spread(rows_ref, 1, flat)
    gate[...] = flat[:, pl.ds(pl.multiple_of(2 * width + member * share, PAIR), share)]
    for copy in copies:
        copy.wait()


def columns_kernel(where_ref, source, out, sems):
    copies = copies_of(source.at[:, lanes_at(1 - where_ref[1], out.shape[1])], out, sems, 4)
    for copy in copies:
        copy.start()
    for copy in copies:
        copy.wait()


def columns_of_twin(where, blocks):
    rows, width = blocks.shape
    return pl.pallas_call(
        columns_kernel,
        out_shape=near_out((rows, width // 2)),
        in_specs=[smem_spec(), any_spec()],
        out_specs=vmem_spec(),
        scratch_shapes=[pltpu.SemaphoreType.DMA((4,))],
        compiler_params=pltpu.CompilerParams(vmem_limit_bytes=2 * MIB),
        cost_estimate=cost(1, 1),
    )(where, blocks)


def tail_inputs(where, mod_rows, out_weight, w_twin, w_far, w_far_twin):
    block, share = w_twin.shape
    width = out_weight.shape[1]
    return pl.pallas_call(
        tail_kernel,
        out_shape=(near_out((4 * block, share)), near_out((1, share), jnp.float32)),
        in_specs=[smem_spec(), vmem_spec()] + [any_spec()] * 4,
        out_specs=(vmem_spec(),) * 2,
        scratch_shapes=[pltpu.VMEM((1, 3 * width), jnp.float32), pltpu.SemaphoreType.DMA((8,))],
        compiler_params=pltpu.CompilerParams(vmem_limit_bytes=2 * MIB),
        cost_estimate=cost(1, 1),
    )(where, mod_rows, far(out_weight), w_twin, w_far, w_far_twin)


def first_out_kernel(where_ref, same, cross, held, weight, partial):
    here = (where_ref[4] == 0) & (where_ref[1] == 1)
    attn = jnp.concatenate([jnp.where(here, held[...], same[...]), cross[...]], axis=1)
    partial[...] = jnp.dot(attn, weight[: attn.shape[1], :], preferred_element_type=jnp.float32)


def first_out(where, same, cross, held, weight):
    span, share = same.shape[0], weight.shape[1]
    return pl.pallas_call(
        first_out_kernel,
        out_shape=near_out((span, share), jnp.float32),
        in_specs=[smem_spec()] + [vmem_spec()] * 4,
        out_specs=vmem_spec(),
        compiler_params=pltpu.CompilerParams(vmem_limit_bytes=8 * MIB),
        cost_estimate=cost(1, 1),
    )(where, same, cross, near(held), near(weight))


TILE = 128


def last_out_kernel(
    where_ref, same, cross, held, weight, partial, kept, residual, gate, fresh, out, ready, sems
):
    here = (where_ref[4] == 0) & (where_ref[1] == 0)
    holds = (where_ref[4] == 0) & (where_ref[1] == 1)
    last = where_ref[5] == 1
    span = partial.shape[0]
    tiles = span // TILE

    @pl.when(last)
    def _():
        for source, target in ((fresh, ready), (ready, out)):
            copies = copies_of(source, target, sems, tiles)
            for copy in copies:
                copy.start()
            for copy in copies:
                copy.wait()

    @pl.when(jnp.logical_not(last))
    def _():
        copies = []
        for index, first_row in enumerate(range(0, span, TILE)):
            rows = slice(first_row, first_row + TILE)
            attn = jnp.concatenate([jnp.where(here, held[rows, :], same[rows, :]), cross[rows, :]], axis=1)
            summed = partial[rows, :] + jnp.dot(
                attn, weight[attn.shape[1] :, :], preferred_element_type=jnp.float32
            )
            states = jnp.where(holds, kept[rows, :], residual[rows, :])
            ready[rows, :] = (states.astype(jnp.float32) + gate[...] * summed).astype(jnp.bfloat16)
            block = pl.ds(first_row, TILE)
            copies.append(pltpu.make_async_copy(ready.at[block, :], out.at[block, :], sems.at[index]))
            copies[-1].start()
        for copy in copies:
            copy.wait()


def last_out(where, same, cross, held, weight, partial, kept, residual, gate, fresh):
    span, share = partial.shape
    return pl.pallas_call(
        last_out_kernel,
        out_shape=jax.ShapeDtypeStruct((span, share), jnp.bfloat16),
        in_specs=[smem_spec()] + [vmem_spec()] * 8 + [any_spec()],
        out_specs=any_spec(),
        scratch_shapes=[pltpu.VMEM((span, share), jnp.bfloat16), pltpu.SemaphoreType.DMA((4,))],
        compiler_params=pltpu.CompilerParams(vmem_limit_bytes=8 * MIB),
        cost_estimate=cost(1, 1),
    )(where, same, cross, held, near(weight), near(partial), near(kept), residual, near(gate), far(fresh))


def on_device(hidden, levels, frame_counts, mod_weight, qkv_weight, out_weight, fresh):
    rows, width = hidden.shape
    slot = lax.axis_index("queue")
    queue_len = lax.axis_size("queue")
    member = lax.axis_index("heads")
    members = lax.axis_size("heads")
    share = width // members
    parity, core, y_hi = slot % 2, member % 2, member // 2
    z_half = (slot // 8) % 2
    half = rows // 2
    route = functools.partial(routed, queue_len=queue_len, members=members)
    twin = lambda a: route(a, target=lambda s, y, k: (s, y, 1 - k))

    where = jnp.stack(
        [member, core, y_hi, z_half, parity, (slot == queue_len - 1).astype(jnp.int32), slot]
    ).astype(jnp.int32)
    after = lambda a, *b: lax.optimization_barrier((a, *b))[0]
    frame_counts = frame_counts.astype(jnp.int32)

    twin_weight = twin(qkv_weight)
    mine, far_mine = slices(where, hidden, out_weight, members)
    second = route(mine, target=lambda s, y, k: (s ^ 1, y ^ k, k))

    payload = modulate(where, embed_levels(levels, mod_weight.shape[0]), mod_weight)
    mod_rows = lax.all_to_all(payload, "queue", 0, 0, tiled=True)[:, 0, :]

    first = twin(after(second, mod_rows))
    w_far = route(after(far_mine, mod_rows), target=lambda s, y, k: (s ^ 1, 1 - y, k))
    kv, k, v, normed, q_weight, twin_mine, share_states = keys_values(where, mod_rows, hidden, first, second, qkv_weight, twin_weight, out_weight)

    def remote_target(s, y, k):
        back = (s % 2 == 0) == (k == 0)
        return (s - 2 if back else s + 2, y, 1 - k)

    kv_remote = route(kv, target=remote_target)
    k_twin, v_twin = twin(k), twin(v)
    query = queries(after(normed, kv), q_weight)
    o, m, l = local_attention(where, frame_counts, query, kv, k_twin, v_twin)
    residual = route(
        after(share_states, o),
        target=lambda s, y, k: (s - 1, y, 0) if k == 0 else ((s - 2, y, 1) if s % 2 else None),
    )
    attn = remote_attention(where, frame_counts, query, kv_remote, o, m, l)

    def goal(s, y, k):
        if k == 0:
            return (s - 1, y, 0)
        return (s if s % 2 == 0 else s - 2, y, 1)

    same = route(attn, target=lambda s, y, k: None if s % 2 == 0 and k == 1 else goal(s, y, k))
    cross = route(attn, target=lambda s, y, k: goal(s, 1 - y, k))
    twin_attn = twin(attn)
    w_far_twin = twin(columns_of_twin(after(where, attn), w_far))
    w_twin = twin(after(twin_mine, attn))
    weight, gate = tail_inputs(where, mod_rows, out_weight, w_twin, w_far, w_far_twin)
    same, cross, residual, _ = lax.optimization_barrier((same, cross, residual, weight))
    partial = first_out(where, same, cross, attn, weight)
    return last_out(where, twin(same), twin(cross), twin_attn, weight, partial, share_states, residual, gate, fresh)


def solution(mesh):
    placed = (
        P("queue", None),
        P(),
        P(),
        P(None, "queue"),
        P(None, None, "heads"),
        P("heads", None),
        P(None, "heads"),
    )
    return jax.shard_map(
        on_device, mesh=mesh, in_specs=placed, out_specs=P("queue", "heads"), check_vma=False
    )
```

```python
import functools
import math

import jax
import jax.numpy as jnp
from jax import lax
from jax.experimental import pallas as pl
from jax.experimental.pallas import tpu as pltpu
from jax.sharding import PartitionSpec as P

HD = 64
P_SIZE = 256
PAIR = 2 * HD
NEG = -1e30
BOTH = ("queue", "heads")
MIB = 1024 * 1024


def embed_levels(levels, width):
    halfway = width // 2
    freqs = jnp.exp(-math.log(10000.0) * jnp.arange(halfway, dtype=jnp.float32) / halfway)
    angles = levels.astype(jnp.float32)[:, None] * freqs[None, :]
    return jax.nn.silu(jnp.concatenate([jnp.cos(angles), jnp.sin(angles)], axis=1)).astype(
        jnp.bfloat16
    )


def routed(array, queue_len, members, target):
    pairs = []
    for slot in range(queue_len):
        for member in range(members):
            goal = target(slot, member // 2, member % 2)
            if goal is not None and 0 <= goal[0] < queue_len:
                pairs.append((slot * members + member, goal[0] * members + goal[1] * 2 + goal[2]))
    return lax.ppermute(array, BOTH, pairs)


def low_lanes(shape):
    return lax.broadcasted_iota(jnp.int32, shape, len(shape) - 1) < HD


def copies_of(source, target, sems, chunks, first=0):
    step = source.shape[0] // chunks
    return [
        pltpu.make_async_copy(
            source.at[pl.ds(i * step, step), :], target.at[pl.ds(i * step, step), :], sems.at[first + i]
        )
        for i in range(chunks)
    ]


def place():
    slot, member = lax.axis_index("queue"), lax.axis_index("heads")
    return member, member & 1, member >> 1, slot & 1, slot


def any_spec():
    return pl.BlockSpec(memory_space=pl.ANY)


def far(array):
    return pltpu.with_memory_space_constraint(array, pltpu.HBM)


def near(array):
    return pltpu.with_memory_space_constraint(array, pltpu.VMEM)


def near_out(shape, dtype=jnp.bfloat16):
    return pltpu.VMEM(shape, dtype)


def cost(flops, moved, transcendentals=0):
    return pl.CostEstimate(flops=flops, bytes_accessed=moved, transcendentals=transcendentals)


def vmem_spec():
    return pl.BlockSpec(memory_space=pltpu.VMEM)


def smem_spec():
    return pl.BlockSpec(memory_space=pltpu.SMEM)


def lanes_at(index, size):
    return pl.ds(pl.multiple_of(index * size, size), size)


def slices_kernel(hidden, out_weight, mine, far_out, sems):
    _, core, y_hi, _, _ = place()
    half, width = mine.shape[0], far_out.shape[1]
    copies = (
        copies_of(hidden.at[lanes_at(core, half), :], mine, sems, 4)
        + copies_of(out_weight.at[:, lanes_at(1 - y_hi, width)], far_out, sems, 4, 4)
    )
    for copy in copies:
        copy.start()
    for copy in copies:
        copy.wait()


def slices(hidden, out_weight, members):
    rows, width = hidden.shape
    share, depth = width // members, out_weight.shape[0]
    return pl.pallas_call(
        slices_kernel,
        out_shape=(
            near_out((rows // 2, width)),
            near_out((depth, 2 * share)),
        ),
        in_specs=[any_spec(), any_spec()],
        out_specs=(vmem_spec(),) * 2,
        scratch_shapes=[pltpu.SemaphoreType.DMA((8,))],
        compiler_params=pltpu.CompilerParams(vmem_limit_bytes=2 * MIB),
        cost_estimate=cost(0, 4 * MIB),
    )(far(hidden), far(out_weight))


ROW = 384


def modulate_kernel(emb_ref, mod_ref, payload, rows_ref):
    rows_ref[...] = jnp.zeros_like(rows_ref)
    columns = mod_ref.shape[0]
    rows_ref[:, :columns] = lax.dot_general(
        emb_ref[...], mod_ref[...], (((1,), (1,)), ((), ())), preferred_element_type=jnp.float32
    )
    rows = rows_ref[...]
    slots = rows.shape[0]
    even = lax.broadcasted_iota(jnp.int32, rows.shape, 0) % 2 == 0
    following = pltpu.roll(rows, slots - 1, 0)
    partner = jnp.where(even, following, pltpu.roll(rows, 1, 0))
    joined = jnp.where(place()[1] == 0, rows, partner) + pltpu.roll(following, columns, 1)
    for slot in range(slots):
        payload[slot] = joined[slot : slot + 1, :]


def modulate(emb, mod_weight):
    return pl.pallas_call(
        modulate_kernel,
        out_shape=jax.ShapeDtypeStruct((emb.shape[0], 1, ROW), jnp.float32),
        in_specs=[vmem_spec(), vmem_spec()],
        out_specs=vmem_spec(),
        scratch_shapes=[pltpu.VMEM((emb.shape[0], ROW), jnp.float32)],
        compiler_params=pltpu.CompilerParams(vmem_limit_bytes=2 * MIB),
        cost_estimate=cost(10**7, MIB),
    )(emb, mod_weight.T)


NORM_ROWS = 16


def spread(rows_ref, part, flat):
    slots = rows_ref.shape[0]
    columns = flat.shape[1] // slots
    step = columns - PAIR
    row = lax.broadcasted_iota(jnp.int32, (8, 2 * PAIR), 0)
    at = lax.broadcasted_iota(jnp.int32, (8, 2 * PAIR), 1) - step * row
    held = (at >= 0) & (at < columns)
    first_row = row[:, :PAIR] == 0
    for i in range(slots // 8):
        block = rows_ref[8 * i : 8 * i + 8, :]
        if part:
            block = pltpu.roll(block, ROW - columns * part, 1)
        turned = pltpu.roll(block, 0, 1, stride=step, stride_axis=0)
        turned = jnp.where(held, turned[:, : 2 * PAIR], 0.0)
        carried = turned[:, PAIR:]
        tiles = turned[:, :PAIR] + jnp.where(first_row, 0.0, pltpu.roll(carried, 1, 0))
        base = 8 * i * columns
        for j in range(8):
            flat[:, base + j * PAIR : base + (j + 1) * PAIR] = tiles[j : j + 1, :]
        flat[:, base + 8 * PAIR : base + 9 * PAIR] = carried[7:8, :]


def kv_kernel(
    counts_ref, rows_ref, hidden, first, second, own_weight, twin_weight, out_weight, kv_ref, k_ref, v_ref, states_ref, q_weight,
    twin_out, share_ref, dead_ref,
    flat, weight, x_sems, w_sems,
):
    member, core, y_hi, parity, slot = place()
    rows, width = states_ref.shape
    half = rows // 2
    each = q_weight.shape[1]
    from_own = copies_of(hidden, states_ref, x_sems, 4)
    from_pair = copies_of(first, states_ref.at[pl.ds(0, half), :], x_sems, 2) + copies_of(
        second, states_ref.at[pl.ds(half, half), :], x_sems, 2, 2
    )

    def weights_from(source):
        return [
            copies_of(source.at[kind], target, w_sems, 2, 2 * kind)
            for kind, target in (
                (1, weight.at[:, pl.ds(0, each)]),
                (2, weight.at[:, pl.ds(each, each)]),
                (0, q_weight),
            )
        ]

    def start(condition, copies):
        @pl.when(condition)
        def _():
            for copy in copies:
                copy.start()

    start(core == 0, from_own)
    start(core == 1, from_pair)
    start(core == parity, sum(weights_from(own_weight)[:2], []))
    start(core != parity, sum(weights_from(twin_weight)[:2], []))
    beside = y_hi * 2 + 1 - core
    asides = copies_of(out_weight.at[:, lanes_at(beside, twin_out.shape[1])], twin_out, w_sems, 2, 6)
    spread(rows_ref, 0, flat)
    step = 1 - 2 * parity
    mine = slot + core * step
    for index, stretch in enumerate((mine, slot + (1 - core) * step, jnp.where(core == 0, slot - step, slot + 2 * step))):
        dead_ref[pl.ds(index * rows, rows), :] = dead_rows(rows, count_at(counts_ref, stretch))
    scale, shift = 1.0 + flat[:, width : 2 * width], flat[:, :width]

    def normalise(first_row, count):
        for start in range(first_row, first_row + count, NORM_ROWS):
            block = pl.ds(start, NORM_ROWS)
            states = states_ref[block, :].astype(jnp.float32)
            mean = jnp.mean(states, axis=1, keepdims=True)
            centred = states - mean
            var = jnp.mean(centred * centred, axis=1, keepdims=True)
            states_ref[block, :] = (centred * lax.rsqrt(var + 1e-05) * scale + shift).astype(jnp.bfloat16)

    chunk = rows // len(from_own)
    for index, copy in enumerate(from_own):
        copy.wait()
        block = pl.ds(index * chunk, chunk)
        share_ref[block, :] = states_ref[block, lanes_at(member, share_ref.shape[1])]
        normalise(index * chunk, chunk)
    keys, values, queries = weights_from(own_weight)
    for copy in keys + values:
        copy.wait()
    start(core == parity, weights_from(own_weight)[2])
    start(core != parity, weights_from(twin_weight)[2])
    for copy in asides:
        copy.start()
    kv = jnp.dot(states_ref[...], weight[...], preferred_element_type=jnp.float32).astype(jnp.bfloat16)
    kv_ref[...] = kv
    k_ref[...] = kv[:, :each]
    v_ref[...] = kv[:, each:]
    for copy in queries + asides:
        copy.wait()


def keys_values(counts, mod_rows, hidden, first, second, own_weight, twin_weight, out_weight):
    rows, width = hidden.shape
    each = own_weight.shape[2]
    return pl.pallas_call(
        kv_kernel,
        out_shape=(
            near_out((rows, 2 * each)),
            near_out((rows, each)),
            near_out((rows, each)),
            near_out((rows, width)),
            near_out((width, each)),
            near_out((out_weight.shape[0], width // 4)),
            near_out((rows, width // 4)),
            near_out((3 * rows, PAIR)),
        ),
        in_specs=[smem_spec(), vmem_spec()] + [any_spec()] * 6,
        out_specs=(vmem_spec(),) * 8,
        scratch_shapes=[
            pltpu.VMEM((1, 3 * width), jnp.float32),
            pltpu.VMEM((width, 2 * each), jnp.bfloat16),
            pltpu.SemaphoreType.DMA((4,)),
            pltpu.SemaphoreType.DMA((8,)),
        ],
        compiler_params=pltpu.CompilerParams(vmem_limit_bytes=24 * MIB),
        cost_estimate=cost(1, 1),
    )(counts, mod_rows, far(hidden), first, second, far(own_weight), twin_weight, far(out_weight))


def query_kernel(normed, weight, query_ref):
    query = jnp.dot(normed[...], weight[...], preferred_element_type=jnp.float32).astype(jnp.bfloat16)
    query_ref[...] = (query * HD ** (-0.5)).astype(jnp.bfloat16)


def queries(normed, weight):
    return pl.pallas_call(
        query_kernel,
        out_shape=near_out((normed.shape[0], weight.shape[1])),
        in_specs=[vmem_spec()] * 2,
        out_specs=vmem_spec(),
        compiler_params=pltpu.CompilerParams(vmem_limit_bytes=4 * MIB),
        cost_estimate=cost(1, 1),
    )(near(normed), near(weight))


def count_at(counts_ref, at):
    inside = (at >= 0) & (at < counts_ref.shape[0])
    return jnp.where(inside, counts_ref[jnp.where(inside, at, 0)], 0)


LOG2E = math.log2(math.e)


def scores_of(query, keys):
    return lax.dot_general(query, keys, (((1,), (1,)), ((), ())), preferred_element_type=jnp.float32)


def dead_rows(span, count):
    row = lax.broadcasted_iota(jnp.int32, (span, PAIR), 0)
    return jnp.where(row < count * P_SIZE, 0.0, NEG).astype(jnp.bfloat16)


def two_heads(keys, values, dead):
    low = low_lanes(keys.shape)
    lane = lax.broadcasted_iota(jnp.int32, keys.shape, 1)
    zero, one = jnp.zeros_like(keys), jnp.ones_like(values)
    return (
        (jnp.where(low, keys, jnp.where(lane == HD, dead, zero)), jnp.where(low, values, one)),
        (jnp.where(low, jnp.where(lane == 0, dead, zero), keys), jnp.where(low, one, values)),
    )


def two_queries(query):
    low = low_lanes(query.shape)
    lane = lax.broadcasted_iota(jnp.int32, query.shape, 1)
    zero, one = jnp.zeros_like(query), jnp.ones_like(query)
    return (
        jnp.where(low, query, jnp.where(lane == HD, one, zero)),
        jnp.where(low, jnp.where(lane == 0, one, zero), query),
    )


def attend(query_of, pairs, blocks, before_of, finish):
    units = [(pair, rows) for pair in range(len(pairs)) for rows in blocks]

    def scores(unit):
        pair, rows = unit
        return [scores_of(q, keys) for q, (keys, _) in zip(two_queries(query_of(pair, rows)), pairs[pair])]

    following = scores(units[0])
    for index, (pair, rows) in enumerate(units):
        current = following
        if index + 1 < len(units):
            following = scores(units[index + 1])
        peaks, numers = [], []
        for head in range(2):
            peak = jnp.max(current[head], axis=1, keepdims=True)
            before = before_of(pair, rows, head)
            peak = peak if before is None else jnp.maximum(peak, before)
            probs = jnp.exp2((current[head] - peak) * LOG2E).astype(jnp.bfloat16)
            peaks.append(peak)
            numers.append(jnp.dot(probs, pairs[pair][head][1], preferred_element_type=jnp.float32))
        low = low_lanes(numers[0].shape)
        total = pltpu.roll(jnp.where(low, numers[1], numers[0]), HD, 1)
        finish(pair, rows, jnp.where(low, *numers), jnp.where(low, *peaks), total)


def pair_lanes(pair):
    return slice(pair * PAIR, (pair + 1) * PAIR)


def local_kernel(dead_ref, q_ref, own_ref, k_twin, v_twin, o_ref, m_ref, l_ref):
    span = own_ref.shape[0]
    tile = 256
    dead = dead_ref[: 2 * span, :]
    pairs = [
        two_heads(
            jnp.concatenate([own_ref[:, pair_lanes(pair)], k_twin[:, pair_lanes(pair)]], axis=0),
            jnp.concatenate([own_ref[:, pair_lanes(3 + pair)], v_twin[:, pair_lanes(pair)]], axis=0),
            dead,
        )
        for pair in range(3)
    ]

    def finish(pair, rows, numer, peak, total):
        o_ref[rows, pair_lanes(pair)] = numer
        m_ref[rows, pair_lanes(pair)] = peak
        l_ref[rows, pair_lanes(pair)] = total

    attend(
        lambda pair, rows: q_ref[rows, pair_lanes(pair)],
        pairs,
        [pl.ds(start, tile) for start in range(0, span, tile)],
        lambda pair, rows, head: None,
        finish,
    )


def local_attention(dead, query, own, k_twin, v_twin):
    span = query.shape[0]
    part = near_out((span, 3 * PAIR), jnp.float32)
    return pl.pallas_call(
        local_kernel,
        out_shape=(part,) * 3,
        in_specs=[vmem_spec()] * 5,
        out_specs=(vmem_spec(),) * 3,
        compiler_params=pltpu.CompilerParams(vmem_limit_bytes=16 * MIB),
        cost_estimate=cost(1, 1),
    )(near(dead), near(query), near(own), k_twin, v_twin)


def remote_kernel(dead_ref, q_ref, kv_ref, o_ref, m_ref, l_ref, piece_ref):
    span = kv_ref.shape[0]
    tile = 256
    dead = dead_ref[2 * span :, :]
    pairs = [
        two_heads(kv_ref[:, pair_lanes(pair)], kv_ref[:, pair_lanes(3 + pair)], dead) for pair in range(3)
    ]

    def before(pair, rows, head):
        at = pair * PAIR + head * HD
        return m_ref[rows, at : at + 1]

    def finish(pair, rows, numer, peak, total):
        lanes = pair_lanes(pair)
        fade = jnp.exp2((m_ref[rows, lanes] - peak) * LOG2E)
        attn = (numer + fade * o_ref[rows, lanes]) / (total + fade * l_ref[rows, lanes])
        piece_ref[rows, lanes] = attn.astype(jnp.bfloat16)

    attend(
        lambda pair, rows: q_ref[rows, pair_lanes(pair)],
        pairs,
        [pl.ds(start, tile) for start in range(0, span, tile)],
        before,
        finish,
    )


def remote_attention(dead, query, kv, o, m, l):
    span = query.shape[0]
    return pl.pallas_call(
        remote_kernel,
        out_shape=near_out((span, 3 * PAIR)),
        in_specs=[vmem_spec()] * 6,
        out_specs=vmem_spec(),
        compiler_params=pltpu.CompilerParams(vmem_limit_bytes=16 * MIB),
        cost_estimate=cost(1, 1),
    )(near(dead), near(query), kv, near(o), near(m), near(l))


def tail_kernel(
    rows_ref, out_weight, w_twin, w_far, w_far_twin, gathered, gate, flat, sems,
):
    member, core, _, parity, _ = place()
    share = gathered.shape[1]
    width = flat.shape[1] // 3
    block = out_weight.shape[0]
    local = jnp.where(core == 0, 1 - parity, parity)
    whole, mine, own = pl.ds(0, share), lanes_at(core, share), lanes_at(member, share)
    copies = []
    for source, lanes, far_half, y_lo in (
        (out_weight, own, 0, core),
        (w_twin, whole, 0, 1 - core),
        (w_far, mine, 1, core),
        (w_far_twin, whole, 1, 1 - core),
    ):
        base = jnp.where(local == y_lo, 0, 2 * block) + far_half * block
        to = pl.ds(pl.multiple_of(base, block), block)
        copies += copies_of(source.at[:, lanes], gathered.at[to, :], sems, 2, len(copies))
    for copy in copies:
        copy.start()
    spread(rows_ref, 1, flat)
    gate[...] = flat[:, pl.ds(pl.multiple_of(2 * width + member * share, PAIR), share)]
    for copy in copies:
        copy.wait()


def columns_kernel(source, out, sems):
    copies = copies_of(source.at[:, lanes_at(1 - place()[1], out.shape[1])], out, sems, 4)
    for copy in copies:
        copy.start()
    for copy in copies:
        copy.wait()


def columns_of_twin(blocks):
    rows, width = blocks.shape
    return pl.pallas_call(
        columns_kernel,
        out_shape=near_out((rows, width // 2)),
        in_specs=[any_spec()],
        out_specs=vmem_spec(),
        scratch_shapes=[pltpu.SemaphoreType.DMA((4,))],
        compiler_params=pltpu.CompilerParams(vmem_limit_bytes=2 * MIB),
        cost_estimate=cost(1, 1),
    )(blocks)


def tail_inputs(mod_rows, out_weight, w_twin, w_far, w_far_twin):
    block, share = w_twin.shape
    width = out_weight.shape[1]
    return pl.pallas_call(
        tail_kernel,
        out_shape=(near_out((4 * block, share)), near_out((1, share), jnp.float32)),
        in_specs=[vmem_spec()] + [any_spec()] * 4,
        out_specs=(vmem_spec(),) * 2,
        scratch_shapes=[pltpu.VMEM((1, 3 * width), jnp.float32), pltpu.SemaphoreType.DMA((8,))],
        compiler_params=pltpu.CompilerParams(vmem_limit_bytes=2 * MIB),
        cost_estimate=cost(1, 1),
    )(mod_rows, far(out_weight), w_twin, w_far, w_far_twin)


def first_out_kernel(same, cross, held, weight, partial):
    _, core, _, parity, _ = place()
    here = (parity == 0) & (core == 1)
    attn = jnp.concatenate([jnp.where(here, held[...], same[...]), cross[...]], axis=1)
    partial[...] = jnp.dot(attn, weight[: attn.shape[1], :], preferred_element_type=jnp.float32)


def first_out(same, cross, held, weight):
    span, share = same.shape[0], weight.shape[1]
    return pl.pallas_call(
        first_out_kernel,
        out_shape=near_out((span, share), jnp.float32),
        in_specs=[vmem_spec()] * 4,
        out_specs=vmem_spec(),
        compiler_params=pltpu.CompilerParams(vmem_limit_bytes=8 * MIB),
        cost_estimate=cost(1, 1),
    )(same, cross, near(held), near(weight))


TILE = 128


def last_out_kernel(
    same, cross, held, weight, partial, kept, residual, gate, fresh, out, ready, sems
):
    _, core, _, parity, slot = place()
    here = (parity == 0) & (core == 0)
    holds = (parity == 0) & (core == 1)
    last = slot == lax.axis_size("queue") - 1
    span = partial.shape[0]
    tiles = span // TILE

    @pl.when(last)
    def _():
        for source, target in ((fresh, ready), (ready, out)):
            copies = copies_of(source, target, sems, tiles)
            for copy in copies:
                copy.start()
            for copy in copies:
                copy.wait()

    @pl.when(jnp.logical_not(last))
    def _():
        copies = []
        for index, first_row in enumerate(range(0, span, TILE)):
            rows = slice(first_row, first_row + TILE)
            attn = jnp.concatenate([jnp.where(here, held[rows, :], same[rows, :]), cross[rows, :]], axis=1)
            summed = partial[rows, :] + jnp.dot(
                attn, weight[attn.shape[1] :, :], preferred_element_type=jnp.float32
            )
            states = jnp.where(holds, kept[rows, :], residual[rows, :])
            ready[rows, :] = (states.astype(jnp.float32) + gate[...] * summed).astype(jnp.bfloat16)
            block = pl.ds(first_row, TILE)
            copies.append(pltpu.make_async_copy(ready.at[block, :], out.at[block, :], sems.at[index]))
            copies[-1].start()
        for copy in copies:
            copy.wait()


def last_out(same, cross, held, weight, partial, kept, residual, gate, fresh):
    span, share = partial.shape
    return pl.pallas_call(
        last_out_kernel,
        out_shape=jax.ShapeDtypeStruct((span, share), jnp.bfloat16),
        in_specs=[vmem_spec()] * 8 + [any_spec()],
        out_specs=any_spec(),
        scratch_shapes=[pltpu.VMEM((span, share), jnp.bfloat16), pltpu.SemaphoreType.DMA((4,))],
        compiler_params=pltpu.CompilerParams(vmem_limit_bytes=8 * MIB),
        cost_estimate=cost(1, 1),
    )(same, cross, held, near(weight), near(partial), near(kept), residual, near(gate), far(fresh))


def on_device(hidden, levels, frame_counts, mod_weight, qkv_weight, out_weight, fresh):
    queue_len = lax.axis_size("queue")
    members = lax.axis_size("heads")
    route = functools.partial(routed, queue_len=queue_len, members=members)
    twin = lambda a: route(a, target=lambda s, y, k: (s, y, 1 - k))

    after = lambda a, *b: lax.optimization_barrier((a, *b))[0]
    frame_counts = frame_counts.astype(jnp.int32)

    twin_weight = twin(qkv_weight)
    mine, far_mine = slices(hidden, out_weight, members)
    second = route(mine, target=lambda s, y, k: (s ^ 1, y ^ k, k))

    payload = modulate(embed_levels(levels, mod_weight.shape[0]), mod_weight)
    mod_rows = lax.all_to_all(payload, "queue", 0, 0, tiled=True)[:, 0, :]

    first = twin(after(second, mod_rows))
    w_far = route(after(far_mine, mod_rows), target=lambda s, y, k: (s ^ 1, 1 - y, k))
    kv, k, v, normed, q_weight, twin_mine, share_states, dead = keys_values(frame_counts, mod_rows, hidden, first, second, qkv_weight, twin_weight, out_weight)

    def remote_target(s, y, k):
        back = (s % 2 == 0) == (k == 0)
        return (s - 2 if back else s + 2, y, 1 - k)

    kv_remote = route(kv, target=remote_target)
    k_twin, v_twin = twin(k), twin(v)
    query = queries(after(normed, kv), q_weight)
    o, m, l = local_attention(dead, query, kv, k_twin, v_twin)
    residual = route(
        after(share_states, o),
        target=lambda s, y, k: (s - 1, y, 0) if k == 0 else ((s - 2, y, 1) if s % 2 else None),
    )
    attn = remote_attention(dead, query, kv_remote, o, m, l)

    def goal(s, y, k):
        if k == 0:
            return (s - 1, y, 0)
        return (s if s % 2 == 0 else s - 2, y, 1)

    same = route(attn, target=lambda s, y, k: None if s % 2 == 0 and k == 1 else goal(s, y, k))
    cross = route(attn, target=lambda s, y, k: goal(s, 1 - y, k))
    twin_attn = twin(attn)
    w_far_twin = twin(columns_of_twin(after(w_far, attn)))
    w_twin = twin(after(twin_mine, attn))
    weight, gate = tail_inputs(mod_rows, out_weight, w_twin, w_far, w_far_twin)
    same, cross, residual, _ = lax.optimization_barrier((same, cross, residual, weight))
    partial = first_out(same, cross, attn, weight)
    return last_out(twin(same), twin(cross), twin_attn, weight, partial, share_states, residual, gate, fresh)


def solution(mesh):
    placed = (
        P("queue", None),
        P(),
        P(),
        P(None, "queue"),
        P(None, None, "heads"),
        P("heads", None),
        P(None, "heads"),
    )
    return jax.shard_map(
        on_device, mesh=mesh, in_specs=placed, out_specs=P("queue", "heads"), check_vma=False
    )
```

```python
import functools
import math

import jax
import jax.numpy as jnp
from jax import lax
from jax.experimental import pallas as pl
from jax.experimental.pallas import tpu as pltpu
from jax.sharding import PartitionSpec as P

HD = 64
P_SIZE = 256
PAIR = 2 * HD
NEG = -1e30
BOTH = ("queue", "heads")
MIB = 1024 * 1024


def embed_levels(levels, width):
    halfway = width // 2
    freqs = jnp.exp(-math.log(10000.0) * jnp.arange(halfway, dtype=jnp.float32) / halfway)
    angles = levels.astype(jnp.float32)[:, None] * freqs[None, :]
    return jax.nn.silu(jnp.concatenate([jnp.cos(angles), jnp.sin(angles)], axis=1)).astype(
        jnp.bfloat16
    )


def routed(array, queue_len, members, target):
    pairs = []
    for slot in range(queue_len):
        for member in range(members):
            goal = target(slot, member // 2, member % 2)
            if goal is not None and 0 <= goal[0] < queue_len:
                pairs.append((slot * members + member, goal[0] * members + goal[1] * 2 + goal[2]))
    return lax.ppermute(array, BOTH, pairs)


def low_lanes(shape):
    return lax.broadcasted_iota(jnp.int32, shape, len(shape) - 1) < HD


def copies_of(source, target, sems, chunks, first=0):
    step = source.shape[0] // chunks
    return [
        pltpu.make_async_copy(
            source.at[pl.ds(i * step, step), :], target.at[pl.ds(i * step, step), :], sems.at[first + i]
        )
        for i in range(chunks)
    ]


def place():
    slot, member = lax.axis_index("queue"), lax.axis_index("heads")
    return member, member & 1, member >> 1, slot & 1, slot


def any_spec():
    return pl.BlockSpec(memory_space=pl.ANY)


def far(array):
    return pltpu.with_memory_space_constraint(array, pltpu.HBM)


def near(array):
    return pltpu.with_memory_space_constraint(array, pltpu.VMEM)


def near_out(shape, dtype=jnp.bfloat16):
    return pltpu.VMEM(shape, dtype)


def cost(flops, moved, transcendentals=0):
    return pl.CostEstimate(flops=flops, bytes_accessed=moved, transcendentals=transcendentals)


def vmem_spec():
    return pl.BlockSpec(memory_space=pltpu.VMEM)


def smem_spec():
    return pl.BlockSpec(memory_space=pltpu.SMEM)


def lanes_at(index, size):
    return pl.ds(pl.multiple_of(index * size, size), size)


def slices_kernel(hidden, out_weight, mine, far_out, sems):
    _, core, y_hi, _, _ = place()
    half, width = mine.shape[0], far_out.shape[1]
    copies = (
        copies_of(hidden.at[lanes_at(core, half), :], mine, sems, 4)
        + copies_of(out_weight.at[:, lanes_at(1 - y_hi, width)], far_out, sems, 4, 4)
    )
    for copy in copies:
        copy.start()
    for copy in copies:
        copy.wait()


def slices(hidden, out_weight, members):
    rows, width = hidden.shape
    share, depth = width // members, out_weight.shape[0]
    return pl.pallas_call(
        slices_kernel,
        out_shape=(
            near_out((rows // 2, width)),
            near_out((depth, 2 * share)),
        ),
        in_specs=[any_spec(), any_spec()],
        out_specs=(vmem_spec(),) * 2,
        scratch_shapes=[pltpu.SemaphoreType.DMA((8,))],
        compiler_params=pltpu.CompilerParams(vmem_limit_bytes=2 * MIB),
        cost_estimate=cost(0, 4 * MIB),
    )(far(hidden), far(out_weight))


ROW = 384


def modulate_kernel(emb_ref, mod_ref, payload, rows_ref):
    rows_ref[...] = jnp.zeros_like(rows_ref)
    columns = mod_ref.shape[0]
    rows_ref[:, :columns] = lax.dot_general(
        emb_ref[...], mod_ref[...], (((1,), (1,)), ((), ())), preferred_element_type=jnp.float32
    )
    rows = rows_ref[...]
    slots = rows.shape[0]
    even = lax.broadcasted_iota(jnp.int32, rows.shape, 0) % 2 == 0
    following = pltpu.roll(rows, slots - 1, 0)
    partner = jnp.where(even, following, pltpu.roll(rows, 1, 0))
    joined = jnp.where(place()[1] == 0, rows, partner) + pltpu.roll(following, columns, 1)
    for slot in range(slots):
        payload[slot] = joined[slot : slot + 1, :]


def modulate(emb, mod_weight):
    return pl.pallas_call(
        modulate_kernel,
        out_shape=jax.ShapeDtypeStruct((emb.shape[0], 1, ROW), jnp.float32),
        in_specs=[vmem_spec(), vmem_spec()],
        out_specs=vmem_spec(),
        scratch_shapes=[pltpu.VMEM((emb.shape[0], ROW), jnp.float32)],
        compiler_params=pltpu.CompilerParams(vmem_limit_bytes=2 * MIB),
        cost_estimate=cost(10**7, MIB),
    )(emb, mod_weight.T)


NORM_ROWS = 16


def spread(rows_ref, part, flat):
    slots = rows_ref.shape[0]
    columns = flat.shape[1] // slots
    step = columns - PAIR
    row = lax.broadcasted_iota(jnp.int32, (8, 2 * PAIR), 0)
    at = lax.broadcasted_iota(jnp.int32, (8, 2 * PAIR), 1) - step * row
    held = (at >= 0) & (at < columns)
    first_row = row[:, :PAIR] == 0
    for i in range(slots // 8):
        block = rows_ref[8 * i : 8 * i + 8, :]
        if part:
            block = pltpu.roll(block, ROW - columns * part, 1)
        turned = pltpu.roll(block, 0, 1, stride=step, stride_axis=0)
        turned = jnp.where(held, turned[:, : 2 * PAIR], 0.0)
        carried = turned[:, PAIR:]
        tiles = turned[:, :PAIR] + jnp.where(first_row, 0.0, pltpu.roll(carried, 1, 0))
        base = 8 * i * columns
        for j in range(8):
            flat[:, base + j * PAIR : base + (j + 1) * PAIR] = tiles[j : j + 1, :]
        flat[:, base + 8 * PAIR : base + 9 * PAIR] = carried[7:8, :]


def kv_kernel(
    rows_ref, hidden, first, second, own_weight, twin_weight, out_weight, kv_ref, k_ref, v_ref, states_ref, q_weight,
    twin_a, twin_b, share_ref,
    flat, weight, x_sems, w_sems,
):
    member, core, y_hi, parity, _ = place()
    rows, width = states_ref.shape
    half = rows // 2
    each = q_weight.shape[1]
    from_own = copies_of(hidden, states_ref, x_sems, 4)
    from_pair = copies_of(first, states_ref.at[pl.ds(0, half), :], x_sems, 2) + copies_of(
        second, states_ref.at[pl.ds(half, half), :], x_sems, 2, 2
    )

    def weights_from(source):
        return [
            copies_of(source.at[kind], target, w_sems, 2, 2 * kind)
            for kind, target in (
                (1, weight.at[:, pl.ds(0, each)]),
                (2, weight.at[:, pl.ds(each, each)]),
                (0, q_weight),
            )
        ]

    def start(condition, copies):
        @pl.when(condition)
        def _():
            for copy in copies:
                copy.start()

    start(core == 0, from_own)
    start(core == 1, from_pair)
    start(core == parity, sum(weights_from(own_weight)[:2], []))
    start(core != parity, sum(weights_from(twin_weight)[:2], []))
    beside = y_hi * 2 + 1 - core
    asides = sum(
        (
            copies_of(
                out_weight.at[lanes_at(index, out.shape[0]), lanes_at(beside, out.shape[1])], out, w_sems, 1, 6 + index
            )
            for index, out in enumerate((twin_a, twin_b))
        ),
        [],
    )
    spread(rows_ref, 0, flat)
    scale, shift = 1.0 + flat[:, width : 2 * width], flat[:, :width]

    def normalise(first_row, count):
        for start in range(first_row, first_row + count, NORM_ROWS):
            block = pl.ds(start, NORM_ROWS)
            states = states_ref[block, :].astype(jnp.float32)
            mean = jnp.mean(states, axis=1, keepdims=True)
            centred = states - mean
            var = jnp.mean(centred * centred, axis=1, keepdims=True)
            states_ref[block, :] = (centred * lax.rsqrt(var + 1e-05) * scale + shift).astype(jnp.bfloat16)

    chunk = rows // len(from_own)
    for index, copy in enumerate(from_own):
        copy.wait()
        block = pl.ds(index * chunk, chunk)
        share_ref[block, :] = states_ref[block, lanes_at(member, share_ref.shape[1])]
        normalise(index * chunk, chunk)
    keys, values, queries = weights_from(own_weight)
    for copy in keys + values:
        copy.wait()
    start(core == parity, weights_from(own_weight)[2])
    start(core != parity, weights_from(twin_weight)[2])
    for copy in asides:
        copy.start()
    kv = jnp.dot(states_ref[...], weight[...], preferred_element_type=jnp.float32).astype(jnp.bfloat16)
    kv_ref[...] = kv
    k_ref[...] = kv[:, :each]
    v_ref[...] = kv[:, each:]
    for copy in queries + asides:
        copy.wait()


def keys_values(mod_rows, hidden, first, second, own_weight, twin_weight, out_weight):
    rows, width = hidden.shape
    each = own_weight.shape[2]
    return pl.pallas_call(
        kv_kernel,
        out_shape=(
            near_out((rows, 2 * each)),
            near_out((rows, each)),
            near_out((rows, each)),
            near_out((rows, width)),
            near_out((width, each)),
            near_out((out_weight.shape[0] // 2, width // 4)),
            near_out((out_weight.shape[0] // 2, width // 4)),
            near_out((rows, width // 4)),
        ),
        in_specs=[vmem_spec()] + [any_spec()] * 6,
        out_specs=(vmem_spec(),) * 8,
        scratch_shapes=[
            pltpu.VMEM((1, 3 * width), jnp.float32),
            pltpu.VMEM((width, 2 * each), jnp.bfloat16),
            pltpu.SemaphoreType.DMA((4,)),
            pltpu.SemaphoreType.DMA((8,)),
        ],
        compiler_params=pltpu.CompilerParams(vmem_limit_bytes=24 * MIB),
        cost_estimate=cost(1, 1),
    )(mod_rows, far(hidden), first, second, far(own_weight), twin_weight, far(out_weight))


def query_kernel(normed, weight, query_ref):
    query = jnp.dot(normed[...], weight[...], preferred_element_type=jnp.float32).astype(jnp.bfloat16)
    query_ref[...] = (query * HD ** (-0.5)).astype(jnp.bfloat16)


def queries(normed, weight):
    return pl.pallas_call(
        query_kernel,
        out_shape=near_out((normed.shape[0], weight.shape[1])),
        in_specs=[vmem_spec()] * 2,
        out_specs=vmem_spec(),
        compiler_params=pltpu.CompilerParams(vmem_limit_bytes=4 * MIB),
        cost_estimate=cost(1, 1),
    )(near(normed), near(weight))


def count_at(counts_ref, at):
    inside = (at >= 0) & (at < counts_ref.shape[0])
    return jnp.where(inside, counts_ref[jnp.where(inside, at, 0)], 0)


LOG2E = math.log2(math.e)


def scores_of(query, keys):
    return lax.dot_general(query, keys, (((1,), (1,)), ((), ())), preferred_element_type=jnp.float32)


def dead_rows(span, count):
    row = lax.broadcasted_iota(jnp.int32, (span, PAIR), 0)
    return jnp.where(row < count * P_SIZE, 0.0, NEG).astype(jnp.bfloat16)


def two_heads(keys, values, dead):
    low = low_lanes(keys.shape)
    lane = lax.broadcasted_iota(jnp.int32, keys.shape, 1)
    zero, one = jnp.zeros_like(keys), jnp.ones_like(values)
    return (
        (jnp.where(low, keys, jnp.where(lane == HD, dead, zero)), jnp.where(low, values, one)),
        (jnp.where(low, jnp.where(lane == 0, dead, zero), keys), jnp.where(low, one, values)),
    )


def two_queries(query):
    low = low_lanes(query.shape)
    lane = lax.broadcasted_iota(jnp.int32, query.shape, 1)
    zero, one = jnp.zeros_like(query), jnp.ones_like(query)
    return (
        jnp.where(low, query, jnp.where(lane == HD, one, zero)),
        jnp.where(low, jnp.where(lane == 0, one, zero), query),
    )


def attend(query_of, pairs, blocks, before_of, finish):
    units = [(pair, rows) for pair in range(len(pairs)) for rows in blocks]

    def scores(unit):
        pair, rows = unit
        return [scores_of(q, keys) for q, (keys, _) in zip(two_queries(query_of(pair, rows)), pairs[pair])]

    following = scores(units[0])
    for index, (pair, rows) in enumerate(units):
        current = following
        if index + 1 < len(units):
            following = scores(units[index + 1])
        peaks, numers = [], []
        for head in range(2):
            peak = jnp.max(current[head], axis=1, keepdims=True)
            before = before_of(pair, rows, head)
            peak = peak if before is None else jnp.maximum(peak, before)
            probs = jnp.exp2((current[head] - peak) * LOG2E).astype(jnp.bfloat16)
            peaks.append(peak)
            numers.append(jnp.dot(probs, pairs[pair][head][1], preferred_element_type=jnp.float32))
        low = low_lanes(numers[0].shape)
        total = pltpu.roll(jnp.where(low, numers[1], numers[0]), HD, 1)
        finish(pair, rows, jnp.where(low, *numers), jnp.where(low, *peaks), total)


def pair_lanes(pair):
    return slice(pair * PAIR, (pair + 1) * PAIR)


def masks_kernel(counts_ref, dead_ref):
    _, core, _, parity, slot = place()
    rows = dead_ref.shape[0] // 3
    step = 1 - 2 * parity
    stretches = (slot + core * step, slot + (1 - core) * step, jnp.where(core == 0, slot - step, slot + 2 * step))
    for index, stretch in enumerate(stretches):
        dead_ref[index * rows : (index + 1) * rows, :] = dead_rows(rows, count_at(counts_ref, stretch))


def masks(counts, rows):
    return pl.pallas_call(
        masks_kernel,
        out_shape=near_out((3 * rows, PAIR)),
        in_specs=[smem_spec()],
        out_specs=vmem_spec(),
        compiler_params=pltpu.CompilerParams(vmem_limit_bytes=2 * MIB),
        cost_estimate=cost(1, 1),
    )(counts)


def local_kernel(dead_ref, q_ref, own_ref, k_twin, v_twin, o_ref, m_ref, l_ref):
    span = own_ref.shape[0]
    tile = 256
    dead = dead_ref[: 2 * span, :]
    pairs = [
        two_heads(
            jnp.concatenate([own_ref[:, pair_lanes(pair)], k_twin[:, pair_lanes(pair)]], axis=0),
            jnp.concatenate([own_ref[:, pair_lanes(3 + pair)], v_twin[:, pair_lanes(pair)]], axis=0),
            dead,
        )
        for pair in range(3)
    ]

    def finish(pair, rows, numer, peak, total):
        o_ref[rows, pair_lanes(pair)] = numer
        m_ref[rows, pair_lanes(pair)] = peak
        l_ref[rows, pair_lanes(pair)] = total

    attend(
        lambda pair, rows: q_ref[rows, pair_lanes(pair)],
        pairs,
        [pl.ds(start, tile) for start in range(0, span, tile)],
        lambda pair, rows, head: None,
        finish,
    )


def local_attention(dead, query, own, k_twin, v_twin):
    span = query.shape[0]
    part = near_out((span, 3 * PAIR), jnp.float32)
    return pl.pallas_call(
        local_kernel,
        out_shape=(part,) * 3,
        in_specs=[vmem_spec()] * 5,
        out_specs=(vmem_spec(),) * 3,
        compiler_params=pltpu.CompilerParams(vmem_limit_bytes=16 * MIB),
        cost_estimate=cost(1, 1),
    )(near(dead), near(query), near(own), k_twin, v_twin)


def remote_kernel(dead_ref, q_ref, kv_ref, o_ref, m_ref, l_ref, piece_ref):
    span = kv_ref.shape[0]
    tile = 256
    dead = dead_ref[2 * span :, :]
    pairs = [
        two_heads(kv_ref[:, pair_lanes(pair)], kv_ref[:, pair_lanes(3 + pair)], dead) for pair in range(3)
    ]

    def before(pair, rows, head):
        at = pair * PAIR + head * HD
        return m_ref[rows, at : at + 1]

    def finish(pair, rows, numer, peak, total):
        lanes = pair_lanes(pair)
        fade = jnp.exp2((m_ref[rows, lanes] - peak) * LOG2E)
        attn = (numer + fade * o_ref[rows, lanes]) / (total + fade * l_ref[rows, lanes])
        piece_ref[rows, lanes] = attn.astype(jnp.bfloat16)

    attend(
        lambda pair, rows: q_ref[rows, pair_lanes(pair)],
        pairs,
        [pl.ds(start, tile) for start in range(0, span, tile)],
        before,
        finish,
    )


def remote_attention(dead, query, kv, o, m, l):
    span = query.shape[0]
    return pl.pallas_call(
        remote_kernel,
        out_shape=near_out((span, 3 * PAIR)),
        in_specs=[vmem_spec()] * 6,
        out_specs=vmem_spec(),
        compiler_params=pltpu.CompilerParams(vmem_limit_bytes=16 * MIB),
        cost_estimate=cost(1, 1),
    )(near(dead), near(query), kv, near(o), near(m), near(l))


def tail_kernel(
    rows_ref, out_weight, w_far, twin_a, twin_b, far_a, far_b, gathered, gate, flat, sems,
):
    member, core, _, parity, _ = place()
    share = gathered.shape[1]
    width = flat.shape[1] // 3
    block = out_weight.shape[0]
    local = jnp.where(core == 0, 1 - parity, parity)
    whole, mine, own = pl.ds(0, share), lanes_at(core, share), lanes_at(member, share)
    copies = []
    for sources, lanes, far_half, y_lo in (
        ((out_weight,), own, 0, core),
        ((twin_a, twin_b), whole, 0, 1 - core),
        ((w_far,), mine, 1, core),
        ((far_a, far_b), whole, 1, 1 - core),
    ):
        base = jnp.where(local == y_lo, 0, 2 * block) + far_half * block
        each = block // len(sources)
        for index, source in enumerate(sources):
            to = pl.ds(pl.multiple_of(base + index * each, each), each)
            copies += copies_of(source.at[:, lanes], gathered.at[to, :], sems, 2 // len(sources), len(copies))
    for copy in copies:
        copy.start()
    spread(rows_ref, 1, flat)
    gate[...] = flat[:, pl.ds(pl.multiple_of(2 * width + member * share, PAIR), share)]
    for copy in copies:
        copy.wait()


def columns_kernel(source, first, second, sems):
    half, width = first.shape
    copies = []
    for index, out in enumerate((first, second)):
        copies += copies_of(source.at[pl.ds(index * half, half), lanes_at(1 - place()[1], width)], out, sems, 2, 2 * index)
    for copy in copies:
        copy.start()
    for copy in copies:
        copy.wait()


def columns_of_twin(blocks):
    rows, width = blocks.shape
    return pl.pallas_call(
        columns_kernel,
        out_shape=(near_out((rows // 2, width // 2)),) * 2,
        in_specs=[any_spec()],
        out_specs=(vmem_spec(),) * 2,
        scratch_shapes=[pltpu.SemaphoreType.DMA((4,))],
        compiler_params=pltpu.CompilerParams(vmem_limit_bytes=2 * MIB),
        cost_estimate=cost(1, 1),
    )(blocks)


def tail_inputs(mod_rows, out_weight, w_far, twin_a, twin_b, far_a, far_b):
    block, width = out_weight.shape
    share = twin_a.shape[1]
    return pl.pallas_call(
        tail_kernel,
        out_shape=(near_out((4 * block, share)), near_out((1, share), jnp.float32)),
        in_specs=[vmem_spec()] + [any_spec()] * 6,
        out_specs=(vmem_spec(),) * 2,
        scratch_shapes=[pltpu.VMEM((1, 3 * width), jnp.float32), pltpu.SemaphoreType.DMA((8,))],
        compiler_params=pltpu.CompilerParams(vmem_limit_bytes=2 * MIB),
        cost_estimate=cost(1, 1),
    )(mod_rows, far(out_weight), w_far, twin_a, twin_b, far_a, far_b)


def first_out_kernel(same, cross, held, weight, partial):
    _, core, _, parity, _ = place()
    here = (parity == 0) & (core == 1)
    attn = jnp.concatenate([jnp.where(here, held[...], same[...]), cross[...]], axis=1)
    partial[...] = jnp.dot(attn, weight[: attn.shape[1], :], preferred_element_type=jnp.float32)


def first_out(same, cross, held, weight):
    span, share = same.shape[0], weight.shape[1]
    return pl.pallas_call(
        first_out_kernel,
        out_shape=near_out((span, share), jnp.float32),
        in_specs=[vmem_spec()] * 4,
        out_specs=vmem_spec(),
        compiler_params=pltpu.CompilerParams(vmem_limit_bytes=8 * MIB),
        cost_estimate=cost(1, 1),
    )(same, cross, near(held), near(weight))


TILE = 128


def last_out_kernel(
    same, cross, held, weight, partial, kept, residual, gate, fresh, out, ready, sems
):
    _, core, _, parity, slot = place()
    here = (parity == 0) & (core == 0)
    holds = (parity == 0) & (core == 1)
    last = slot == lax.axis_size("queue") - 1
    span = partial.shape[0]
    tiles = span // TILE

    @pl.when(last)
    def _():
        for source, target in ((fresh, ready), (ready, out)):
            copies = copies_of(source, target, sems, tiles)
            for copy in copies:
                copy.start()
            for copy in copies:
                copy.wait()

    @pl.when(jnp.logical_not(last))
    def _():
        copies = []
        for index, first_row in enumerate(range(0, span, TILE)):
            rows = slice(first_row, first_row + TILE)
            attn = jnp.concatenate([jnp.where(here, held[rows, :], same[rows, :]), cross[rows, :]], axis=1)
            summed = partial[rows, :] + jnp.dot(
                attn, weight[attn.shape[1] :, :], preferred_element_type=jnp.float32
            )
            states = jnp.where(holds, kept[rows, :], residual[rows, :])
            ready[rows, :] = (states.astype(jnp.float32) + gate[...] * summed).astype(jnp.bfloat16)
            block = pl.ds(first_row, TILE)
            copies.append(pltpu.make_async_copy(ready.at[block, :], out.at[block, :], sems.at[index]))
            copies[-1].start()
        for copy in copies:
            copy.wait()


def last_out(same, cross, held, weight, partial, kept, residual, gate, fresh):
    span, share = partial.shape
    return pl.pallas_call(
        last_out_kernel,
        out_shape=jax.ShapeDtypeStruct((span, share), jnp.bfloat16),
        in_specs=[vmem_spec()] * 8 + [any_spec()],
        out_specs=any_spec(),
        scratch_shapes=[pltpu.VMEM((span, share), jnp.bfloat16), pltpu.SemaphoreType.DMA((4,))],
        compiler_params=pltpu.CompilerParams(vmem_limit_bytes=8 * MIB),
        cost_estimate=cost(1, 1),
    )(same, cross, held, near(weight), near(partial), near(kept), residual, near(gate), far(fresh))


def on_device(hidden, levels, frame_counts, mod_weight, qkv_weight, out_weight, fresh):
    queue_len = lax.axis_size("queue")
    members = lax.axis_size("heads")
    route = functools.partial(routed, queue_len=queue_len, members=members)
    twin = lambda a: route(a, target=lambda s, y, k: (s, y, 1 - k))

    after = lambda a, *b: lax.optimization_barrier((a, *b))[0]
    frame_counts = frame_counts.astype(jnp.int32)

    twin_weight = twin(qkv_weight)
    mine, far_mine = slices(hidden, out_weight, members)
    second = route(mine, target=lambda s, y, k: (s ^ 1, y ^ k, k))

    payload = modulate(embed_levels(levels, mod_weight.shape[0]), mod_weight)
    mod_rows = lax.all_to_all(payload, "queue", 0, 0, tiled=True)[:, 0, :]

    first = twin(after(second, mod_rows))
    w_far = route(after(far_mine, mod_rows), target=lambda s, y, k: (s ^ 1, 1 - y, k))
    dead = masks(after(frame_counts, mod_rows), hidden.shape[0])
    kv, k, v, normed, q_weight, twin_a, twin_b, share_states = keys_values(after(mod_rows, dead), hidden, first, second, qkv_weight, twin_weight, out_weight)

    def remote_target(s, y, k):
        back = (s % 2 == 0) == (k == 0)
        return (s - 2 if back else s + 2, y, 1 - k)

    kv_remote = route(kv, target=remote_target)
    k_twin, v_twin = twin(k), twin(v)
    query = queries(after(normed, kv), q_weight)
    o, m, l = local_attention(dead, query, kv, k_twin, v_twin)
    residual = route(
        after(share_states, o),
        target=lambda s, y, k: (s - 1, y, 0) if k == 0 else ((s - 2, y, 1) if s % 2 else None),
    )
    attn = remote_attention(dead, query, kv_remote, o, m, l)

    def goal(s, y, k):
        if k == 0:
            return (s - 1, y, 0)
        return (s if s % 2 == 0 else s - 2, y, 1)

    same = route(attn, target=lambda s, y, k: None if s % 2 == 0 and k == 1 else goal(s, y, k))
    cross = route(attn, target=lambda s, y, k: goal(s, 1 - y, k))
    twin_attn = twin(attn)
    blocks = [*columns_of_twin(after(w_far, attn)), after(twin_a, attn), after(twin_b, attn)]
    far_a, far_b, twin_a, twin_b = [twin(a) for a in blocks]
    weight, gate = tail_inputs(mod_rows, out_weight, w_far, twin_a, twin_b, far_a, far_b)
    same, cross, residual, _ = lax.optimization_barrier((same, cross, residual, weight))
    partial = first_out(same, cross, attn, weight)
    return last_out(twin(same), twin(cross), twin_attn, weight, partial, share_states, residual, gate, fresh)


def solution(mesh):
    placed = (
        P("queue", None),
        P(),
        P(),
        P(None, "queue"),
        P(None, None, "heads"),
        P("heads", None),
        P(None, "heads"),
    )
    return jax.shard_map(
        on_device, mesh=mesh, in_specs=placed, out_specs=P("queue", "heads"), check_vma=False
    )
```

```python
import functools
import math

import jax
import jax.numpy as jnp
from jax import lax
from jax.experimental import pallas as pl
from jax.experimental.pallas import tpu as pltpu
from jax.sharding import PartitionSpec as P

HD = 64
P_SIZE = 256
PAIR = 2 * HD
NEG = -1e30
BOTH = ("queue", "heads")
MIB = 1024 * 1024


def embed_levels(levels, width):
    halfway = width // 2
    freqs = jnp.exp(-math.log(10000.0) * jnp.arange(halfway, dtype=jnp.float32) / halfway)
    angles = levels.astype(jnp.float32)[:, None] * freqs[None, :]
    return jax.nn.silu(jnp.concatenate([jnp.cos(angles), jnp.sin(angles)], axis=1)).astype(
        jnp.bfloat16
    )


def routed(array, queue_len, members, target):
    pairs = []
    for slot in range(queue_len):
        for member in range(members):
            goal = target(slot, member // 2, member % 2)
            if goal is not None and 0 <= goal[0] < queue_len:
                pairs.append((slot * members + member, goal[0] * members + goal[1] * 2 + goal[2]))
    return lax.ppermute(array, BOTH, pairs)


def low_lanes(shape):
    return lax.broadcasted_iota(jnp.int32, shape, len(shape) - 1) < HD


def copies_of(source, target, sems, chunks, first=0):
    step = source.shape[0] // chunks
    return [
        pltpu.make_async_copy(
            source.at[pl.ds(i * step, step), :], target.at[pl.ds(i * step, step), :], sems.at[first + i]
        )
        for i in range(chunks)
    ]


def place():
    slot, member = lax.axis_index("queue"), lax.axis_index("heads")
    return member, member & 1, member >> 1, slot & 1, slot


def any_spec():
    return pl.BlockSpec(memory_space=pl.ANY)


def far(array):
    return pltpu.with_memory_space_constraint(array, pltpu.HBM)


def near(array):
    return pltpu.with_memory_space_constraint(array, pltpu.VMEM)


def near_out(shape, dtype=jnp.bfloat16):
    return pltpu.VMEM(shape, dtype)


def cost(flops, moved, transcendentals=0):
    return pl.CostEstimate(flops=flops, bytes_accessed=moved, transcendentals=transcendentals)


def vmem_spec():
    return pl.BlockSpec(memory_space=pltpu.VMEM)


def smem_spec():
    return pl.BlockSpec(memory_space=pltpu.SMEM)


def lanes_at(index, size):
    return pl.ds(pl.multiple_of(index * size, size), size)


def slices_kernel(hidden, out_weight, mine, far_out, sems):
    _, core, y_hi, _, _ = place()
    half, width = mine.shape[0], far_out.shape[1]
    copies = (
        copies_of(hidden.at[lanes_at(core, half), :], mine, sems, 4)
        + copies_of(out_weight.at[:, lanes_at(1 - y_hi, width)], far_out, sems, 4, 4)
    )
    for copy in copies:
        copy.start()
    for copy in copies:
        copy.wait()


def slices(hidden, out_weight, members):
    rows, width = hidden.shape
    share, depth = width // members, out_weight.shape[0]
    return pl.pallas_call(
        slices_kernel,
        out_shape=(
            near_out((rows // 2, width)),
            near_out((depth, 2 * share)),
        ),
        in_specs=[any_spec(), any_spec()],
        out_specs=(vmem_spec(),) * 2,
        scratch_shapes=[pltpu.SemaphoreType.DMA((8,))],
        compiler_params=pltpu.CompilerParams(vmem_limit_bytes=2 * MIB),
        cost_estimate=cost(0, 4 * MIB),
    )(far(hidden), far(out_weight))


ROW = 384


def modulate_kernel(emb_ref, mod_ref, payload, rows_ref):
    rows_ref[...] = jnp.zeros_like(rows_ref)
    columns = mod_ref.shape[0]
    rows_ref[:, :columns] = lax.dot_general(
        emb_ref[...], mod_ref[...], (((1,), (1,)), ((), ())), preferred_element_type=jnp.float32
    )
    rows = rows_ref[...]
    slots = rows.shape[0]
    even = lax.broadcasted_iota(jnp.int32, rows.shape, 0) % 2 == 0
    following = pltpu.roll(rows, slots - 1, 0)
    partner = jnp.where(even, following, pltpu.roll(rows, 1, 0))
    joined = jnp.where(place()[1] == 0, rows, partner) + pltpu.roll(following, columns, 1)
    for slot in range(slots):
        payload[slot] = joined[slot : slot + 1, :]


def modulate(emb, mod_weight):
    return pl.pallas_call(
        modulate_kernel,
        out_shape=jax.ShapeDtypeStruct((emb.shape[0], 1, ROW), jnp.float32),
        in_specs=[vmem_spec(), vmem_spec()],
        out_specs=vmem_spec(),
        scratch_shapes=[pltpu.VMEM((emb.shape[0], ROW), jnp.float32)],
        compiler_params=pltpu.CompilerParams(vmem_limit_bytes=2 * MIB),
        cost_estimate=cost(10**7, MIB),
    )(emb, mod_weight.T)


NORM_ROWS = 16


def spread(rows_ref, part, flat):
    slots = rows_ref.shape[0]
    columns = flat.shape[1] // slots
    step = columns - PAIR
    row = lax.broadcasted_iota(jnp.int32, (8, 2 * PAIR), 0)
    at = lax.broadcasted_iota(jnp.int32, (8, 2 * PAIR), 1) - step * row
    held = (at >= 0) & (at < columns)
    first_row = row[:, :PAIR] == 0
    for i in range(slots // 8):
        block = rows_ref[8 * i : 8 * i + 8, :]
        if part:
            block = pltpu.roll(block, ROW - columns * part, 1)
        turned = pltpu.roll(block, 0, 1, stride=step, stride_axis=0)
        turned = jnp.where(held, turned[:, : 2 * PAIR], 0.0)
        carried = turned[:, PAIR:]
        tiles = turned[:, :PAIR] + jnp.where(first_row, 0.0, pltpu.roll(carried, 1, 0))
        base = 8 * i * columns
        for j in range(8):
            flat[:, base + j * PAIR : base + (j + 1) * PAIR] = tiles[j : j + 1, :]
        flat[:, base + 8 * PAIR : base + 9 * PAIR] = carried[7:8, :]


def kv_kernel(
    rows_ref, hidden, first, second, own_weight, twin_weight, out_weight, kv_ref, k_ref, v_ref, states_ref, q_weight,
    twin_a, twin_b, share_ref,
    flat, weight, x_sems, w_sems,
):
    member, core, y_hi, parity, _ = place()
    rows, width = states_ref.shape
    half = rows // 2
    each = q_weight.shape[1]
    from_own = copies_of(hidden, states_ref, x_sems, 4)
    from_pair = copies_of(first, states_ref.at[pl.ds(0, half), :], x_sems, 2) + copies_of(
        second, states_ref.at[pl.ds(half, half), :], x_sems, 2, 2
    )

    def weights_from(source):
        return [
            copies_of(source.at[kind], target, w_sems, 2, 2 * kind)
            for kind, target in (
                (1, weight.at[:, pl.ds(0, each)]),
                (2, weight.at[:, pl.ds(each, each)]),
                (0, q_weight),
            )
        ]

    def start(condition, copies):
        @pl.when(condition)
        def _():
            for copy in copies:
                copy.start()

    start(core == 0, from_own)
    start(core == 1, from_pair)
    start(core == parity, sum(weights_from(own_weight)[:2], []))
    start(core != parity, sum(weights_from(twin_weight)[:2], []))
    beside = y_hi * 2 + 1 - core
    asides = sum(
        (
            copies_of(
                out_weight.at[lanes_at(index, out.shape[0]), lanes_at(beside, out.shape[1])], out, w_sems, 1, 6 + index
            )
            for index, out in enumerate((twin_a, twin_b))
        ),
        [],
    )
    spread(rows_ref, 0, flat)
    scale, shift = 1.0 + flat[:, width : 2 * width], flat[:, :width]

    def normalise(first_row, count):
        for start in range(first_row, first_row + count, NORM_ROWS):
            block = pl.ds(start, NORM_ROWS)
            states = states_ref[block, :].astype(jnp.float32)
            mean = jnp.mean(states, axis=1, keepdims=True)
            centred = states - mean
            var = jnp.mean(centred * centred, axis=1, keepdims=True)
            states_ref[block, :] = (centred * lax.rsqrt(var + 1e-05) * scale + shift).astype(jnp.bfloat16)

    chunk = rows // len(from_own)
    for index, copy in enumerate(from_own):
        copy.wait()
        block = pl.ds(index * chunk, chunk)
        share_ref[block, :] = states_ref[block, lanes_at(member, share_ref.shape[1])]
        normalise(index * chunk, chunk)
    keys, values, queries = weights_from(own_weight)
    for copy in keys + values:
        copy.wait()
    start(core == parity, weights_from(own_weight)[2])
    start(core != parity, weights_from(twin_weight)[2])
    for copy in asides:
        copy.start()
    kv = jnp.dot(states_ref[...], weight[...], preferred_element_type=jnp.float32).astype(jnp.bfloat16)
    kv_ref[...] = kv
    k_ref[...] = kv[:, :each]
    v_ref[...] = kv[:, each:]
    for copy in queries + asides:
        copy.wait()


def keys_values(mod_rows, hidden, first, second, own_weight, twin_weight, out_weight):
    rows, width = hidden.shape
    each = own_weight.shape[2]
    return pl.pallas_call(
        kv_kernel,
        out_shape=(
            near_out((rows, 2 * each)),
            near_out((rows, each)),
            near_out((rows, each)),
            near_out((rows, width)),
            near_out((width, each)),
            near_out((out_weight.shape[0] // 2, width // 4)),
            near_out((out_weight.shape[0] // 2, width // 4)),
            near_out((rows, width // 4)),
        ),
        in_specs=[vmem_spec()] + [any_spec()] * 6,
        out_specs=(vmem_spec(),) * 8,
        scratch_shapes=[
            pltpu.VMEM((1, 3 * width), jnp.float32),
            pltpu.VMEM((width, 2 * each), jnp.bfloat16),
            pltpu.SemaphoreType.DMA((4,)),
            pltpu.SemaphoreType.DMA((8,)),
        ],
        compiler_params=pltpu.CompilerParams(vmem_limit_bytes=24 * MIB),
        cost_estimate=cost(1, 1),
    )(mod_rows, far(hidden), first, second, far(own_weight), twin_weight, far(out_weight))


def query_kernel(normed, weight, query_ref):
    query = jnp.dot(normed[...], weight[...], preferred_element_type=jnp.float32).astype(jnp.bfloat16)
    query_ref[...] = (query * HD ** (-0.5)).astype(jnp.bfloat16)


def queries(normed, weight):
    return pl.pallas_call(
        query_kernel,
        out_shape=near_out((normed.shape[0], weight.shape[1])),
        in_specs=[vmem_spec()] * 2,
        out_specs=vmem_spec(),
        compiler_params=pltpu.CompilerParams(vmem_limit_bytes=4 * MIB),
        cost_estimate=cost(1, 1),
    )(near(normed), near(weight))


def count_at(counts_ref, at):
    inside = (at >= 0) & (at < counts_ref.shape[0])
    return jnp.where(inside, counts_ref[jnp.where(inside, at, 0)], 0)


LOG2E = math.log2(math.e)


def scores_of(query, keys):
    return lax.dot_general(query, keys, (((1,), (1,)), ((), ())), preferred_element_type=jnp.float32)


def dead_rows(span, count):
    row = lax.broadcasted_iota(jnp.int32, (span, PAIR), 0)
    return jnp.where(row < count * P_SIZE, 0.0, NEG).astype(jnp.bfloat16)


def two_heads(keys, values, dead):
    low = low_lanes(keys.shape)
    lane = lax.broadcasted_iota(jnp.int32, keys.shape, 1)
    zero, one = jnp.zeros_like(keys), jnp.ones_like(values)
    return (
        (jnp.where(low, keys, jnp.where(lane == HD, dead, zero)), jnp.where(low, values, one)),
        (jnp.where(low, jnp.where(lane == 0, dead, zero), keys), jnp.where(low, one, values)),
    )


def two_queries(query):
    low = low_lanes(query.shape)
    lane = lax.broadcasted_iota(jnp.int32, query.shape, 1)
    zero, one = jnp.zeros_like(query), jnp.ones_like(query)
    return (
        jnp.where(low, query, jnp.where(lane == HD, one, zero)),
        jnp.where(low, jnp.where(lane == 0, one, zero), query),
    )


def attend(query_of, pairs, blocks, before_of, finish):
    units = [(pair, rows) for pair in range(len(pairs)) for rows in blocks]

    def scores(unit):
        pair, rows = unit
        return [scores_of(q, keys) for q, (keys, _) in zip(two_queries(query_of(pair, rows)), pairs[pair])]

    following = scores(units[0])
    for index, (pair, rows) in enumerate(units):
        current = following
        if index + 1 < len(units):
            following = scores(units[index + 1])
        peaks, numers = [], []
        for head in range(2):
            peak = jnp.max(current[head], axis=1, keepdims=True)
            before = before_of(pair, rows, head)
            peak = peak if before is None else jnp.maximum(peak, before)
            probs = jnp.exp2((current[head] - peak) * LOG2E).astype(jnp.bfloat16)
            peaks.append(peak)
            numers.append(jnp.dot(probs, pairs[pair][head][1], preferred_element_type=jnp.float32))
        low = low_lanes(numers[0].shape)
        total = pltpu.roll(jnp.where(low, numers[1], numers[0]), HD, 1)
        finish(pair, rows, jnp.where(low, *numers), jnp.where(low, *peaks), total)


def pair_lanes(pair):
    return slice(pair * PAIR, (pair + 1) * PAIR)


def masks_kernel(counts_ref, dead_ref):
    _, core, _, parity, slot = place()
    rows = dead_ref.shape[0] // 3
    step = 1 - 2 * parity
    stretches = (slot + core * step, slot + (1 - core) * step, jnp.where(core == 0, slot - step, slot + 2 * step))
    for index, stretch in enumerate(stretches):
        dead_ref[index * rows : (index + 1) * rows, :] = dead_rows(rows, count_at(counts_ref, stretch))


def masks(counts, rows):
    return pl.pallas_call(
        masks_kernel,
        out_shape=near_out((3 * rows, PAIR)),
        in_specs=[smem_spec()],
        out_specs=vmem_spec(),
        compiler_params=pltpu.CompilerParams(vmem_limit_bytes=2 * MIB),
        cost_estimate=cost(1, 1),
    )(counts)


def local_kernel(dead_ref, q_ref, own_ref, k_twin, v_twin, o_ref, m_ref, l_ref):
    span = own_ref.shape[0]
    tile = 256
    dead = dead_ref[: 2 * span, :]
    pairs = [
        two_heads(
            jnp.concatenate([own_ref[:, pair_lanes(pair)], k_twin[:, pair_lanes(pair)]], axis=0),
            jnp.concatenate([own_ref[:, pair_lanes(3 + pair)], v_twin[:, pair_lanes(pair)]], axis=0),
            dead,
        )
        for pair in range(3)
    ]

    def finish(pair, rows, numer, peak, total):
        o_ref[rows, pair_lanes(pair)] = numer
        m_ref[rows, pair_lanes(pair)] = peak
        l_ref[rows, pair_lanes(pair)] = total

    attend(
        lambda pair, rows: q_ref[rows, pair_lanes(pair)],
        pairs,
        [pl.ds(start, tile) for start in range(0, span, tile)],
        lambda pair, rows, head: None,
        finish,
    )


def local_attention(dead, query, own, k_twin, v_twin):
    span = query.shape[0]
    part = near_out((span, 3 * PAIR), jnp.float32)
    return pl.pallas_call(
        local_kernel,
        out_shape=(part,) * 3,
        in_specs=[vmem_spec()] * 5,
        out_specs=(vmem_spec(),) * 3,
        compiler_params=pltpu.CompilerParams(vmem_limit_bytes=16 * MIB),
        cost_estimate=cost(1, 1),
    )(near(dead), near(query), near(own), k_twin, v_twin)


def remote_kernel(dead_ref, q_ref, kv_ref, o_ref, m_ref, l_ref, piece_ref):
    span = kv_ref.shape[0]
    tile = 256
    dead = dead_ref[2 * span :, :]
    pairs = [
        two_heads(kv_ref[:, pair_lanes(pair)], kv_ref[:, pair_lanes(3 + pair)], dead) for pair in range(3)
    ]

    def before(pair, rows, head):
        at = pair * PAIR + head * HD
        return m_ref[rows, at : at + 1]

    def finish(pair, rows, numer, peak, total):
        lanes = pair_lanes(pair)
        fade = jnp.exp2((m_ref[rows, lanes] - peak) * LOG2E)
        attn = (numer + fade * o_ref[rows, lanes]) / (total + fade * l_ref[rows, lanes])
        piece_ref[rows, lanes] = attn.astype(jnp.bfloat16)

    attend(
        lambda pair, rows: q_ref[rows, pair_lanes(pair)],
        pairs,
        [pl.ds(start, tile) for start in range(0, span, tile)],
        before,
        finish,
    )


def remote_attention(dead, query, kv, o, m, l):
    span = query.shape[0]
    return pl.pallas_call(
        remote_kernel,
        out_shape=near_out((span, 3 * PAIR)),
        in_specs=[vmem_spec()] * 6,
        out_specs=vmem_spec(),
        compiler_params=pltpu.CompilerParams(vmem_limit_bytes=16 * MIB),
        cost_estimate=cost(1, 1),
    )(near(dead), near(query), kv, near(o), near(m), near(l))


def tail_kernel(
    rows_ref, out_weight, w_far, twin_a, twin_b, far_a, far_b, gathered, gate, flat, sems,
):
    member, core, _, parity, _ = place()
    share = gathered.shape[1]
    width = flat.shape[1] // 3
    block = out_weight.shape[0]
    local = jnp.where(core == 0, 1 - parity, parity)
    whole, mine, own = pl.ds(0, share), lanes_at(core, share), lanes_at(member, share)
    copies = []
    for sources, lanes, far_half, y_lo in (
        ((out_weight,), own, 0, core),
        ((twin_a, twin_b), whole, 0, 1 - core),
        ((w_far,), mine, 1, core),
        ((far_a, far_b), whole, 1, 1 - core),
    ):
        base = jnp.where(local == y_lo, 0, 2 * block) + far_half * block
        each = block // len(sources)
        for index, source in enumerate(sources):
            to = pl.ds(pl.multiple_of(base + index * each, each), each)
            copies += copies_of(source.at[:, lanes], gathered.at[to, :], sems, 2 // len(sources), len(copies))
    for copy in copies:
        copy.start()
    spread(rows_ref, 1, flat)
    gate[...] = flat[:, pl.ds(pl.multiple_of(2 * width + member * share, PAIR), share)]
    for copy in copies:
        copy.wait()


def columns_kernel(source, first, second, sems):
    half, width = first.shape
    copies = []
    for index, out in enumerate((first, second)):
        copies += copies_of(source.at[pl.ds(index * half, half), lanes_at(1 - place()[1], width)], out, sems, 2, 2 * index)
    for copy in copies:
        copy.start()
    for copy in copies:
        copy.wait()


def columns_of_twin(blocks):
    rows, width = blocks.shape
    return pl.pallas_call(
        columns_kernel,
        out_shape=(near_out((rows // 2, width // 2)),) * 2,
        in_specs=[any_spec()],
        out_specs=(vmem_spec(),) * 2,
        scratch_shapes=[pltpu.SemaphoreType.DMA((4,))],
        compiler_params=pltpu.CompilerParams(vmem_limit_bytes=2 * MIB),
        cost_estimate=cost(1, 1),
    )(blocks)


def tail_inputs(mod_rows, out_weight, w_far, twin_a, twin_b, far_a, far_b):
    block, width = out_weight.shape
    share = twin_a.shape[1]
    return pl.pallas_call(
        tail_kernel,
        out_shape=(near_out((4 * block, share)), near_out((1, share), jnp.float32)),
        in_specs=[vmem_spec()] + [any_spec()] * 6,
        out_specs=(vmem_spec(),) * 2,
        scratch_shapes=[pltpu.VMEM((1, 3 * width), jnp.float32), pltpu.SemaphoreType.DMA((8,))],
        compiler_params=pltpu.CompilerParams(vmem_limit_bytes=2 * MIB),
        cost_estimate=cost(1, 1),
    )(mod_rows, far(out_weight), w_far, twin_a, twin_b, far_a, far_b)


def first_out_kernel(same, cross, held, weight, partial):
    _, core, _, parity, _ = place()
    here = (parity == 0) & (core == 1)
    attn = jnp.concatenate([jnp.where(here, held[...], same[...]), cross[...]], axis=1)
    partial[...] = jnp.dot(attn, weight[: attn.shape[1], :], preferred_element_type=jnp.float32)


def first_out(same, cross, held, weight):
    span, share = same.shape[0], weight.shape[1]
    return pl.pallas_call(
        first_out_kernel,
        out_shape=near_out((span, share), jnp.float32),
        in_specs=[vmem_spec()] * 4,
        out_specs=vmem_spec(),
        compiler_params=pltpu.CompilerParams(vmem_limit_bytes=8 * MIB),
        cost_estimate=cost(1, 1),
    )(same, cross, near(held), near(weight))


TILE = 128


def last_out_kernel(
    same, cross, held, weight, partial, kept, residual, gate, fresh, out, ready, sems
):
    _, core, _, parity, slot = place()
    here = (parity == 0) & (core == 0)
    holds = (parity == 0) & (core == 1)
    last = slot == lax.axis_size("queue") - 1
    span = partial.shape[0]
    tiles = span // TILE

    @pl.when(last)
    def _():
        for source, target in ((fresh, ready), (ready, out)):
            copies = copies_of(source, target, sems, tiles)
            for copy in copies:
                copy.start()
            for copy in copies:
                copy.wait()

    @pl.when(jnp.logical_not(last))
    def _():
        copies = []
        for index, first_row in enumerate(range(0, span, TILE)):
            rows = slice(first_row, first_row + TILE)
            attn = jnp.concatenate([jnp.where(here, held[rows, :], same[rows, :]), cross[rows, :]], axis=1)
            summed = partial[rows, :] + jnp.dot(
                attn, weight[attn.shape[1] :, :], preferred_element_type=jnp.float32
            )
            states = jnp.where(holds, kept[rows, :], residual[rows, :])
            ready[rows, :] = (states.astype(jnp.float32) + gate[...] * summed).astype(jnp.bfloat16)
            block = pl.ds(first_row, TILE)
            copies.append(pltpu.make_async_copy(ready.at[block, :], out.at[block, :], sems.at[index]))
            copies[-1].start()
        for copy in copies:
            copy.wait()


def last_out(same, cross, held, weight, partial, kept, residual, gate, fresh):
    span, share = partial.shape
    return pl.pallas_call(
        last_out_kernel,
        out_shape=jax.ShapeDtypeStruct((span, share), jnp.bfloat16),
        in_specs=[vmem_spec()] * 8 + [any_spec()],
        out_specs=any_spec(),
        scratch_shapes=[pltpu.VMEM((span, share), jnp.bfloat16), pltpu.SemaphoreType.DMA((4,))],
        compiler_params=pltpu.CompilerParams(vmem_limit_bytes=8 * MIB),
        cost_estimate=cost(1, 1),
    )(same, cross, held, near(weight), near(partial), near(kept), residual, near(gate), far(fresh))


def on_device(hidden, levels, frame_counts, mod_weight, qkv_weight, out_weight, fresh):
    queue_len = lax.axis_size("queue")
    members = lax.axis_size("heads")
    route = functools.partial(routed, queue_len=queue_len, members=members)
    twin = lambda a: route(a, target=lambda s, y, k: (s, y, 1 - k))

    after = lambda a, *b: lax.optimization_barrier((a, *b))[0]
    frame_counts = frame_counts.astype(jnp.int32)

    twin_weight = twin(qkv_weight)
    mine, far_mine = slices(hidden, out_weight, members)
    second = route(mine, target=lambda s, y, k: (s ^ 1, y ^ k, k))

    payload = modulate(embed_levels(levels, mod_weight.shape[0]), mod_weight)
    mod_rows = lax.all_to_all(payload, "queue", 0, 0, tiled=True)[:, 0, :]

    first = twin(after(second, mod_rows))
    w_far = route(after(far_mine, mod_rows), target=lambda s, y, k: (s ^ 1, 1 - y, k))
    dead = masks(after(frame_counts, mod_rows), hidden.shape[0])
    kv, k, v, normed, q_weight, twin_a, twin_b, share_states = keys_values(after(mod_rows, dead), hidden, first, second, qkv_weight, twin_weight, out_weight)

    def remote_target(s, y, k):
        back = (s % 2 == 0) == (k == 0)
        return (s - 2 if back else s + 2, y, 1 - k)

    kv_remote = route(kv, target=remote_target)
    k_twin, v_twin = twin(k), twin(v)
    query = queries(after(normed, kv), q_weight)
    o, m, l = local_attention(dead, query, kv, k_twin, v_twin)
    residual = route(
        after(share_states, o),
        target=lambda s, y, k: (s - 1, y, 0) if k == 0 else ((s - 2, y, 1) if s % 2 else None),
    )
    attn = remote_attention(dead, query, kv_remote, o, m, l)

    def goal(s, y, k):
        if k == 0:
            return (s - 1, y, 0)
        return (s if s % 2 == 0 else s - 2, y, 1)

    same = route(attn, target=lambda s, y, k: None if s % 2 == 0 and k == 1 else goal(s, y, k))
    cross = route(attn, target=lambda s, y, k: goal(s, 1 - y, k))
    twin_attn = twin(attn)
    blocks = [*columns_of_twin(after(w_far, attn)), after(twin_a, attn), after(twin_b, attn)]
    far_a, far_b, twin_a, twin_b = [twin(a) for a in blocks]
    weight, gate = tail_inputs(mod_rows, out_weight, w_far, twin_a, twin_b, far_a, far_b)
    cross, residual, _ = lax.optimization_barrier((cross, residual, weight))
    same = after(same, weight)
    partial = first_out(same, cross, attn, weight)
    return last_out(twin(same), twin(cross), twin_attn, weight, partial, share_states, residual, gate, fresh)


def solution(mesh):
    placed = (
        P("queue", None),
        P(),
        P(),
        P(None, "queue"),
        P(None, None, "heads"),
        P("heads", None),
        P(None, "heads"),
    )
    return jax.shard_map(
        on_device, mesh=mesh, in_specs=placed, out_specs=P("queue", "heads"), check_vma=False
    )
```
